32 devices in a mesh: dp: 4 (over y, x), rows: 8 (over z, core).
Axes of the slice: x: 2, y: 2, z: 4, core: 2. Of those that a mesh axis runs over, the one named last changes fastest.
Arguments:
- grads: bfloat16 [4, 8, 1024, 1024], P('dp', None, 'rows'), may hold values from -6 to 6
- weight: bfloat16 [8, 1024, 1024], P(None, 'rows'), may hold values from -6 to 6
- basis: float32 [8, 1024, 256], P(None, 'rows'), may hold values from -6 to 6
- first_moment: float32 [32, 256, 1024], P('rows', None, 'dp'), may hold values from -6 to 6
- second_moment: float32 [32, 256, 1024], P('rows', None, 'dp'), may hold values from 0.5 to 4
- sketch: bfloat16 [1024, 256], replicated, may hold values from -6 to 6
- owner: int32 [8], replicated, may hold values from 0 to 7, as said below
- rank: int32 [8], replicated, may hold values from 128 to 256
Outputs:
- new_weight: bfloat16 [8, 1024, 1024], P(None, 'rows')
- new_basis: float32 [8, 1024, 256], P(None, 'rows')
- first_out: float32 [32, 256, 1024], P('rows', None, 'dp')
- second_out: float32 [32, 256, 1024], P('rows', None, 'dp')
The draws below stay inside these ranges and needn't reach their ends.
Inputs may be any that keep to these rules, and one draw needn't show every extreme that they name: No owner is named by more than 4 matrices, and some owner is named by exactly 4.
All inputs are finite; a program needn't handle non-finite values.
Results may differ from the reference program's by a relative error of at most 0.012.
Values may be sent and summed in bfloat16 or wider, within the bound.
No kernel may reach another device: no remote copies, remote signals or barrier semaphores. Data moves between devices by JAX's collectives and lax.ppermute only.
A program may use at most 128 MiB of HBM per device.

```python
import jax
import jax.numpy as jnp
from jax import lax

MR = 1024
D = 1024
R = 256
CAP = 4
NMAT = 8
SLOTS = 32
GROUPS = 4
N_ROWS = 8


def draw_owner(key, part):
    key_first, key_second, key_third = jax.random.split(key, 3)
    slot_ids = jnp.arange(SLOTS, dtype=jnp.int32)
    chosen = jax.random.randint(key_first, (), 0, N_ROWS, dtype=jnp.int32)
    noise = jax.random.randint(key_second, (SLOTS,), 0, 1 << 20, dtype=jnp.int32)
    scores = noise * SLOTS + slot_ids
    scores = jnp.where(slot_ids // CAP == chosen, -1 - slot_ids, scores)
    ordering = jnp.argsort(scores, stable=True)
    picked = ordering[:NMAT]
    shuffle = jax.random.permutation(key_third, NMAT)
    return (picked[shuffle] // CAP).astype(jnp.int32)


def with_ends(result, stream_key, smallest, high):
    spot = [jax.random.randint(jax.random.fold_in(stream_key, axis), (), 0, length) for axis, length in enumerate(result.shape)]
    longest = result.shape.index(max(result.shape))
    next_to = spot[:longest] + [(spot[longest] + 1) % result.shape[longest]] + spot[longest + 1:]
    return result.at[tuple(spot)].set(smallest).at[tuple(next_to)].set(high)


def block_scale(stream_key, shape, cuts, low, largest):
    gain = 1.0
    for axis_at, blocks in cuts:
        steps = jax.random.uniform(jax.random.fold_in(jax.random.fold_in(stream_key, 6), axis_at), (blocks,), jnp.float32, low / len(cuts), largest / len(cuts))
        gain = gain * jnp.repeat(jnp.exp(steps), shape[axis_at] // blocks).reshape((-1,) + (1,) * (len(shape) - 1 - axis_at))
    return gain


def gaussian(rng, shape, spread, reach, pieces=(), kind=jnp.bfloat16):
    entries = spread * jax.random.normal(rng, shape, jnp.float32)
    if pieces:
        entries = entries * block_scale(rng, shape, pieces, -0.22, 0.18)
    return jnp.clip(entries, -reach, reach).astype(kind)


def setup_inputs(seed: int = 0) -> dict:
    keys = jax.random.split(jax.random.key(seed), 9)
    grads = gaussian(keys[0], (GROUPS, NMAT, MR, D), 1.0, 6.0, ((0, 4), (2, 8)))
    weight = gaussian(keys[1], (NMAT, MR, D), 1.0, 6.0, ((1, 8),))
    basis = gaussian(keys[2], (NMAT, MR, R), 1.0, 6.0, ((1, 8),), jnp.float32)
    first_moment = gaussian(keys[3], (SLOTS, R, D), 1.0, 6.0, ((0, 8), (2, 4)), jnp.float32)
    second_moment = jnp.clip(0.5 + 3.5 * jax.random.uniform(keys[4], (SLOTS, R, D), jnp.float32) ** block_scale(keys[4], (SLOTS, R, D), ((0, 8), (2, 4)), -0.2, 0.2), 0.5, 4.0)
    sketch = gaussian(keys[5], (D, R), 1.0, 6.0)
    owner = draw_owner(jax.random.fold_in(keys[8], 71), 0)
    rank = with_ends(jax.random.randint(keys[7], (NMAT,), R // 2, R + 1), jax.random.fold_in(keys[7], 1), R // 2, R).astype(jnp.int32)
    return dict(grads=grads, weight=weight, basis=basis, first_moment=first_moment, second_moment=second_moment, sketch=sketch, owner=owner, rank=rank)


beta_one = 0.9
beta_two = 0.95
bias_one = 1.0 - 0.9 ** 10
bias_two = 1.0 - 0.95 ** 10
step_size = 0.5
epsilon = 1e-08

def slot_of(owner):
    same = owner[:, None] == owner[None, :]
    places = jnp.arange(owner.shape[0], dtype=jnp.int32)
    earlier = places[None, :] < places[:, None]
    within = lax.optimization_barrier(jnp.sum((same & earlier).astype(jnp.int32), axis=1))
    return (owner * CAP + within).astype(jnp.int32)

def refresh(gradient, sketch, root):
    sample = jnp.dot(gradient.astype(jnp.float32), sketch.astype(jnp.float32), preferred_element_type=jnp.float32)
    gram = jnp.dot(sample.T, sample, precision=lax.Precision.HIGHEST)
    lower = jnp.linalg.cholesky(gram)
    solved = lax.linalg.triangular_solve(lower, sample, left_side=False, lower=True, transpose_a=True)
    return solved * root

def reference(grads, weight, basis, first_moment, second_moment, sketch, owner, rank):
    root = float(MR) ** 0.5
    inverse_root = float(MR) ** (-0.5)
    gradient = lax.optimization_barrier(jnp.sum(grads.astype(jnp.float32), axis=0)).astype(jnp.bfloat16)
    slots = slot_of(owner)
    rank_rows = jnp.arange(R, dtype=jnp.int32)

    def single(index):
        grad_one = gradient[index]
        basis_one = basis[index]
        slot_one = slots[index]
        grad_wide = lax.optimization_barrier(grad_one).astype(jnp.float32)
        projected = jnp.dot(basis_one.T, grad_wide, precision=lax.Precision.HIGHEST) * inverse_root
        first_new = beta_one * first_moment[slot_one] + (1.0 - beta_one) * projected
        second_new = beta_two * second_moment[slot_one] + (1.0 - beta_two) * projected * projected
        keeping = (rank_rows < rank[index]).astype(jnp.float32)[:, None]
        update = keeping * (first_new / bias_one) / (jnp.sqrt(second_new / bias_two) + epsilon)
        delta = (jnp.dot(basis_one, update, precision=lax.Precision.HIGHEST) * inverse_root).astype(jnp.bfloat16)
        delta = lax.optimization_barrier(delta)
        weight_new = (weight[index].astype(jnp.float32) - step_size * delta.astype(jnp.float32)).astype(jnp.bfloat16)
        return (weight_new, refresh(grad_one, sketch, root), first_new, second_new)
    new_weight, new_basis, first_new, second_new = lax.map(single, jnp.arange(NMAT, dtype=jnp.int32))
    first_out = jnp.zeros((SLOTS, R, D), jnp.float32).at[slots].set(first_new)
    second_out = jnp.zeros((SLOTS, R, D), jnp.float32).at[slots].set(second_new)
    return (new_weight, new_basis, first_out, second_out)
```

```python
import functools

import jax
import jax.numpy as jnp
from jax import lax
from jax.experimental import pallas as pl
from jax.experimental.pallas import tpu as pltpu
from jax.sharding import PartitionSpec as P

beta_one = 0.9
beta_two = 0.95
bias_one = 1.0 - 0.9**10
bias_two = 1.0 - 0.95**10
step_size = 0.5
epsilon = 1e-08
BLOCK = 64
HIGHEST = lax.Precision.HIGHEST
VMEM_LIMIT = 48 * 1024 * 1024


def slot_of(owner, capacity):
    same = owner[:, None] == owner[None, :]
    places = jnp.arange(owner.shape[0], dtype=jnp.int32)
    earlier = places[None, :] < places[:, None]
    within = jnp.sum((same & earlier).astype(jnp.int32), axis=1)
    return owner * capacity + within


def factor_kernel(gram_ref, rows_ref, out_ref, work, *, scale):
    pair, size = gram_ref.shape[0], gram_ref.shape[1]
    lane = lax.broadcasted_iota(jnp.int32, (BLOCK, 2 * BLOCK), 1)
    sub = lax.broadcasted_iota(jnp.int32, (BLOCK, 2 * BLOCK), 0)
    eye_right = (lane - BLOCK == sub).astype(jnp.float32)
    wide_row = lax.broadcasted_iota(jnp.int32, (size, size), 0)
    wide_col = lax.broadcasted_iota(jnp.int32, (size, size), 1)
    eye = (wide_row == wide_col).astype(jnp.float32)
    for b in range(pair):
        work[b, :, :size] = gram_ref[b]
        work[b, :, size:] = eye
    blocks = size // BLOCK
    for j in range(blocks):
        lo = j * BLOCK
        tiles = []
        for b in range(pair):
            base = lo // 128 * 128
            slab = work[b, lo : lo + BLOCK, base : base + 128]
            if lo > base:
                slab = pltpu.roll(slab, 128 - (lo - base), 1)
            tiles.append(jnp.where(lane < BLOCK, slab, eye_right))
        for k in range(BLOCK - 1):
            for b in range(pair):
                tile = tiles[b]
                column = jnp.where(sub[:, :1] > k, tile[:, k : k + 1], 0.0)
                row = tile[k : k + 1, :] * (1.0 / tile[k : k + 1, k : k + 1])
                tiles[b] = tile - column * row
        for b in range(pair):
            tile = tiles[b]
            diagonal = jnp.sum(jnp.where(lane == sub, tile, 0.0), axis=1, keepdims=True)
            inverse = pltpu.roll(tile, BLOCK, 1)[:, :BLOCK] * lax.rsqrt(diagonal)
            solved = jnp.dot(
                inverse,
                work[b, lo : lo + BLOCK, :],
                precision=HIGHEST,
                preferred_element_type=jnp.float32,
            )
            work[b, lo : lo + BLOCK, size:] = solved[:, size:]
            if j + 1 < blocks:
                change = lax.dot_general(
                    solved[:, :size],
                    solved,
                    (((0,), (0,)), ((), ())),
                    precision=HIGHEST,
                    preferred_element_type=jnp.float32,
                )
                work[b, lo + BLOCK :, :] = work[b, lo + BLOCK :, :] - change[lo + BLOCK :, :]
    for b in range(pair):
        basis = lax.dot_general(
            rows_ref[b].astype(jnp.float32),
            work[b, :, size:],
            (((1,), (1,)), ((), ())),
            precision=HIGHEST,
            preferred_element_type=jnp.float32,
        )
        out_ref[b] = (basis * scale).astype(out_ref.dtype)


def factor(gram, rows, scale):
    count, size, _ = gram.shape
    pair = 2 if count % 2 == 0 else 1
    shard = rows.shape[1]
    return pl.pallas_call(
        functools.partial(factor_kernel, scale=scale),
        out_shape=jax.ShapeDtypeStruct((count, shard, size), jnp.bfloat16),
        grid=(count // pair,),
        in_specs=[
            pl.BlockSpec((pair, size, size), lambda i: (i, 0, 0)),
            pl.BlockSpec((pair, shard, size), lambda i: (i, 0, 0)),
        ],
        out_specs=pl.BlockSpec((pair, shard, size), lambda i: (i, 0, 0)),
        scratch_shapes=[pltpu.VMEM((pair, size, 2 * size), jnp.float32)],
        compiler_params=pltpu.CompilerParams(vmem_limit_bytes=VMEM_LIMIT),
        cost_estimate=pl.CostEstimate(
            flops=4_000_000_000, bytes_accessed=count * size * size * 8, transcendentals=0
        ),
    )(gram, rows)


def pick_kernel(index_ref, first_ref, second_ref, out_ref):
    out_ref[0, 0] = first_ref[0].astype(out_ref.dtype)
    out_ref[0, 1] = second_ref[0].astype(out_ref.dtype)


def pick_moments(index, first, second):
    count = index.shape[0]
    _, rank, width = first.shape
    spec = pl.BlockSpec((1, rank, width), lambda i, index: (index[i], 0, 0))
    return pl.pallas_call(
        pick_kernel,
        out_shape=jax.ShapeDtypeStruct((count, 2, rank, width), jnp.bfloat16),
        grid_spec=pltpu.PrefetchScalarGridSpec(
            num_scalar_prefetch=1,
            grid=(count,),
            in_specs=[spec, spec],
            out_specs=pl.BlockSpec((1, 2, rank, width), lambda i, index: (i, 0, 0, 0)),
        ),
        cost_estimate=pl.CostEstimate(
            flops=0, bytes_accessed=count * rank * width * 12, transcendentals=0
        ),
    )(index, first, second)


def project_kernel(grad_ref, basis_ref, out_ref, *, scale):
    total = grad_ref[0, 0].astype(jnp.float32)
    for g in range(1, grad_ref.shape[0]):
        total = total + grad_ref[g, 0].astype(jnp.float32)
    product = lax.dot_general(
        basis_ref[0],
        total,
        (((0,), (0,)), ((), ())),
        precision=HIGHEST,
        preferred_element_type=jnp.float32,
    )
    out_ref[0] = (product * scale).astype(out_ref.dtype)


def project(parts, basis, scale):
    groups, count, shard, quarter = parts.shape
    rank = basis.shape[2]
    return pl.pallas_call(
        functools.partial(project_kernel, scale=scale),
        out_shape=jax.ShapeDtypeStruct((count, rank, quarter), jnp.bfloat16),
        grid=(count,),
        in_specs=[
            pl.BlockSpec((groups, 1, shard, quarter), lambda i: (0, i, 0, 0)),
            pl.BlockSpec((1, shard, rank), lambda i: (i, 0, 0)),
        ],
        out_specs=pl.BlockSpec((1, rank, quarter), lambda i: (i, 0, 0)),
        cost_estimate=pl.CostEstimate(
            flops=12 * count * shard * quarter * rank,
            bytes_accessed=count * (shard * quarter * 12 + rank * quarter * 2),
            transcendentals=0,
        ),
    )(parts, basis)


def moment_kernel(index_ref, valid_ref, proj_ref, first_ref, second_ref, first_out, second_out):
    keep = valid_ref[pl.program_id(0)] > 0
    projected = proj_ref[0].astype(jnp.float32)
    first_new = beta_one * first_ref[0] + (1.0 - beta_one) * projected
    second_new = beta_two * second_ref[0] + (1.0 - beta_two) * projected * projected
    first_out[0] = jnp.where(keep, first_new, 0.0)
    second_out[0] = jnp.where(keep, second_new, 0.0)


def update_moments(index, valid, projected, first, second):
    capacity, rank, width = first.shape
    spec = pl.BlockSpec((1, rank, width), lambda i, index, valid: (i, 0, 0))
    picked = pl.BlockSpec((1, rank, width), lambda i, index, valid: (index[i], 0, 0))
    shape = jax.ShapeDtypeStruct(first.shape, jnp.float32)
    return pl.pallas_call(
        moment_kernel,
        out_shape=(shape, shape),
        grid_spec=pltpu.PrefetchScalarGridSpec(
            num_scalar_prefetch=2,
            grid=(capacity,),
            in_specs=[picked, spec, spec],
            out_specs=(spec, spec),
        ),
        cost_estimate=pl.CostEstimate(
            flops=0, bytes_accessed=capacity * rank * width * 18, transcendentals=0
        ),
    )(index, valid, projected, first, second)


def per_device(grads, weight, basis, first_moment, second_moment, sketch, owner, rank):
    owners = lax.axis_size("rows")
    groups = lax.axis_size("dp")
    here = lax.axis_index("rows")
    capacity, rank_full, quarter = first_moment.shape
    count, shard, width = weight.shape
    per = count // owners
    total_rows = shard * owners
    root = float(total_rows) ** 0.5
    inverse_root = float(total_rows) ** (-0.5)
    local = grads[0]
    slots = slot_of(owner, capacity)

    sent = lax.all_to_all(
        local.reshape(count, shard, groups, quarter), "dp", split_axis=2, concat_axis=0
    )
    part = jnp.einsum("mrd,dk->mrk", local, sketch, preferred_element_type=jnp.float32)
    part = part.astype(jnp.bfloat16).reshape(groups, count // groups, shard, rank_full)
    got = lax.all_to_all(part, "dp", split_axis=0, concat_axis=0)
    sample = jnp.sum(got.astype(jnp.float32), axis=0).astype(jnp.bfloat16)
    whole = lax.all_gather(sample, "rows", axis=1, tiled=True)

    offset = slots - here * capacity
    held = pick_moments(jnp.clip(offset, 0, capacity - 1), first_moment, second_moment)
    moved = lax.all_to_all(
        held.reshape(owners, per, 2, rank_full, quarter), "rows", split_axis=0, concat_axis=0
    )
    mine = here * per + jnp.arange(per, dtype=jnp.int32)
    from_owner = owner[mine]
    moments = jnp.stack([moved[from_owner[i], i] for i in range(per)]).astype(jnp.float32)

    partial = project(sent, basis, inverse_root)
    terms = lax.all_to_all(
        partial.reshape(owners, per, rank_full, quarter), "rows", split_axis=0, concat_axis=0
    )
    projected = jnp.sum(terms.astype(jnp.float32), axis=0)
    first_new = beta_one * moments[:, 0] + (1.0 - beta_one) * projected
    second_new = beta_two * moments[:, 1] + (1.0 - beta_two) * projected * projected
    keeping = jnp.arange(rank_full, dtype=jnp.int32)[None, :] < rank[mine][:, None]
    update = (first_new / bias_one) / (jnp.sqrt(second_new / bias_two) + epsilon)
    update = jnp.where(keeping[:, :, None], update, 0.0).astype(jnp.bfloat16)
    updates = lax.all_gather(update, "rows", axis=0, tiled=True)
    all_projected = lax.all_gather(projected.astype(jnp.bfloat16), "rows", axis=0, tiled=True)

    delta = jnp.einsum(
        "mrk,mkd->mrd",
        basis.astype(jnp.bfloat16),
        updates,
        preferred_element_type=jnp.float32,
    )
    delta = (delta * inverse_root).astype(jnp.bfloat16)
    full_delta = lax.all_gather(delta, "dp", axis=2, tiled=True)
    new_weight = (weight.astype(jnp.float32) - step_size * full_delta.astype(jnp.float32)).astype(
        jnp.bfloat16
    )

    gram = jnp.einsum("cmr,cms->crs", whole, whole, preferred_element_type=jnp.float32)
    rows_basis = factor(gram, sample, root)
    new_basis = lax.all_gather(rows_basis, "dp", axis=0, tiled=True).astype(jnp.float32)

    matched = slots[None, :] == (here * capacity + jnp.arange(capacity, dtype=jnp.int32))[:, None]
    valid = jnp.any(matched, axis=1).astype(jnp.int32)
    index = jnp.sum(
        jnp.where(matched, jnp.arange(count, dtype=jnp.int32)[None, :], 0), axis=1
    )
    first_out, second_out = update_moments(
        index, valid, all_projected, first_moment, second_moment
    )
    return (new_weight, new_basis, first_out, second_out)


def solution(mesh):
    in_specs = (
        P("dp", None, "rows", None),
        P(None, "rows", None),
        P(None, "rows", None),
        P("rows", None, "dp"),
        P("rows", None, "dp"),
        P(),
        P(),
        P(),
    )
    out_specs = (
        P(None, "rows", None),
        P(None, "rows", None),
        P("rows", None, "dp"),
        P("rows", None, "dp"),
    )
    return jax.shard_map(
        per_device, mesh=mesh, in_specs=in_specs, out_specs=out_specs, check_vma=False
    )
```

```python
import functools

import jax
import jax.numpy as jnp
from jax import lax
from jax.experimental import pallas as pl
from jax.experimental.pallas import tpu as pltpu
from jax.sharding import PartitionSpec as P

beta_one = 0.9
beta_two = 0.95
bias_one = 1.0 - 0.9**10
bias_two = 1.0 - 0.95**10
step_size = 0.5
epsilon = 1e-08
BLOCK = 64
CHUNKS = 1
HIGHEST = lax.Precision.HIGHEST
VMEM_LIMIT = 48 * 1024 * 1024
VMEM = pl.BlockSpec(memory_space=pltpu.VMEM)
SMEM = pl.BlockSpec(memory_space=pltpu.SMEM)
f32 = jnp.float32
bf16 = jnp.bfloat16


def call(kernel, out_shape, args, scalars=0, us=2.0, aliases=None, scratch=()):
    many = isinstance(out_shape, (tuple, list))
    return pl.pallas_call(
        kernel,
        out_shape=out_shape,
        in_specs=[SMEM] * scalars + [VMEM] * (len(args) - scalars),
        out_specs=[VMEM] * len(out_shape) if many else VMEM,
        scratch_shapes=list(scratch),
        input_output_aliases=aliases or {},
        compiler_params=pltpu.CompilerParams(vmem_limit_bytes=VMEM_LIMIT),
        cost_estimate=pl.CostEstimate(
            flops=0, bytes_accessed=int(us * 3_000_000), transcendentals=0
        ),
    )(*args)


def swap(x, axis, mask):
    size = lax.axis_size(axis)
    return lax.ppermute(x, axis, [(i, i ^ mask) for i in range(size)])


def split_kernel(place, grad_ref, *outs, groups, chunks):
    width = outs[0].shape[2]
    for h in range(chunks):
        for k in range(groups):
            start = ((place[0] ^ k) * chunks + h) * width
            columns = pl.ds(pl.multiple_of(start, 128), width)
            outs[h * groups + k][...] = grad_ref[0, :, :, columns]


def sample_kernel(place, grad_ref, sketch_ref, *outs):
    each = outs[0].shape[0]
    for k, out in enumerate(outs):
        for i in range(each):
            m = (place[0] ^ k) * each + i
            out[i] = jnp.dot(
                grad_ref[0, m], sketch_ref[...], preferred_element_type=f32
            ).astype(bf16)


def sum_kernel(*refs):
    out = refs[-1]
    total = refs[0][...].astype(f32)
    for ref in refs[1:-1]:
        total = total + ref[...].astype(f32)
    out[...] = total.astype(bf16)


def gram_kernel(*refs):
    out = refs[-1]
    for i in range(out.shape[0]):
        total = None
        for ref in refs[:-1]:
            term = lax.dot_general(
                ref[i], ref[i], (((0,), (0,)), ((), ())), preferred_element_type=f32
            )
            total = term if total is None else total + term
        out[i] = total


def eliminate(work, j):
    pair, size = work.shape[0], work.shape[1]
    lane = lax.broadcasted_iota(jnp.int32, (BLOCK, 2 * BLOCK), 1)
    sub = lax.broadcasted_iota(jnp.int32, (BLOCK, 2 * BLOCK), 0)
    eye_right = (lane - BLOCK == sub).astype(f32)
    lo = j * BLOCK
    base = lo // 128 * 128
    tiles = []
    for b in range(pair):
        slab = work[b, lo : lo + BLOCK, base : base + 128]
        if lo > base:
            slab = pltpu.roll(slab, 128 - (lo - base), 1)
        tiles.append(jnp.where(lane < BLOCK, slab, eye_right))
    for k in range(BLOCK - 1):
        for b in range(pair):
            tile = tiles[b]
            column = jnp.where(sub[:, :1] > k, tile[:, k : k + 1], 0.0)
            row = tile[k : k + 1, :] * (1.0 / tile[k : k + 1, k : k + 1])
            tiles[b] = tile - column * row
    for b in range(pair):
        tile = tiles[b]
        diagonal = jnp.sum(jnp.where(lane == sub, tile, 0.0), axis=1, keepdims=True)
        inverse = pltpu.roll(tile, BLOCK, 1)[:, :BLOCK] * lax.rsqrt(diagonal)
        solved = jnp.dot(
            inverse, work[b, lo : lo + BLOCK, :], precision=HIGHEST, preferred_element_type=f32
        )
        work[b, lo : lo + BLOCK, size:] = solved[:, size:]
        if lo + BLOCK < size:
            change = lax.dot_general(
                solved[:, :size],
                solved,
                (((0,), (0,)), ((), ())),
                precision=HIGHEST,
                preferred_element_type=f32,
            )
            work[b, lo + BLOCK :, :] = work[b, lo + BLOCK :, :] - change[lo + BLOCK :, :]


def start_kernel(own_ref, other_ref, work):
    pair, size = own_ref.shape[0], own_ref.shape[1]
    row = lax.broadcasted_iota(jnp.int32, (size, size), 0)
    col = lax.broadcasted_iota(jnp.int32, (size, size), 1)
    eye = (row == col).astype(f32)
    for b in range(pair):
        work[b, :, :size] = own_ref[b] + other_ref[b]
        work[b, :, size:] = eye
    eliminate(work, 0)


def middle_kernel(work_in, work, *, j):
    work[...] = work_in[...]
    eliminate(work, j)


def finish_kernel(work_in, rows_ref, out_ref, work, *, j, scale):
    work[...] = work_in[...]
    eliminate(work, j)
    size = work.shape[1]
    for b in range(work.shape[0]):
        basis = lax.dot_general(
            rows_ref[b].astype(f32),
            work[b, :, size:],
            (((1,), (1,)), ((), ())),
            precision=HIGHEST,
            preferred_element_type=f32,
        )
        out_ref[b] = (basis * scale).astype(out_ref.dtype)


def factor(own, other, rows, scale):
    pair, size, _ = own.shape
    shape = jax.ShapeDtypeStruct((pair, size, 2 * size), f32)
    blocks = size // BLOCK
    work = call(start_kernel, shape, (own, other), us=8.0)
    for j in range(1, blocks - 1):
        work = call(functools.partial(middle_kernel, j=j), shape, (work,), us=7.0)
    return call(
        functools.partial(finish_kernel, j=blocks - 1, scale=scale),
        jax.ShapeDtypeStruct(rows.shape, bf16),
        (work, rows),
        us=8.0,
        scratch=[pltpu.VMEM(shape.shape, f32)],
    )


def pick_kernel(place, owner, first_ref, second_ref, mine_ref, other_ref):
    here, core = place[1] * 2 + place[2], place[2]
    capacity = first_ref.shape[0]
    seen = jnp.int32(0)
    at = []
    for m in range(owner.shape[0]):
        at.append(jnp.minimum(seen, capacity - 1))
        seen = seen + (owner[m] == here).astype(jnp.int32)
    for i in range(mine_ref.shape[0]):
        even, odd = at[2 * i], at[2 * i + 1]
        for out, want in ((mine_ref, core), (other_ref, 1 - core)):
            slot = jnp.where(want == 0, even, odd)
            out[i, 0] = first_ref[slot].astype(bf16)
            out[i, 1] = second_ref[slot].astype(bf16)


def merge_kernel(place, owner, mine_ref, other_ref, *outs):
    z, core = place[1], place[2]
    for k, out in enumerate(outs):
        i = z ^ k
        local = owner[2 * i + core] == 2 * z + core
        out[...] = jnp.where(local, mine_ref[i], other_ref[i])


def project_kernel(place, *refs, scale):
    *grad_refs, basis_ref, mine_ref, other_ref = refs
    core = place[2]
    for i in range(mine_ref.shape[0]):
        for out, want in ((other_ref, 1 - core), (mine_ref, core)):
            m = 2 * i + want
            total = grad_refs[0][m].astype(f32)
            for ref in grad_refs[1:]:
                total = total + ref[m].astype(f32)
            product = lax.dot_general(
                (basis_ref[m] * scale).astype(bf16),
                total.astype(bf16),
                (((0,), (0,)), ((), ())),
                preferred_element_type=f32,
            )
            out[i] = product.astype(out.dtype)


def pair_kernel(place, mine_ref, other_ref, *outs):
    for k, out in enumerate(outs):
        i = place[1] ^ k
        out[...] = (mine_ref[i] + other_ref[i].astype(f32)).astype(out.dtype)


def update_kernel(place, owner, rank, *refs, chips, start):
    terms, moments = refs[:chips], refs[chips : 2 * chips]
    update_ref, projected_ref = refs[2 * chips :]
    z, core = place[1], place[2]
    m = 2 * z + core
    projected = terms[0][...].astype(f32)
    for ref in terms[1:]:
        projected = projected + ref[...].astype(f32)
    width = projected.shape[1]
    columns = slice(start, start + width)
    source = (owner[m] // 2) ^ z
    first = moments[0][0, :, columns]
    second = moments[0][1, :, columns]
    for k in range(1, chips):
        first = jnp.where(source == k, moments[k][0, :, columns], first)
        second = jnp.where(source == k, moments[k][1, :, columns], second)
    first_new = beta_one * first.astype(f32) + (1.0 - beta_one) * projected
    second_new = beta_two * second.astype(f32) + (1.0 - beta_two) * projected * projected
    update = (first_new / bias_one) / (jnp.sqrt(second_new / bias_two) + epsilon)
    row = lax.broadcasted_iota(jnp.int32, update.shape, 0)
    update_ref[...] = jnp.where(row < rank[m], update, 0.0).astype(bf16)
    projected_ref[...] = projected.astype(bf16)


def delta_kernel(place, *refs, chips, scale):
    near, far = refs[:chips], refs[chips : 2 * chips]
    basis_ref, out_ref = refs[2 * chips :]
    z, core = place[1], place[2]
    for k in range(chips):
        for ref, want in ((near[k], core), (far[k], 1 - core)):
            m = 2 * (z ^ k) + want
            product = jnp.dot(
                (basis_ref[m] * scale).astype(bf16), ref[...], preferred_element_type=f32
            )
            out_ref[m] = product.astype(bf16)


def weight_kernel(place, weight_ref, *refs, groups, chunks):
    out_ref = refs[-1]
    width = refs[0].shape[2]
    for h in range(chunks):
        for k in range(groups):
            start = ((place[0] ^ k) * chunks + h) * width
            columns = pl.ds(pl.multiple_of(start, 128), width)
            for m in range(out_ref.shape[0]):
                delta = refs[h * groups + k][m].astype(f32)
                old = weight_ref[m, :, columns].astype(f32)
                out_ref[m, :, columns] = (old - step_size * delta).astype(bf16)


def basis_kernel(place, *refs):
    out_ref = refs[-1]
    each = refs[0].shape[0]
    for k, ref in enumerate(refs[:-1]):
        for i in range(each):
            out_ref[(place[0] ^ k) * each + i] = ref[i].astype(f32)


def moment_kernel(place, owner, *refs, chunks):
    projected_refs = refs[:chunks]
    first_ref, second_ref, first_out, second_out = refs[chunks:]
    here = place[1] * 2 + place[2]
    capacity, rank_full, _ = first_out.shape
    width = projected_refs[0].shape[2]
    seen = jnp.int32(0)
    index = [jnp.int32(0)] * capacity
    for m in range(owner.shape[0]):
        hit = owner[m] == here
        for s in range(capacity):
            index[s] = jnp.where(hit & (seen == s), m, index[s])
        seen = seen + hit.astype(jnp.int32)
    for s in range(capacity):
        keep = seen > s
        for h in range(chunks):
            columns = slice(h * width, (h + 1) * width)
            projected = projected_refs[h][index[s]].astype(f32)
            first_new = beta_one * first_ref[s, :, columns] + (1.0 - beta_one) * projected
            second_new = (
                beta_two * second_ref[s, :, columns] + (1.0 - beta_two) * projected * projected
            )
            first_out[s, :, columns] = jnp.where(keep, first_new, 0.0)
            second_out[s, :, columns] = jnp.where(keep, second_new, 0.0)


def per_device(grads, weight, basis, first_moment, second_moment, sketch, owner, rank):
    owners = lax.axis_size("rows")
    groups = lax.axis_size("dp")
    here = lax.axis_index("rows")
    group = lax.axis_index("dp")
    capacity, rank_full, quarter = first_moment.shape
    count, shard, width = weight.shape
    chips = owners // 2
    each = count // groups
    piece = quarter // CHUNKS
    total_rows = shard * owners
    root = float(total_rows) ** 0.5
    inverse_root = float(total_rows) ** (-0.5)
    place = jnp.stack([group, here // 2, here % 2]).astype(jnp.int32)
    struct = jax.ShapeDtypeStruct

    parts = call(
        sample_kernel,
        [struct((each, shard, rank_full), bf16)] * groups,
        (place, grads, sketch),
        scalars=1,
        us=2.0,
    )
    blocks = call(
        functools.partial(split_kernel, groups=groups, chunks=CHUNKS),
        [struct((count, shard, piece), bf16)] * (groups * CHUNKS),
        (place, grads),
        scalars=1,
        us=2.0,
    )
    parts = [parts[0]] + [swap(parts[k], "dp", k) for k in range(1, groups)]
    moved = []
    for h in range(CHUNKS):
        mine = blocks[h * groups : (h + 1) * groups]
        moved.append([mine[0]] + [swap(mine[k], "dp", k) for k in range(1, groups)])

    picked, lent = call(
        pick_kernel,
        [struct((chips, 2, rank_full, quarter), bf16)] * 2,
        (place, owner, first_moment, second_moment),
        scalars=2,
        us=2.5,
    )
    lent = swap(lent, "rows", 1)
    sample = call(sum_kernel, struct((each, shard, rank_full), bf16), tuple(parts), us=0.5)
    samples = [sample] + [swap(sample, "rows", 2 * k) for k in range(1, chips)]
    ready = call(
        merge_kernel,
        [struct((2, rank_full, quarter), bf16)] * chips,
        (place, owner, picked, lent),
        scalars=2,
        us=1.5,
    )
    moments = [ready[0]] + [swap(ready[k], "rows", 2 * k) for k in range(1, chips)]
    gram = call(
        gram_kernel, struct((each, rank_full, rank_full), f32), tuple(samples), us=1.0
    )
    rows_basis = factor(gram, swap(gram, "rows", 1), sample, root)

    deltas, gathered = [], []
    for h in range(CHUNKS):
        mine, other = call(
            functools.partial(project_kernel, scale=inverse_root),
            [struct((chips, rank_full, piece), f32), struct((chips, rank_full, piece), bf16)],
            (place, *moved[h], basis),
            scalars=1,
            us=2.0,
        )
        other = swap(other, "rows", 1)
        terms = call(
            pair_kernel,
            [struct((rank_full, piece), f32)] + [struct((rank_full, piece), bf16)] * (chips - 1),
            (place, mine, other),
            scalars=1,
            us=0.7,
        )
        terms = [terms[0]] + [swap(terms[k], "rows", 2 * k) for k in range(1, chips)]
        update, projected = call(
            functools.partial(update_kernel, chips=chips, start=h * piece),
            [struct((rank_full, piece), bf16)] * 2,
            (place, owner, rank, *terms, *moments),
            scalars=3,
            us=0.7,
        )
        near = [update] + [swap(update, "rows", 2 * k) for k in range(1, chips)]
        far = [swap(x, "rows", 1) for x in near]
        gathered.append(lax.all_gather(projected, "rows", axis=0))
        delta = call(
            functools.partial(delta_kernel, chips=chips, scale=inverse_root),
            struct((count, shard, piece), bf16),
            (place, *near, *far, basis),
            scalars=1,
            us=1.5,
        )
        deltas += [delta] + [swap(delta, "dp", k) for k in range(1, groups)]

    first_out, second_out = call(
        functools.partial(moment_kernel, chunks=CHUNKS),
        [struct(first_moment.shape, f32)] * 2,
        (place, owner, *gathered, first_moment, second_moment),
        scalars=2,
        us=3.0,
    )
    shared = [rows_basis] + [swap(rows_basis, "dp", k) for k in range(1, groups)]
    new_basis = call(
        basis_kernel, struct(basis.shape, f32), (place, *shared), scalars=1, us=1.5
    )
    new_weight = call(
        functools.partial(weight_kernel, groups=groups, chunks=CHUNKS),
        struct(weight.shape, bf16),
        (place, weight, *deltas),
        scalars=1,
        us=3.0,
    )
    return (new_weight, new_basis, first_out, second_out)


def solution(mesh):
    in_specs = (
        P("dp", None, "rows", None),
        P(None, "rows", None),
        P(None, "rows", None),
        P("rows", None, "dp"),
        P("rows", None, "dp"),
        P(),
        P(),
        P(),
    )
    out_specs = (
        P(None, "rows", None),
        P(None, "rows", None),
        P("rows", None, "dp"),
        P("rows", None, "dp"),
    )
    return jax.shard_map(
        per_device, mesh=mesh, in_specs=in_specs, out_specs=out_specs, check_vma=False
    )
```

```python
import functools

import jax
import jax.numpy as jnp
from jax import lax
from jax.experimental import pallas as pl
from jax.experimental.pallas import tpu as pltpu
from jax.sharding import PartitionSpec as P

beta_one = 0.9
beta_two = 0.95
bias_one = 1.0 - 0.9**10
bias_two = 1.0 - 0.95**10
step_size = 0.5
epsilon = 1e-08
BLOCK = 64
CHUNKS = 1
HIGHEST = lax.Precision.HIGHEST
VMEM_LIMIT = 48 * 1024 * 1024
VMEM = pl.BlockSpec(memory_space=pltpu.VMEM)
SMEM = pl.BlockSpec(memory_space=pltpu.SMEM)
f32 = jnp.float32
bf16 = jnp.bfloat16


class Sequence:
    def __init__(self):
        self.last = None

    def __call__(self, kernel, out_shape, args, scalars=0, us=2.0, scratch=()):
        many = isinstance(out_shape, (tuple, list))
        specs = [SMEM] * scalars + [VMEM] * (len(args) - scalars)
        body = kernel
        if self.last is not None:
            specs = [pl.BlockSpec(memory_space=pl.ANY)] + specs
            args = (self.last, *args)

            def body(_, *refs):
                kernel(*refs)

        result = pl.pallas_call(
            body,
            out_shape=out_shape,
            in_specs=specs,
            out_specs=[VMEM] * len(out_shape) if many else VMEM,
            scratch_shapes=list(scratch),
            compiler_params=pltpu.CompilerParams(vmem_limit_bytes=VMEM_LIMIT),
            cost_estimate=pl.CostEstimate(
                flops=0, bytes_accessed=int(us * 3_000_000), transcendentals=0
            ),
        )(*args)
        self.last = result[-1] if many else result
        return result


def swap(x, axis, mask):
    size = lax.axis_size(axis)
    return lax.ppermute(x, axis, [(i, i ^ mask) for i in range(size)])


def split_kernel(place, grad_ref, *outs, groups, chunks):
    width = outs[0].shape[2]
    for h in range(chunks):
        for k in range(groups):
            start = ((place[0] ^ k) * chunks + h) * width
            columns = pl.ds(pl.multiple_of(start, 128), width)
            outs[h * groups + k][...] = grad_ref[0, :, :, columns]


def sample_kernel(place, grad_ref, sketch_ref, *outs):
    each = outs[0].shape[0]
    for k, out in enumerate(outs):
        for i in range(each):
            m = (place[0] ^ k) * each + i
            out[i] = jnp.dot(
                grad_ref[0, m], sketch_ref[...], preferred_element_type=f32
            ).astype(bf16)


def sum_kernel(*refs):
    out = refs[-1]
    total = refs[0][...].astype(f32)
    for ref in refs[1:-1]:
        total = total + ref[...].astype(f32)
    out[...] = total.astype(bf16)


def stack_kernel(own_ref, other_ref, out_ref):
    half = own_ref.shape[0]
    out_ref[:half] = own_ref[...]
    out_ref[half:] = other_ref[...]


def gram_kernel(*refs):
    out = refs[-1]
    each = out.shape[0]
    for i in range(each):
        total = None
        for ref in refs[:-1]:
            for j in range(i, ref.shape[0], each):
                block = ref[j]
                term = lax.dot_general(
                    block, block, (((0,), (0,)), ((), ())), preferred_element_type=f32
                )
                total = term if total is None else total + term
        out[i] = total


def eliminate(work, j):
    pair, size = work.shape[0], work.shape[1]
    lane = lax.broadcasted_iota(jnp.int32, (BLOCK, 2 * BLOCK), 1)
    sub = lax.broadcasted_iota(jnp.int32, (BLOCK, 2 * BLOCK), 0)
    eye_right = (lane - BLOCK == sub).astype(f32)
    lo = j * BLOCK
    base = lo // 128 * 128
    tiles = []
    for b in range(pair):
        slab = work[b, lo : lo + BLOCK, base : base + 128]
        if lo > base:
            slab = pltpu.roll(slab, 128 - (lo - base), 1)
        tiles.append(jnp.where(lane < BLOCK, slab, eye_right))
    for k in range(BLOCK - 1):
        for b in range(pair):
            tile = tiles[b]
            column = jnp.where(sub[:, :1] > k, tile[:, k : k + 1], 0.0)
            row = tile[k : k + 1, :] * (1.0 / tile[k : k + 1, k : k + 1])
            tiles[b] = tile - column * row
    for b in range(pair):
        tile = tiles[b]
        diagonal = jnp.sum(jnp.where(lane == sub, tile, 0.0), axis=1, keepdims=True)
        inverse = pltpu.roll(tile, BLOCK, 1)[:, :BLOCK] * lax.rsqrt(diagonal)
        solved = jnp.dot(
            inverse, work[b, lo : lo + BLOCK, :], precision=HIGHEST, preferred_element_type=f32
        )
        work[b, lo : lo + BLOCK, size:] = solved[:, size:]
        if lo + BLOCK < size:
            change = lax.dot_general(
                solved[:, :size],
                solved,
                (((0,), (0,)), ((), ())),
                precision=HIGHEST,
                preferred_element_type=f32,
            )
            work[b, lo + BLOCK :, :] = work[b, lo + BLOCK :, :] - change[lo + BLOCK :, :]


def start_kernel(own_ref, other_ref, work):
    pair, size = own_ref.shape[0], own_ref.shape[1]
    row = lax.broadcasted_iota(jnp.int32, (size, size), 0)
    col = lax.broadcasted_iota(jnp.int32, (size, size), 1)
    eye = (row == col).astype(f32)
    for b in range(pair):
        work[b, :, :size] = own_ref[b] + other_ref[b]
        work[b, :, size:] = eye
    eliminate(work, 0)


def middle_kernel(work_in, work, *, j):
    work[...] = work_in[...]
    eliminate(work, j)


def finish_kernel(work_in, rows_ref, out_ref, work, *, j, scale):
    work[...] = work_in[...]
    eliminate(work, j)
    size = work.shape[1]
    for b in range(work.shape[0]):
        basis = lax.dot_general(
            rows_ref[b].astype(f32),
            work[b, :, size:],
            (((1,), (1,)), ((), ())),
            precision=HIGHEST,
            preferred_element_type=f32,
        )
        out_ref[b] = (basis * scale).astype(out_ref.dtype)


def pick_kernel(place, owner, first_ref, second_ref, mine_ref, other_ref):
    here, core = place[1] * 2 + place[2], place[2]
    capacity = first_ref.shape[0]
    seen = jnp.int32(0)
    at = []
    for m in range(owner.shape[0]):
        at.append(jnp.minimum(seen, capacity - 1))
        seen = seen + (owner[m] == here).astype(jnp.int32)
    chips = mine_ref.shape[0]
    for i in range(chips):
        for out, want in ((mine_ref, core), (other_ref, 1 - core)):
            slot = jnp.int32(0)
            m = 2 * (place[1] ^ i) + want
            for j in range(owner.shape[0]):
                slot = jnp.where(m == j, at[j], slot)
            out[i, 0] = first_ref[slot].astype(bf16)
            out[i, 1] = second_ref[slot].astype(bf16)


def merge_kernel(place, owner, mine_ref, other_ref, *outs, bit):
    z, core = place[1], place[2]
    stride = 1 if bit < 0 else 2 << bit
    split = len(outs)
    for i in range(mine_ref.shape[0]):
        source = owner[2 * (z ^ (i * stride)) + core]
        if bit < 0:
            local = (source & 1) == core
        else:
            local = (((source >> 1) ^ z) >> bit) & 1 == 0
        outs[i % split][i // split] = jnp.where(local, mine_ref[i], other_ref[i])


def project_kernel(place, *refs, scale):
    *grad_refs, basis_ref, mine_ref, other_ref = refs
    core = place[2]
    for i in range(mine_ref.shape[0]):
        for out, want in ((other_ref, 1 - core), (mine_ref, core)):
            m = 2 * i + want
            total = grad_refs[0][m].astype(f32)
            for ref in grad_refs[1:]:
                total = total + ref[m].astype(f32)
            product = lax.dot_general(
                (basis_ref[m] * scale).astype(bf16),
                total.astype(bf16),
                (((0,), (0,)), ((), ())),
                preferred_element_type=f32,
            )
            out[i] = product.astype(out.dtype)


def pair_kernel(place, mine_ref, other_ref, *outs):
    for k, out in enumerate(outs):
        i = place[1] ^ k
        out[...] = (mine_ref[i] + other_ref[i].astype(f32)).astype(out.dtype)


def update_kernel(place, rank, *refs, chips, start):
    terms = refs[:chips]
    moment_ref, update_ref, projected_ref = refs[chips:]
    z, core = place[1], place[2]
    m = 2 * z + core
    projected = terms[0][...].astype(f32)
    for ref in terms[1:]:
        projected = projected + ref[...].astype(f32)
    width = projected.shape[1]
    columns = slice(start, start + width)
    first = moment_ref[0, 0, :, columns]
    second = moment_ref[0, 1, :, columns]
    first_new = beta_one * first.astype(f32) + (1.0 - beta_one) * projected
    second_new = beta_two * second.astype(f32) + (1.0 - beta_two) * projected * projected
    update = (first_new / bias_one) / (jnp.sqrt(second_new / bias_two) + epsilon)
    row = lax.broadcasted_iota(jnp.int32, update.shape, 0)
    update_ref[...] = jnp.where(row < rank[m], update, 0.0).astype(bf16)
    projected_ref[...] = projected.astype(bf16)


def delta_kernel(place, *refs, chips, scale):
    near, far = refs[:chips], refs[chips : 2 * chips]
    basis_ref, out_ref = refs[2 * chips :]
    z, core = place[1], place[2]
    for k in range(chips):
        for ref, want in ((near[k], core), (far[k], 1 - core)):
            m = 2 * (z ^ k) + want
            product = jnp.dot(
                (basis_ref[m] * scale).astype(bf16), ref[...], preferred_element_type=f32
            )
            out_ref[m] = product.astype(bf16)


def weight_kernel(place, weight_ref, *refs, groups, chunks):
    out_ref = refs[-1]
    width = refs[0].shape[2]
    for h in range(chunks):
        for k in range(groups):
            start = ((place[0] ^ k) * chunks + h) * width
            columns = pl.ds(pl.multiple_of(start, 128), width)
            for m in range(out_ref.shape[0]):
                delta = refs[h * groups + k][m].astype(f32)
                old = weight_ref[m, :, columns].astype(f32)
                out_ref[m, :, columns] = (old - step_size * delta).astype(bf16)


def basis_kernel(place, *refs):
    out_ref = refs[-1]
    each = refs[0].shape[0]
    for k, ref in enumerate(refs[:-1]):
        for i in range(each):
            out_ref[(place[0] ^ k) * each + i] = ref[i].astype(f32)


def moment_kernel(place, owner, *refs, chunks):
    projected_refs = refs[:chunks]
    first_ref, second_ref, first_out, second_out = refs[chunks:]
    here = place[1] * 2 + place[2]
    capacity, rank_full, _ = first_out.shape
    width = projected_refs[0].shape[2]
    seen = jnp.int32(0)
    index = [jnp.int32(0)] * capacity
    for m in range(owner.shape[0]):
        hit = owner[m] == here
        for s in range(capacity):
            index[s] = jnp.where(hit & (seen == s), m, index[s])
        seen = seen + hit.astype(jnp.int32)
    for s in range(capacity):
        keep = seen > s
        for h in range(chunks):
            columns = slice(h * width, (h + 1) * width)
            projected = projected_refs[h][index[s]].astype(f32)
            first_new = beta_one * first_ref[s, :, columns] + (1.0 - beta_one) * projected
            second_new = (
                beta_two * second_ref[s, :, columns] + (1.0 - beta_two) * projected * projected
            )
            first_out[s, :, columns] = jnp.where(keep, first_new, 0.0)
            second_out[s, :, columns] = jnp.where(keep, second_new, 0.0)


def per_device(grads, weight, basis, first_moment, second_moment, sketch, owner, rank):
    owners = lax.axis_size("rows")
    groups = lax.axis_size("dp")
    here = lax.axis_index("rows")
    group = lax.axis_index("dp")
    capacity, rank_full, quarter = first_moment.shape
    count, shard, width = weight.shape
    chips = owners // 2
    each = count // groups
    piece = quarter // CHUNKS
    total_rows = shard * owners
    root = float(total_rows) ** 0.5
    inverse_root = float(total_rows) ** (-0.5)
    place = jnp.stack([group, here // 2, here % 2]).astype(jnp.int32)
    struct = jax.ShapeDtypeStruct

    call = Sequence()
    parts = call(
        sample_kernel,
        [struct((each, shard, rank_full), bf16)] * groups,
        (place, grads, sketch),
        scalars=1,
        us=2.0,
    )
    parts = [parts[0]] + [swap(parts[k], "dp", k) for k in range(1, groups)]
    blocks = call(
        functools.partial(split_kernel, groups=groups, chunks=CHUNKS),
        [struct((count, shard, piece), bf16)] * (groups * CHUNKS),
        (place, grads),
        scalars=1,
        us=2.0,
    )
    moved = []
    for h in range(CHUNKS):
        mine = blocks[h * groups : (h + 1) * groups]
        moved.append([mine[0]] + [swap(mine[k], "dp", k) for k in range(1, groups)])
    sample = call(sum_kernel, struct((each, shard, rank_full), bf16), tuple(parts), us=0.5)
    stacked = sample
    mask = 1
    while mask < chips // 2:
        other = swap(stacked, "rows", 2 * mask)
        both = struct((2 * stacked.shape[0], shard, rank_full), bf16)
        stacked = call(stack_kernel, both, (stacked, other), us=0.5)
        mask *= 2
    far_samples = swap(stacked, "rows", 2 * mask)

    moment_shape = struct((chips, 2, rank_full, quarter), bf16)
    moments, lent = call(
        pick_kernel,
        [moment_shape] * 2,
        (place, owner, first_moment, second_moment),
        scalars=2,
        us=2.0,
    )
    lent = swap(lent, "rows", 1)
    halves = [struct((chips // 2, 2, rank_full, quarter), bf16)] * 2
    moments, lent_next = call(
        functools.partial(merge_kernel, bit=-1),
        halves,
        (place, owner, moments, lent),
        scalars=2,
        us=1.0,
    )
    lent = swap(lent_next, "rows", 2)
    gram = call(
        gram_kernel,
        struct((each, rank_full, rank_full), f32),
        (stacked, far_samples),
        us=1.0,
    )
    other_gram = swap(gram, "rows", 1)
    bit = 0
    while moments.shape[0] > 1:
        halves = [struct((moments.shape[0] // 2, 2, rank_full, quarter), bf16)] * 2
        moments, lent_next = call(
            functools.partial(merge_kernel, bit=bit),
            halves,
            (place, owner, moments, lent),
            scalars=2,
            us=1.0,
        )
        bit += 1
        lent = swap(lent_next, "rows", 2 << bit)
    work_shape = struct((each, rank_full, 2 * rank_full), f32)
    work = call(start_kernel, work_shape, (gram, other_gram), us=8.0)
    last = rank_full // BLOCK - 1

    deltas, gathered = [], []
    h = 0
    mine, other = call(
        functools.partial(project_kernel, scale=inverse_root),
        [struct((chips, rank_full, piece), f32), struct((chips, rank_full, piece), bf16)],
        (place, *moved[h], basis),
        scalars=1,
        us=2.0,
    )
    other = swap(other, "rows", 1)
    terms = call(
        pair_kernel,
        [struct((rank_full, piece), f32)] + [struct((rank_full, piece), bf16)] * (chips - 1),
        (place, mine, other),
        scalars=1,
        us=0.7,
    )
    terms = [terms[0]] + [swap(terms[k], "rows", 2 * k) for k in range(1, chips)]
    for j in range(1, 2):
        work = call(functools.partial(middle_kernel, j=j), work_shape, (work,), us=8.0)
    moments = call(
        functools.partial(merge_kernel, bit=bit),
        [struct((1, 2, rank_full, quarter), bf16)],
        (place, owner, moments, lent),
        scalars=2,
        us=0.5,
    )[0]
    update, projected = call(
        functools.partial(update_kernel, chips=chips, start=h * piece),
        [struct((rank_full, piece), bf16)] * 2,
        (place, rank, *terms, moments),
        scalars=2,
        us=0.7,
    )
    near = [update] + [swap(update, "rows", 2 * k) for k in range(1, chips)]
    far = [swap(x, "rows", 1) for x in near]
    gathered.append(lax.all_gather(projected, "rows", axis=0))
    for j in range(2, last):
        work = call(functools.partial(middle_kernel, j=j), work_shape, (work,), us=8.0)
    rows_basis = call(
        functools.partial(finish_kernel, j=last, scale=root),
        struct(sample.shape, bf16),
        (work, sample),
        us=6.0,
        scratch=[pltpu.VMEM(work_shape.shape, f32)],
    )
    delta = call(
        functools.partial(delta_kernel, chips=chips, scale=inverse_root),
        struct((count, shard, piece), bf16),
        (place, *near, *far, basis),
        scalars=1,
        us=1.5,
    )
    deltas += [delta] + [swap(delta, "dp", k) for k in range(1, groups)]
    shared = [rows_basis] + [swap(rows_basis, "dp", k) for k in range(1, groups)]
    first_out, second_out = call(
        functools.partial(moment_kernel, chunks=CHUNKS),
        [struct(first_moment.shape, f32)] * 2,
        (place, owner, *gathered, first_moment, second_moment),
        scalars=2,
        us=3.0,
    )
    new_basis = call(
        basis_kernel, struct(basis.shape, f32), (place, *shared), scalars=1, us=1.5
    )
    new_weight = call(
        functools.partial(weight_kernel, groups=groups, chunks=CHUNKS),
        struct(weight.shape, bf16),
        (place, weight, *deltas),
        scalars=1,
        us=3.0,
    )
    return (new_weight, new_basis, first_out, second_out)


def solution(mesh):
    in_specs = (
        P("dp", None, "rows", None),
        P(None, "rows", None),
        P(None, "rows", None),
        P("rows", None, "dp"),
        P("rows", None, "dp"),
        P(),
        P(),
        P(),
    )
    out_specs = (
        P(None, "rows", None),
        P(None, "rows", None),
        P("rows", None, "dp"),
        P("rows", None, "dp"),
    )
    return jax.shard_map(
        per_device, mesh=mesh, in_specs=in_specs, out_specs=out_specs, check_vma=False
    )
```

```python
import functools

import jax
import jax.numpy as jnp
from jax import lax
from jax.experimental import pallas as pl
from jax.experimental.pallas import tpu as pltpu
from jax.sharding import PartitionSpec as P

beta_one = 0.9
beta_two = 0.95
bias_one = 1.0 - 0.9**10
bias_two = 1.0 - 0.95**10
step_size = 0.5
epsilon = 1e-08
BLOCK = 64
COST = 10_000
HIGHEST = lax.Precision.HIGHEST
VMEM_LIMIT = 48 * 1024 * 1024
VMEM = pl.BlockSpec(memory_space=pltpu.VMEM)
SMEM = pl.BlockSpec(memory_space=pltpu.SMEM)
f32 = jnp.float32
bf16 = jnp.bfloat16


class Sequence:
    def __init__(self):
        self.last = None

    def __call__(self, kernel, out_shape, args, scalars=0, us=2.0, scratch=(), after=()):
        many = isinstance(out_shape, (tuple, list))
        specs = [SMEM] * scalars + [VMEM] * (len(args) - scalars)
        body = kernel
        if self.last is not None:
            after = (self.last, *after)
        unread = len(after)
        if unread:
            specs = [pl.BlockSpec(memory_space=pl.ANY)] * unread + specs
            args = (*after, *args)

            def body(*refs):
                kernel(*refs[unread:])

        result = pl.pallas_call(
            body,
            out_shape=out_shape,
            in_specs=specs,
            out_specs=[VMEM] * len(out_shape) if many else VMEM,
            scratch_shapes=list(scratch),
            compiler_params=pltpu.CompilerParams(vmem_limit_bytes=VMEM_LIMIT),
            cost_estimate=pl.CostEstimate(
                flops=0, bytes_accessed=int(us * COST), transcendentals=0
            ),
        )(*args)
        self.last = result[-1] if many else result
        return result


def swap(x, axis, mask):
    size = lax.axis_size(axis)
    return lax.ppermute(x, axis, [(i, i ^ mask) for i in range(size)])


def split_kernel(place, grad_ref, *outs, groups, chunks):
    width = outs[0].shape[2]
    for h in range(chunks):
        for k in range(groups):
            start = ((place[0] ^ k) * chunks + h) * width
            columns = pl.ds(pl.multiple_of(start, 128), width)
            outs[h * groups + k][...] = grad_ref[0, :, :, columns]


def sample_kernel(place, grad_ref, sketch_ref, keep_ref, send_ref):
    half, each = keep_ref.shape[0], keep_ref.shape[1]
    for k in range(2 * half):
        out = (keep_ref, send_ref)[k % 2]
        for i in range(each):
            m = (place[0] ^ k) * each + i
            product = jnp.dot(grad_ref[0, m], sketch_ref[...], preferred_element_type=f32)
            out[k // 2, i] = product.astype(out.dtype)


def halve_kernel(keep_ref, other_ref, *outs):
    for k in range(keep_ref.shape[0]):
        total = keep_ref[k] + other_ref[k].astype(f32)
        out = outs[k % len(outs)]
        out[k // len(outs)] = total.astype(out.dtype)


def add_kernel(*refs):
    out = refs[-1]
    for m in range(out.shape[0]):
        total = refs[0][m].astype(f32)
        for ref in refs[1:-1]:
            total = total + ref[m].astype(f32)
        out[m] = total


def stack_kernel(own_ref, other_ref, out_ref):
    half = own_ref.shape[0]
    out_ref[:half] = own_ref[...]
    out_ref[half:] = other_ref[...]


def gather_kernel(*refs):
    for k, ref in enumerate(refs[:-1]):
        refs[-1][k] = ref[...]


def gram_kernel(*refs):
    out = refs[-1]
    each = out.shape[0]
    for i in range(each):
        total = None
        for ref in refs[:-1]:
            for j in range(i, ref.shape[0], each):
                block = ref[j]
                term = lax.dot_general(
                    block, block, (((0,), (0,)), ((), ())), preferred_element_type=f32
                )
                total = term if total is None else total + term
        out[i] = total


def eliminate(work, j):
    pair, size = work.shape[0], work.shape[1]
    lane = lax.broadcasted_iota(jnp.int32, (BLOCK, 2 * BLOCK), 1)
    sub = lax.broadcasted_iota(jnp.int32, (BLOCK, 2 * BLOCK), 0)
    eye_right = (lane - BLOCK == sub).astype(f32)
    lo = j * BLOCK
    base = lo // 128 * 128
    tiles = []
    for b in range(pair):
        slab = work[b, lo : lo + BLOCK, base : base + 128]
        if lo > base:
            slab = pltpu.roll(slab, 128 - (lo - base), 1)
        tiles.append(jnp.where(lane < BLOCK, slab, eye_right))
    for k in range(BLOCK - 1):
        for b in range(pair):
            tile = tiles[b]
            column = jnp.where(sub[:, :1] > k, tile[:, k : k + 1], 0.0)
            row = tile[k : k + 1, :] * (1.0 / tile[k : k + 1, k : k + 1])
            tiles[b] = tile - column * row
    for b in range(pair):
        tile = tiles[b]
        diagonal = jnp.sum(jnp.where(lane == sub, tile, 0.0), axis=1, keepdims=True)
        inverse = pltpu.roll(tile, BLOCK, 1)[:, :BLOCK] * lax.rsqrt(diagonal)
        solved = jnp.dot(
            inverse, work[b, lo : lo + BLOCK, :], precision=HIGHEST, preferred_element_type=f32
        )
        work[b, lo : lo + BLOCK, size:] = solved[:, size:]
        if lo + BLOCK < size:
            change = lax.dot_general(
                solved[:, :size],
                solved,
                (((0,), (0,)), ((), ())),
                precision=HIGHEST,
                preferred_element_type=f32,
            )
            work[b, lo + BLOCK :, :] = work[b, lo + BLOCK :, :] - change[lo + BLOCK :, :]


def start_kernel(own_ref, other_ref, work):
    pair, size = own_ref.shape[0], own_ref.shape[1]
    row = lax.broadcasted_iota(jnp.int32, (size, size), 0)
    col = lax.broadcasted_iota(jnp.int32, (size, size), 1)
    eye = (row == col).astype(f32)
    for b in range(pair):
        work[b, :, :size] = own_ref[b] + other_ref[b]
        work[b, :, size:] = eye
    eliminate(work, 0)


def middle_kernel(work_in, work, *, j):
    work[...] = work_in[...]
    eliminate(work, j)


def finish_kernel(work_in, rows_ref, out_ref, work, *, j, scale):
    work[...] = work_in[...]
    eliminate(work, j)
    size = work.shape[1]
    for b in range(work.shape[0]):
        basis = lax.dot_general(
            rows_ref[b].astype(f32),
            work[b, :, size:],
            (((1,), (1,)), ((), ())),
            precision=HIGHEST,
            preferred_element_type=f32,
        )
        out_ref[b] = (basis * scale).astype(out_ref.dtype)


def pick_kernel(place, owner, first_ref, second_ref, mine_ref, other_ref):
    here, core = place[1] * 2 + place[2], place[2]
    capacity = first_ref.shape[0]
    seen = jnp.int32(0)
    at = []
    for m in range(owner.shape[0]):
        at.append(jnp.minimum(seen, capacity - 1))
        seen = seen + (owner[m] == here).astype(jnp.int32)
    chips = mine_ref.shape[0]
    for i in range(chips):
        for out, want in ((mine_ref, core), (other_ref, 1 - core)):
            slot = jnp.int32(0)
            m = 2 * (place[1] ^ i) + want
            for j in range(owner.shape[0]):
                slot = jnp.where(m == j, at[j], slot)
            out[i, 0] = first_ref[slot].astype(bf16)
            out[i, 1] = second_ref[slot].astype(bf16)


def merge_kernel(place, owner, mine_ref, other_ref, *outs, bit):
    z, core = place[1], place[2]
    stride = 1 if bit < 0 else 2 << bit
    split = len(outs)
    for i in range(mine_ref.shape[0]):
        source = owner[2 * (z ^ (i * stride)) + core]
        if bit < 0:
            local = (source & 1) == core
        else:
            local = (((source >> 1) ^ z) >> bit) & 1 == 0
        outs[i % split][i // split] = jnp.where(local, mine_ref[i], other_ref[i])


def project_kernel(place, *refs, scale):
    *grad_refs, basis_ref, mine_ref, other_ref = refs
    core = place[2]
    for i in range(mine_ref.shape[0]):
        for out, want in ((other_ref, 1 - core), (mine_ref, core)):
            m = 2 * i + want
            total = grad_refs[0][m].astype(f32)
            for ref in grad_refs[1:]:
                total = total + ref[m].astype(f32)
            product = lax.dot_general(
                (basis_ref[m] * scale).astype(bf16),
                total.astype(bf16),
                (((0,), (0,)), ((), ())),
                preferred_element_type=f32,
            )
            out[i] = product.astype(out.dtype)


def pair_kernel(place, mine_ref, other_ref, *outs):
    for k, out in enumerate(outs):
        i = place[1] ^ k
        out[...] = (mine_ref[i] + other_ref[i].astype(f32)).astype(out.dtype)


def update_kernel(place, owner, rank, *refs, chips, bit, start):
    terms = refs[:chips]
    moment_ref, lent_ref, update_ref, projected_ref = refs[chips:]
    z, core = place[1], place[2]
    m = 2 * z + core
    projected = terms[0][...].astype(f32)
    for ref in terms[1:]:
        projected = projected + ref[...].astype(f32)
    width = projected.shape[1]
    columns = slice(start, start + width)
    local = (((owner[m] >> 1) ^ z) >> bit) & 1 == 0
    first = jnp.where(local, moment_ref[0, 0, :, columns], lent_ref[0, 0, :, columns])
    second = jnp.where(local, moment_ref[0, 1, :, columns], lent_ref[0, 1, :, columns])
    first_new = beta_one * first.astype(f32) + (1.0 - beta_one) * projected
    second_new = beta_two * second.astype(f32) + (1.0 - beta_two) * projected * projected
    update = (first_new / bias_one) / (jnp.sqrt(second_new / bias_two) + epsilon)
    row = lax.broadcasted_iota(jnp.int32, update.shape, 0)
    update_ref[...] = jnp.where(row < rank[m], update, 0.0).astype(bf16)
    projected_ref[...] = projected.astype(bf16)


def delta_kernel(place, *refs, chips, scale):
    near, far, basis_ref, projected_ref, out_ref, passed_ref = refs
    z, core = place[1], place[2]
    passed_ref[...] = projected_ref[...]
    for k in range(chips):
        for ref, want in ((near, core), (far, 1 - core)):
            m = 2 * (z ^ k) + want
            product = jnp.dot(
                (basis_ref[m] * scale).astype(bf16), ref[k], preferred_element_type=f32
            )
            out_ref[m] = product.astype(bf16)


def weight_kernel(place, weight_ref, *refs, groups, chunks):
    out_ref = refs[-1]
    width = refs[0].shape[2]
    for h in range(chunks):
        for k in range(groups):
            start = ((place[0] ^ k) * chunks + h) * width
            columns = pl.ds(pl.multiple_of(start, 128), width)
            for m in range(out_ref.shape[0]):
                delta = refs[h * groups + k][m].astype(f32)
                old = weight_ref[m, :, columns].astype(f32)
                out_ref[m, :, columns] = (old - step_size * delta).astype(bf16)


def basis_kernel(place, *refs):
    out_ref = refs[-1]
    each = refs[0].shape[0]
    for k, ref in enumerate(refs[:-1]):
        for i in range(each):
            out_ref[(place[0] ^ k) * each + i] = ref[i].astype(f32)


def moment_kernel(place, owner, *refs, chunks):
    projected_refs = refs[:chunks]
    first_ref, second_ref, first_out, second_out = refs[chunks:]
    here = place[1] * 2 + place[2]
    capacity, rank_full, _ = first_out.shape
    width = projected_refs[0].shape[2]
    seen = jnp.int32(0)
    index = [jnp.int32(0)] * capacity
    for m in range(owner.shape[0]):
        hit = owner[m] == here
        for s in range(capacity):
            index[s] = jnp.where(hit & (seen == s), m, index[s])
        seen = seen + hit.astype(jnp.int32)
    for s in range(capacity):
        keep = seen > s
        for h in range(chunks):
            columns = slice(h * width, (h + 1) * width)
            projected = projected_refs[h][index[s]].astype(f32)
            first_new = beta_one * first_ref[s, :, columns] + (1.0 - beta_one) * projected
            second_new = (
                beta_two * second_ref[s, :, columns] + (1.0 - beta_two) * projected * projected
            )
            first_out[s, :, columns] = jnp.where(keep, first_new, 0.0)
            second_out[s, :, columns] = jnp.where(keep, second_new, 0.0)


def per_device(grads, weight, basis, first_moment, second_moment, sketch, owner, rank):
    owners = lax.axis_size("rows")
    groups = lax.axis_size("dp")
    here = lax.axis_index("rows")
    group = lax.axis_index("dp")
    capacity, rank_full, quarter = first_moment.shape
    count, shard, width = weight.shape
    chips = owners // 2
    each = count // groups
    total_rows = shard * owners
    root = float(total_rows) ** 0.5
    inverse_root = float(total_rows) ** (-0.5)
    place = jnp.stack([group, here // 2, here % 2]).astype(jnp.int32)
    struct = jax.ShapeDtypeStruct

    call = Sequence()
    half = chips
    moments, lent = call(
        pick_kernel,
        [struct((half, 2, rank_full, quarter), bf16)] * 2,
        (place, owner, first_moment, second_moment),
        scalars=2,
    )
    lent = swap(lent, "rows", 1)
    blocks = call(
        functools.partial(split_kernel, groups=groups, chunks=1),
        [struct((count, shard, quarter), bf16)] * groups,
        (place, grads),
        scalars=1,
    )
    keep, send = call(
        sample_kernel,
        [struct((groups // 2, each, shard, rank_full), kind) for kind in (f32, bf16)],
        (place, grads, sketch),
        scalars=1,
    )
    half //= 2
    moments, lent = call(
        functools.partial(merge_kernel, bit=-1),
        [struct((half, 2, rank_full, quarter), bf16)] * 2,
        (place, owner, moments, lent),
        scalars=2,
    )
    lent = swap(lent, "rows", 2)
    sides = [1 << i for i in range(groups.bit_length() - 1)]
    corners = [k for k in range(1, groups) if k not in sides]
    beside = [swap(blocks[k], "dp", k) for k in sides]
    send = swap(send, "dp", 1)
    part = groups // 2
    mask = 1
    while part > 1:
        part //= 2
        keep, send = call(
            halve_kernel,
            [struct((part, each, shard, rank_full), kind) for kind in (f32, bf16)],
            (keep, send),
        )
        mask *= 2
        send = swap(send, "dp", mask)
    total = call(add_kernel, struct((count, shard, quarter), f32), (blocks[0], *beside))
    across = [swap(blocks[k], "dp", k) for k in corners]
    bit = 0
    while half > 1:
        half //= 2
        moments, lent = call(
            functools.partial(merge_kernel, bit=bit),
            [struct((half, 2, rank_full, quarter), bf16)] * 2,
            (place, owner, moments, lent),
            scalars=2,
        )
        bit += 1
        lent = swap(lent, "rows", 2 << bit)
    sample = call(
        halve_kernel,
        [struct((1, each, shard, rank_full), bf16)],
        (keep, send),
    )[0].reshape(each, shard, rank_full)
    mine, other = call(
        functools.partial(project_kernel, scale=inverse_root),
        [struct((chips, rank_full, quarter), f32), struct((chips, rank_full, quarter), bf16)],
        (place, total, *across, basis),
        scalars=1,
        after=(lent,),
    )
    other = swap(other, "rows", 1)
    mask = 1
    arrived = swap(sample, "rows", 2)
    terms = call(
        pair_kernel,
        [struct((rank_full, quarter), f32)] + [struct((rank_full, quarter), bf16)] * (chips - 1),
        (place, mine, other),
        scalars=1,
    )
    terms = [terms[0]] + [swap(terms[k], "rows", 2 * k) for k in range(1, chips)]
    stacked = sample
    while mask < chips // 2:
        both = struct((2 * stacked.shape[0], shard, rank_full), bf16)
        stacked = call(stack_kernel, both, (stacked, arrived))
        mask *= 2
        arrived = swap(stacked, "rows", 2 * mask)
    work_shape = struct((each, rank_full, 2 * rank_full), f32)
    last = rank_full // BLOCK - 1
    update, projected = call(
        functools.partial(update_kernel, chips=chips, bit=bit, start=0),
        [struct((rank_full, quarter), bf16)] * 2,
        (place, owner, rank, *terms, moments, lent),
        scalars=3,
    )
    near = [update] + [swap(update, "rows", 2 * k) for k in range(1, chips)]
    gram = call(
        gram_kernel, struct((each, rank_full, rank_full), f32), (stacked, arrived)
    )
    other_gram = swap(gram, "rows", 1)
    work = call(start_kernel, work_shape, (gram, other_gram))
    near = call(gather_kernel, struct((chips, rank_full, quarter), bf16), tuple(near))
    far = swap(near, "rows", 1)
    delta, projected = call(
        functools.partial(delta_kernel, chips=chips, scale=inverse_root),
        [struct((count, shard, quarter), bf16), struct((rank_full, quarter), bf16)],
        (place, near, far, basis, projected),
        scalars=1,
    )
    deltas = [delta] + [swap(delta, "dp", k) for k in range(1, groups)]
    gathered = lax.all_gather(projected, "rows", axis=0)
    for j in range(1, last):
        work = call(functools.partial(middle_kernel, j=j), work_shape, (work,))
    rows_basis = call(
        functools.partial(finish_kernel, j=last, scale=root),
        struct(sample.shape, bf16),
        (work, sample),
        scratch=[pltpu.VMEM(work_shape.shape, f32)],
    )
    shared = [rows_basis] + [swap(rows_basis, "dp", k) for k in range(1, groups)]
    first_out, second_out = call(
        functools.partial(moment_kernel, chunks=1),
        [struct(first_moment.shape, f32)] * 2,
        (place, owner, gathered, first_moment, second_moment),
        scalars=2,
    )
    new_weight = call(
        functools.partial(weight_kernel, groups=groups, chunks=1),
        struct(weight.shape, bf16),
        (place, weight, *deltas),
        scalars=1,
    )
    new_basis = call(basis_kernel, struct(basis.shape, f32), (place, *shared), scalars=1)
    return (new_weight, new_basis, first_out, second_out)


def solution(mesh):
    in_specs = (
        P("dp", None, "rows", None),
        P(None, "rows", None),
        P(None, "rows", None),
        P("rows", None, "dp"),
        P("rows", None, "dp"),
        P(),
        P(),
        P(),
    )
    out_specs = (
        P(None, "rows", None),
        P(None, "rows", None),
        P("rows", None, "dp"),
        P("rows", None, "dp"),
    )
    return jax.shard_map(
        per_device, mesh=mesh, in_specs=in_specs, out_specs=out_specs, check_vma=False
    )
```

```python
import functools

import jax
import jax.numpy as jnp
from jax import lax
from jax.experimental import pallas as pl
from jax.experimental.pallas import tpu as pltpu
from jax.sharding import PartitionSpec as P

beta_one = 0.9
beta_two = 0.95
bias_one = 1.0 - 0.9**10
bias_two = 1.0 - 0.95**10
step_size = 0.5
epsilon = 1e-08
BLOCK = 64
GROUP = 4
COST = 10_000
HIGHEST = lax.Precision.HIGHEST
VMEM_LIMIT = 48 * 1024 * 1024
VMEM = pl.BlockSpec(memory_space=pltpu.VMEM)
SMEM = pl.BlockSpec(memory_space=pltpu.SMEM)
f32 = jnp.float32
bf16 = jnp.bfloat16


class Sequence:
    def __init__(self):
        self.last = None

    def __call__(self, kernel, out_shape, args, scalars=0, us=2.0, scratch=(), after=()):
        many = isinstance(out_shape, (tuple, list))
        specs = [SMEM] * scalars + [VMEM] * (len(args) - scalars)
        body = kernel
        if self.last is not None:
            after = (self.last, *after)
        unread = len(after)
        if unread:
            specs = [pl.BlockSpec(memory_space=pl.ANY)] * unread + specs
            args = (*after, *args)

            def body(*refs):
                kernel(*refs[unread:])

        result = pl.pallas_call(
            body,
            out_shape=out_shape,
            in_specs=specs,
            out_specs=[VMEM] * len(out_shape) if many else VMEM,
            scratch_shapes=list(scratch),
            compiler_params=pltpu.CompilerParams(vmem_limit_bytes=VMEM_LIMIT),
            cost_estimate=pl.CostEstimate(
                flops=0, bytes_accessed=int(us * COST), transcendentals=0
            ),
        )(*args)
        self.last = result[-1] if many else result
        return result


def swap(x, axis, mask):
    size = lax.axis_size(axis)
    return lax.ppermute(x, axis, [(i, i ^ mask) for i in range(size)])


def split_kernel(place, grad_ref, *outs):
    half = outs[0].shape[3]
    for side, out in enumerate(outs):
        for i, k in enumerate((1 << side, 3)):
            start = (place[0] ^ k) * 2 + side
            columns = pl.ds(pl.multiple_of(start * half, half), half)
            out[i] = grad_ref[0, :, :, columns]


def add_kernel(place, grad_ref, *refs):
    sides = len(refs) // 3
    arrived, sums, sends = refs[:sides], refs[sides : 2 * sides], refs[2 * sides :]
    half = sums[0].shape[2]
    for side in range(sides):
        for i, (k, out) in enumerate(((0, sums[side]), (2 >> side, sends[side]))):
            start = (place[0] ^ k) * 2 + side
            columns = pl.ds(pl.multiple_of(start * half, half), half)
            for m in range(out.shape[0]):
                total = grad_ref[0, m, :, columns].astype(f32) + arrived[side][i, m].astype(f32)
                out[m] = total.astype(out.dtype)


def sample_kernel(place, grad_ref, sketch_ref, keep_ref, send_ref):
    half, each = keep_ref.shape[0], keep_ref.shape[1]
    for k in range(2 * half):
        out = (keep_ref, send_ref)[k % 2]
        for i in range(each):
            m = (place[0] ^ k) * each + i
            product = jnp.dot(grad_ref[0, m], sketch_ref[...], preferred_element_type=f32)
            out[k // 2, i] = product.astype(out.dtype)


def halve_kernel(keep_ref, other_ref, *outs):
    for k in range(keep_ref.shape[0]):
        total = keep_ref[k] + other_ref[k].astype(f32)
        out = outs[k % len(outs)]
        out[k // len(outs)] = total.astype(out.dtype)


def stack_kernel(own_ref, other_ref, out_ref):
    half = own_ref.shape[0]
    out_ref[:half] = own_ref[...]
    out_ref[half:] = other_ref[...]


def gather_kernel(*refs):
    for k, ref in enumerate(refs[:-1]):
        refs[-1][k] = ref[...]


def gram_kernel(*refs):
    out = refs[-1]
    each = out.shape[0]
    for i in range(each):
        total = None
        for ref in refs[:-1]:
            for j in range(i, ref.shape[0], each):
                block = ref[j]
                term = lax.dot_general(
                    block, block, (((0,), (0,)), ((), ())), preferred_element_type=f32
                )
                total = term if total is None else total + term
        out[i] = total


def eliminate(work, j):
    pair, size = work.shape[0], work.shape[1]
    lane = lax.broadcasted_iota(jnp.int32, (BLOCK, 2 * BLOCK), 1)
    sub = lax.broadcasted_iota(jnp.int32, (BLOCK, 2 * BLOCK), 0)
    eye_right = (lane - BLOCK == sub).astype(f32)
    lo = j * BLOCK
    base = lo // 128 * 128
    tiles = []
    for b in range(pair):
        slab = work[b, lo : lo + BLOCK, base : base + 128]
        if lo > base:
            slab = pltpu.roll(slab, 128 - (lo - base), 1)
        tiles.append(jnp.where(lane < BLOCK, slab, eye_right))
    for first in range(0, BLOCK, GROUP):
        for b in range(pair):
            tile = tiles[b]
            columns = [
                jnp.broadcast_to(tile[:, k : k + 1], tile.shape)
                for k in range(first, first + GROUP)
            ]
            rows = []
            for i in range(GROUP):
                k = first + i
                inverse = 1.0 / columns[i][k : k + 1, :]
                row = tile[k : k + 1, :]
                for j in range(i):
                    row = row - columns[j][k : k + 1, :] * rows[j]
                rows.append(row * inverse)
                columns[i] = jnp.where(sub > k, columns[i], 0.0)
                for j in range(i + 1, GROUP):
                    columns[j] = columns[j] - columns[i] * (columns[j][k : k + 1, :] * inverse)
            for i in range(GROUP):
                tile = tile - columns[i] * rows[i]
            tiles[b] = tile
    for b in range(pair):
        tile = tiles[b]
        diagonal = jnp.sum(jnp.where(lane == sub, tile, 0.0), axis=1, keepdims=True)
        inverse = pltpu.roll(tile, BLOCK, 1)[:, :BLOCK] * lax.rsqrt(diagonal)
        solved = jnp.dot(
            inverse, work[b, lo : lo + BLOCK, :], precision=HIGHEST, preferred_element_type=f32
        )
        work[b, lo : lo + BLOCK, size:] = solved[:, size:]
        if lo + BLOCK < size:
            change = lax.dot_general(
                solved[:, :size],
                solved,
                (((0,), (0,)), ((), ())),
                precision=HIGHEST,
                preferred_element_type=f32,
            )
            work[b, lo + BLOCK :, :] = work[b, lo + BLOCK :, :] - change[lo + BLOCK :, :]


def start_kernel(own_ref, other_ref, work):
    pair, size = own_ref.shape[0], own_ref.shape[1]
    row = lax.broadcasted_iota(jnp.int32, (size, size), 0)
    col = lax.broadcasted_iota(jnp.int32, (size, size), 1)
    eye = (row == col).astype(f32)
    for b in range(pair):
        work[b, :, :size] = own_ref[b] + other_ref[b]
        work[b, :, size:] = eye
    eliminate(work, 0)


def middle_kernel(work_in, work, *, j):
    work[...] = work_in[...]
    eliminate(work, j)


def finish_kernel(work_in, rows_ref, out_ref, work, *, j, scale):
    work[...] = work_in[...]
    eliminate(work, j)
    size = work.shape[1]
    for b in range(work.shape[0]):
        basis = lax.dot_general(
            rows_ref[b].astype(f32),
            work[b, :, size:],
            (((1,), (1,)), ((), ())),
            precision=HIGHEST,
            preferred_element_type=f32,
        )
        out_ref[b] = (basis * scale).astype(out_ref.dtype)


def pick_kernel(place, owner, first_ref, second_ref, mine_ref, other_ref):
    here, core = place[1] * 2 + place[2], place[2]
    capacity = first_ref.shape[0]
    seen = jnp.int32(0)
    at = []
    for m in range(owner.shape[0]):
        at.append(jnp.minimum(seen, capacity - 1))
        seen = seen + (owner[m] == here).astype(jnp.int32)
    chips = mine_ref.shape[0]
    for i in range(chips):
        for out, want in ((mine_ref, core), (other_ref, 1 - core)):
            slot = jnp.int32(0)
            m = 2 * (place[1] ^ i) + want
            for j in range(owner.shape[0]):
                slot = jnp.where(m == j, at[j], slot)
            out[i, 0] = first_ref[slot].astype(bf16)
            out[i, 1] = second_ref[slot].astype(bf16)


def merge_kernel(place, owner, mine_ref, other_ref, *outs, bit):
    z, core = place[1], place[2]
    stride = 1 if bit < 0 else 2 << bit
    split = len(outs)
    for i in range(mine_ref.shape[0]):
        source = owner[2 * (z ^ (i * stride)) + core]
        if bit < 0:
            local = (source & 1) == core
        else:
            local = (((source >> 1) ^ z) >> bit) & 1 == 0
        outs[i % split][i // split] = jnp.where(local, mine_ref[i], other_ref[i])


def project_kernel(place, *refs, scale):
    *sums, basis_ref, mine_ref, other_ref = refs
    core = place[2]
    half = sums[0].shape[2]
    for i in range(mine_ref.shape[0]):
        for out, want in ((other_ref, 1 - core), (mine_ref, core)):
            m = 2 * i + want
            scaled = (basis_ref[m] * scale).astype(bf16)
            for side in range(2):
                total = sums[side][m] + sums[2 + side][m].astype(f32)
                product = lax.dot_general(
                    scaled,
                    total.astype(bf16),
                    (((0,), (0,)), ((), ())),
                    preferred_element_type=f32,
                )
                out[i, :, side * half : (side + 1) * half] = product.astype(out.dtype)


def pair_kernel(place, mine_ref, other_ref, *outs):
    for k, out in enumerate(outs):
        i = place[1] ^ k
        out[...] = (mine_ref[i] + other_ref[i].astype(f32)).astype(out.dtype)


def update_kernel(place, owner, rank, *refs, chips, bit, start):
    terms = refs[:chips]
    moment_ref, lent_ref, update_ref, projected_ref = refs[chips:]
    z, core = place[1], place[2]
    m = 2 * z + core
    projected = terms[0][...].astype(f32)
    for ref in terms[1:]:
        projected = projected + ref[...].astype(f32)
    width = projected.shape[1]
    columns = slice(start, start + width)
    local = (((owner[m] >> 1) ^ z) >> bit) & 1 == 0
    first = jnp.where(local, moment_ref[0, 0, :, columns], lent_ref[0, 0, :, columns])
    second = jnp.where(local, moment_ref[0, 1, :, columns], lent_ref[0, 1, :, columns])
    first_new = beta_one * first.astype(f32) + (1.0 - beta_one) * projected
    second_new = beta_two * second.astype(f32) + (1.0 - beta_two) * projected * projected
    update = (first_new / bias_one) / (jnp.sqrt(second_new / bias_two) + epsilon)
    row = lax.broadcasted_iota(jnp.int32, update.shape, 0)
    update_ref[...] = jnp.where(row < rank[m], update, 0.0).astype(bf16)
    projected_ref[...] = projected.astype(bf16)


def delta_kernel(place, *refs, chips, scale):
    near, far, basis_ref, projected_ref, out_ref, passed_ref = refs
    z, core = place[1], place[2]
    passed_ref[...] = projected_ref[...]
    for k in range(chips):
        for ref, want in ((near, core), (far, 1 - core)):
            m = 2 * (z ^ k) + want
            product = jnp.dot(
                (basis_ref[m] * scale).astype(bf16), ref[k], preferred_element_type=f32
            )
            out_ref[m] = product.astype(bf16)


def weight_kernel(place, weight_ref, *refs, groups, chunks):
    out_ref = refs[-1]
    width = refs[0].shape[2]
    for h in range(chunks):
        for k in range(groups):
            start = ((place[0] ^ k) * chunks + h) * width
            columns = pl.ds(pl.multiple_of(start, 128), width)
            for m in range(out_ref.shape[0]):
                delta = refs[h * groups + k][m].astype(f32)
                old = weight_ref[m, :, columns].astype(f32)
                out_ref[m, :, columns] = (old - step_size * delta).astype(bf16)


def basis_kernel(place, *refs):
    out_ref = refs[-1]
    each = refs[0].shape[0]
    for k, ref in enumerate(refs[:-1]):
        for i in range(each):
            out_ref[(place[0] ^ k) * each + i] = ref[i].astype(f32)


def moment_kernel(place, owner, *refs, chunks):
    projected_refs = refs[:chunks]
    first_ref, second_ref, first_out, second_out = refs[chunks:]
    here = place[1] * 2 + place[2]
    capacity, rank_full, _ = first_out.shape
    width = projected_refs[0].shape[2]
    seen = jnp.int32(0)
    index = [jnp.int32(0)] * capacity
    for m in range(owner.shape[0]):
        hit = owner[m] == here
        for s in range(capacity):
            index[s] = jnp.where(hit & (seen == s), m, index[s])
        seen = seen + hit.astype(jnp.int32)
    for s in range(capacity):
        keep = seen > s
        for h in range(chunks):
            columns = slice(h * width, (h + 1) * width)
            projected = projected_refs[h][index[s]].astype(f32)
            first_new = beta_one * first_ref[s, :, columns] + (1.0 - beta_one) * projected
            second_new = (
                beta_two * second_ref[s, :, columns] + (1.0 - beta_two) * projected * projected
            )
            first_out[s, :, columns] = jnp.where(keep, first_new, 0.0)
            second_out[s, :, columns] = jnp.where(keep, second_new, 0.0)


def per_device(grads, weight, basis, first_moment, second_moment, sketch, owner, rank):
    owners = lax.axis_size("rows")
    groups = lax.axis_size("dp")
    here = lax.axis_index("rows")
    group = lax.axis_index("dp")
    capacity, rank_full, quarter = first_moment.shape
    count, shard, width = weight.shape
    chips = owners // 2
    each = count // groups
    total_rows = shard * owners
    root = float(total_rows) ** 0.5
    inverse_root = float(total_rows) ** (-0.5)
    place = jnp.stack([group, here // 2, here % 2]).astype(jnp.int32)
    struct = jax.ShapeDtypeStruct

    call = Sequence()
    halved = struct((2, count, shard, quarter // 2), bf16)
    sides = call(split_kernel, [halved] * 2, (place, grads), scalars=1)
    half = chips
    moments, lent = call(
        pick_kernel,
        [struct((half, 2, rank_full, quarter), bf16)] * 2,
        (place, owner, first_moment, second_moment),
        scalars=2,
    )
    lent = swap(lent, "rows", 1)
    keep, send = call(
        sample_kernel,
        [struct((groups // 2, each, shard, rank_full), kind) for kind in (f32, bf16)],
        (place, grads, sketch),
        scalars=1,
    )
    half //= 2
    moments, lent = call(
        functools.partial(merge_kernel, bit=-1),
        [struct((half, 2, rank_full, quarter), bf16)] * 2,
        (place, owner, moments, lent),
        scalars=2,
    )
    lent = swap(lent, "rows", 2)
    sides = [swap(sides[i], "dp", 1 << i) for i in range(2)]
    send = swap(send, "dp", 1)
    part = groups // 2
    mask = 1
    while part > 1:
        part //= 2
        keep, send = call(
            halve_kernel,
            [struct((part, each, shard, rank_full), kind) for kind in (f32, bf16)],
            (keep, send),
        )
        mask *= 2
        send = swap(send, "dp", mask)
    *sums, left, right = call(
        add_kernel,
        [struct((count, shard, quarter // 2), kind) for kind in (f32, f32, bf16, bf16)],
        (place, grads, *sides),
        scalars=1,
    )
    left, right = swap(left, "dp", 2), swap(right, "dp", 1)
    bit = 0
    while half > 1:
        half //= 2
        moments, lent = call(
            functools.partial(merge_kernel, bit=bit),
            [struct((half, 2, rank_full, quarter), bf16)] * 2,
            (place, owner, moments, lent),
            scalars=2,
        )
        bit += 1
        lent = swap(lent, "rows", 2 << bit)
    sample = call(
        halve_kernel,
        [struct((1, each, shard, rank_full), bf16)],
        (keep, send),
    )[0].reshape(each, shard, rank_full)
    mine, other = call(
        functools.partial(project_kernel, scale=inverse_root),
        [struct((chips, rank_full, quarter), f32), struct((chips, rank_full, quarter), bf16)],
        (place, *sums, left, right, basis),
        scalars=1,
        after=(lent,),
    )
    other = swap(other, "rows", 1)
    mask = chips // 2
    arrived = swap(sample, "rows", 2 * mask)
    terms = call(
        pair_kernel,
        [struct((rank_full, quarter), f32)] + [struct((rank_full, quarter), bf16)] * (chips - 1),
        (place, mine, other),
        scalars=1,
    )
    terms = [terms[0]] + [swap(terms[k], "rows", 2 * k) for k in range(1, chips)]
    stacked = sample
    while mask > 1:
        both = struct((2 * stacked.shape[0], shard, rank_full), bf16)
        stacked = call(stack_kernel, both, (stacked, arrived))
        mask //= 2
        arrived = swap(stacked, "rows", 2 * mask)
    work_shape = struct((each, rank_full, 2 * rank_full), f32)
    last = rank_full // BLOCK - 1
    update, projected = call(
        functools.partial(update_kernel, chips=chips, bit=bit, start=0),
        [struct((rank_full, quarter), bf16)] * 2,
        (place, owner, rank, *terms, moments, lent),
        scalars=3,
    )
    near = [update] + [swap(update, "rows", 2 * k) for k in range(1, chips)]
    gram = call(
        gram_kernel, struct((each, rank_full, rank_full), f32), (stacked, arrived)
    )
    other_gram = swap(gram, "rows", 1)
    work = call(start_kernel, work_shape, (gram, other_gram))
    near = call(gather_kernel, struct((chips, rank_full, quarter), bf16), tuple(near))
    far = swap(near, "rows", 1)
    delta, projected = call(
        functools.partial(delta_kernel, chips=chips, scale=inverse_root),
        [struct((count, shard, quarter), bf16), struct((rank_full, quarter), bf16)],
        (place, near, far, basis, projected),
        scalars=1,
    )
    deltas = [delta] + [swap(delta, "dp", k) for k in range(1, groups)]
    gathered = lax.all_gather(projected, "rows", axis=0)
    for j in range(1, last):
        work = call(functools.partial(middle_kernel, j=j), work_shape, (work,))
    rows_basis = call(
        functools.partial(finish_kernel, j=last, scale=root),
        struct(sample.shape, bf16),
        (work, sample),
        scratch=[pltpu.VMEM(work_shape.shape, f32)],
    )
    shared = [rows_basis] + [swap(rows_basis, "dp", k) for k in range(1, groups)]
    new_weight = call(
        functools.partial(weight_kernel, groups=groups, chunks=1),
        struct(weight.shape, bf16),
        (place, weight, *deltas),
        scalars=1,
    )
    first_out, second_out = call(
        functools.partial(moment_kernel, chunks=1),
        [struct(first_moment.shape, f32)] * 2,
        (place, owner, gathered, first_moment, second_moment),
        scalars=2,
    )
    new_basis = call(basis_kernel, struct(basis.shape, f32), (place, *shared), scalars=1)
    return (new_weight, new_basis, first_out, second_out)


def solution(mesh):
    in_specs = (
        P("dp", None, "rows", None),
        P(None, "rows", None),
        P(None, "rows", None),
        P("rows", None, "dp"),
        P("rows", None, "dp"),
        P(),
        P(),
        P(),
    )
    out_specs = (
        P(None, "rows", None),
        P(None, "rows", None),
        P("rows", None, "dp"),
        P("rows", None, "dp"),
    )
    return jax.shard_map(
        per_device, mesh=mesh, in_specs=in_specs, out_specs=out_specs, check_vma=False
    )
```

```python
import functools

import jax
import jax.numpy as jnp
from jax import lax
from jax.experimental import pallas as pl
from jax.experimental.pallas import tpu as pltpu
from jax.sharding import PartitionSpec as P

beta_one = 0.9
beta_two = 0.95
bias_one = 1.0 - 0.9**10
bias_two = 1.0 - 0.95**10
step_size = 0.5
epsilon = 1e-08
BLOCK = 64
GROUP = 4
COST = 10_000
HIGHEST = lax.Precision.HIGHEST
VMEM_LIMIT = 48 * 1024 * 1024
VMEM = pl.BlockSpec(memory_space=pltpu.VMEM)
SMEM = pl.BlockSpec(memory_space=pltpu.SMEM)
f32 = jnp.float32
bf16 = jnp.bfloat16


class Sequence:
    def __init__(self):
        self.last = None

    def __call__(self, kernel, out_shape, args, scalars=0, us=2.0, scratch=(), after=()):
        many = isinstance(out_shape, (tuple, list))
        specs = [SMEM] * scalars + [VMEM] * (len(args) - scalars)
        body = kernel
        if self.last is not None:
            after = (self.last, *after)
        unread = len(after)
        if unread:
            specs = [pl.BlockSpec(memory_space=pl.ANY)] * unread + specs
            args = (*after, *args)

            def body(*refs):
                kernel(*refs[unread:])

        result = pl.pallas_call(
            body,
            out_shape=out_shape,
            in_specs=specs,
            out_specs=[VMEM] * len(out_shape) if many else VMEM,
            scratch_shapes=list(scratch),
            compiler_params=pltpu.CompilerParams(vmem_limit_bytes=VMEM_LIMIT),
            cost_estimate=pl.CostEstimate(
                flops=0, bytes_accessed=int(us * COST), transcendentals=0
            ),
        )(*args)
        self.last = result[-1] if many else result
        return result


def swap(x, axis, mask):
    size = lax.axis_size(axis)
    return lax.ppermute(x, axis, [(i, i ^ mask) for i in range(size)])


def front_kernel(place, grad_ref, sketch_ref, keep_ref, relay_ref, *outs):
    half = outs[0].shape[3]
    count, each = grad_ref.shape[1], keep_ref.shape[0]
    for side, out in enumerate(outs):
        for i, k in enumerate((1 << side, 3)):
            start = (place[0] ^ k) * 2 + side
            columns = pl.ds(pl.multiple_of(start * half, half), half)
            out[i, :count] = grad_ref[0, :, :, columns]
    for k in range(4):
        for i in range(each):
            m = (place[0] ^ k) * each + i
            part = jnp.dot(grad_ref[0, m], sketch_ref[...], preferred_element_type=f32)
            if k == 0:
                keep_ref[i] = part
                continue
            for side, out in enumerate(outs):
                piece = part[:, side * half : (side + 1) * half]
                if k == 2 >> side:
                    relay_ref[side, i] = piece
                else:
                    out[k // 3, count + i] = piece.astype(bf16)


def add_kernel(place, grad_ref, relay_ref, *refs):
    arrived, sums, sends = refs[:2], refs[2:4], refs[4:]
    count, _, half = sums[0].shape
    for side in range(2):
        for i, (k, out) in enumerate(((0, sums[side]), (2 >> side, sends[side]))):
            start = (place[0] ^ k) * 2 + side
            columns = pl.ds(pl.multiple_of(start * half, half), half)
            for m in range(count):
                total = grad_ref[0, m, :, columns].astype(f32) + arrived[side][i, m].astype(f32)
                out[m] = total.astype(out.dtype)
        for i in range(relay_ref.shape[1]):
            total = relay_ref[side, i] + arrived[side][1, count + i].astype(f32)
            sends[side][count + i] = total.astype(bf16)


def stack_kernel(own_ref, other_ref, out_ref):
    half = own_ref.shape[0]
    out_ref[:half] = own_ref[...]
    out_ref[half:] = other_ref[...]


def gather_kernel(*refs):
    for k, ref in enumerate(refs[:-1]):
        refs[-1][k] = ref[...]


def gram_kernel(*refs):
    out = refs[-1]
    each = out.shape[0]
    for i in range(each):
        total = None
        for ref in refs[:-1]:
            for j in range(i, ref.shape[0], each):
                block = ref[j]
                term = lax.dot_general(
                    block, block, (((0,), (0,)), ((), ())), preferred_element_type=f32
                )
                total = term if total is None else total + term
        out[i] = total


def eliminate(work, j):
    pair, size = work.shape[0], work.shape[1]
    lane = lax.broadcasted_iota(jnp.int32, (BLOCK, 2 * BLOCK), 1)
    sub = lax.broadcasted_iota(jnp.int32, (BLOCK, 2 * BLOCK), 0)
    eye_right = (lane - BLOCK == sub).astype(f32)
    lo = j * BLOCK
    base = lo // 128 * 128
    tiles = []
    for b in range(pair):
        slab = work[b, lo : lo + BLOCK, base : base + 128]
        if lo > base:
            slab = pltpu.roll(slab, 128 - (lo - base), 1)
        tiles.append(jnp.where(lane < BLOCK, slab, eye_right))
    for first in range(0, BLOCK, GROUP):
        for b in range(pair):
            tile = tiles[b]
            columns = [
                jnp.broadcast_to(tile[:, k : k + 1], tile.shape)
                for k in range(first, first + GROUP)
            ]
            rows = []
            for i in range(GROUP):
                k = first + i
                inverse = 1.0 / columns[i][k : k + 1, :]
                row = tile[k : k + 1, :]
                for j in range(i):
                    row = row - columns[j][k : k + 1, :] * rows[j]
                rows.append(row * inverse)
                columns[i] = jnp.where(sub > k, columns[i], 0.0)
                for j in range(i + 1, GROUP):
                    columns[j] = columns[j] - columns[i] * (columns[j][k : k + 1, :] * inverse)
            for i in range(GROUP):
                tile = tile - columns[i] * rows[i]
            tiles[b] = tile
    for b in range(pair):
        tile = tiles[b]
        diagonal = jnp.sum(jnp.where(lane == sub, tile, 0.0), axis=1, keepdims=True)
        inverse = pltpu.roll(tile, BLOCK, 1)[:, :BLOCK] * lax.rsqrt(diagonal)
        solved = jnp.dot(
            inverse, work[b, lo : lo + BLOCK, :], precision=HIGHEST, preferred_element_type=f32
        )
        work[b, lo : lo + BLOCK, size:] = solved[:, size:]
        if lo + BLOCK < size:
            change = lax.dot_general(
                solved[:, :size],
                solved,
                (((0,), (0,)), ((), ())),
                precision=HIGHEST,
                preferred_element_type=f32,
            )
            work[b, lo + BLOCK :, :] = work[b, lo + BLOCK :, :] - change[lo + BLOCK :, :]


def start_kernel(own_ref, other_ref, work):
    pair, size = own_ref.shape[0], own_ref.shape[1]
    row = lax.broadcasted_iota(jnp.int32, (size, size), 0)
    col = lax.broadcasted_iota(jnp.int32, (size, size), 1)
    eye = (row == col).astype(f32)
    for b in range(pair):
        work[b, :, :size] = own_ref[b] + other_ref[b]
        work[b, :, size:] = eye
    eliminate(work, 0)


def middle_kernel(work_in, work, *, j):
    work[...] = work_in[...]
    eliminate(work, j)


def finish_kernel(work_in, rows_ref, out_ref, work, *, j, scale):
    work[...] = work_in[...]
    eliminate(work, j)
    size = work.shape[1]
    for b in range(work.shape[0]):
        basis = lax.dot_general(
            rows_ref[b].astype(f32),
            work[b, :, size:],
            (((1,), (1,)), ((), ())),
            precision=HIGHEST,
            preferred_element_type=f32,
        )
        out_ref[b] = (basis * scale).astype(out_ref.dtype)


def pick_kernel(place, owner, first_ref, second_ref, mine_ref, other_ref):
    here, core = place[1] * 2 + place[2], place[2]
    capacity = first_ref.shape[0]
    seen = jnp.int32(0)
    at = []
    for m in range(owner.shape[0]):
        at.append(jnp.minimum(seen, capacity - 1))
        seen = seen + (owner[m] == here).astype(jnp.int32)
    chips = mine_ref.shape[0]
    for i in range(chips):
        for out, want in ((mine_ref, core), (other_ref, 1 - core)):
            slot = jnp.int32(0)
            m = 2 * (place[1] ^ i) + want
            for j in range(owner.shape[0]):
                slot = jnp.where(m == j, at[j], slot)
            out[i, 0] = first_ref[slot].astype(bf16)
            out[i, 1] = second_ref[slot].astype(bf16)


def merge_kernel(place, owner, mine_ref, other_ref, *outs, bit):
    z, core = place[1], place[2]
    stride = 1 if bit < 0 else 2 << bit
    split = len(outs)
    for i in range(mine_ref.shape[0]):
        source = owner[2 * (z ^ (i * stride)) + core]
        if bit < 0:
            local = (source & 1) == core
        else:
            local = (((source >> 1) ^ z) >> bit) & 1 == 0
        outs[i % split][i // split] = jnp.where(local, mine_ref[i], other_ref[i])


def project_kernel(place, *refs, scale):
    sums, relayed, arrived = refs[:2], refs[2:4], refs[4:6]
    keep_ref, basis_ref, mine_ref, sample_ref, other_ref = refs[6:]
    core = place[2]
    count, _, half = sums[0].shape
    for i in range(mine_ref.shape[0]):
        for out, want in ((other_ref, 1 - core), (mine_ref, core)):
            m = 2 * i + want
            scaled = (basis_ref[m] * scale).astype(bf16)
            for side in range(2):
                total = sums[side][m] + relayed[side][m].astype(f32)
                product = lax.dot_general(
                    scaled,
                    total.astype(bf16),
                    (((0,), (0,)), ((), ())),
                    preferred_element_type=f32,
                )
                out[i, :, side * half : (side + 1) * half] = product.astype(out.dtype)
    for i in range(keep_ref.shape[0]):
        for side in range(2):
            columns = slice(side * half, (side + 1) * half)
            total = keep_ref[i, :, columns] + arrived[side][0, count + i].astype(f32)
            total = total + relayed[side][count + i].astype(f32)
            sample_ref[i, :, columns] = total.astype(bf16)


def pair_kernel(place, mine_ref, other_ref, *outs):
    for k, out in enumerate(outs):
        i = place[1] ^ k
        out[...] = (mine_ref[i] + other_ref[i].astype(f32)).astype(out.dtype)


def update_kernel(place, owner, rank, *refs, chips, bit, start):
    terms = refs[:chips]
    moment_ref, lent_ref, update_ref, projected_ref = refs[chips:]
    z, core = place[1], place[2]
    m = 2 * z + core
    projected = terms[0][...].astype(f32)
    for ref in terms[1:]:
        projected = projected + ref[...].astype(f32)
    width = projected.shape[1]
    columns = slice(start, start + width)
    local = (((owner[m] >> 1) ^ z) >> bit) & 1 == 0
    first = jnp.where(local, moment_ref[0, 0, :, columns], lent_ref[0, 0, :, columns])
    second = jnp.where(local, moment_ref[0, 1, :, columns], lent_ref[0, 1, :, columns])
    first_new = beta_one * first.astype(f32) + (1.0 - beta_one) * projected
    second_new = beta_two * second.astype(f32) + (1.0 - beta_two) * projected * projected
    update = (first_new / bias_one) / (jnp.sqrt(second_new / bias_two) + epsilon)
    row = lax.broadcasted_iota(jnp.int32, update.shape, 0)
    update_ref[...] = jnp.where(row < rank[m], update, 0.0).astype(bf16)
    projected_ref[...] = projected.astype(bf16)


def delta_kernel(place, *refs, chips, scale):
    near, far, basis_ref, projected_ref, out_ref, passed_ref = refs
    z, core = place[1], place[2]
    passed_ref[...] = projected_ref[...]
    for k in range(chips):
        for ref, want in ((near, core), (far, 1 - core)):
            m = 2 * (z ^ k) + want
            product = jnp.dot(
                (basis_ref[m] * scale).astype(bf16), ref[k], preferred_element_type=f32
            )
            out_ref[m] = product.astype(bf16)


def weight_kernel(place, weight_ref, *refs, groups, chunks):
    out_ref = refs[-1]
    width = refs[0].shape[2]
    for h in range(chunks):
        for k in range(groups):
            start = ((place[0] ^ k) * chunks + h) * width
            columns = pl.ds(pl.multiple_of(start, 128), width)
            for m in range(out_ref.shape[0]):
                delta = refs[h * groups + k][m].astype(f32)
                old = weight_ref[m, :, columns].astype(f32)
                out_ref[m, :, columns] = (old - step_size * delta).astype(bf16)


def basis_kernel(place, *refs):
    out_ref = refs[-1]
    each = refs[0].shape[0]
    for k, ref in enumerate(refs[:-1]):
        for i in range(each):
            out_ref[(place[0] ^ k) * each + i] = ref[i].astype(f32)


def moment_kernel(place, owner, *refs, chunks):
    projected_refs = refs[:chunks]
    first_ref, second_ref, first_out, second_out = refs[chunks:]
    here = place[1] * 2 + place[2]
    capacity, rank_full, _ = first_out.shape
    width = projected_refs[0].shape[2]
    seen = jnp.int32(0)
    index = [jnp.int32(0)] * capacity
    for m in range(owner.shape[0]):
        hit = owner[m] == here
        for s in range(capacity):
            index[s] = jnp.where(hit & (seen == s), m, index[s])
        seen = seen + hit.astype(jnp.int32)
    for s in range(capacity):
        keep = seen > s
        for h in range(chunks):
            columns = slice(h * width, (h + 1) * width)
            projected = projected_refs[h][index[s]].astype(f32)
            first_new = beta_one * first_ref[s, :, columns] + (1.0 - beta_one) * projected
            second_new = (
                beta_two * second_ref[s, :, columns] + (1.0 - beta_two) * projected * projected
            )
            first_out[s, :, columns] = jnp.where(keep, first_new, 0.0)
            second_out[s, :, columns] = jnp.where(keep, second_new, 0.0)


def per_device(grads, weight, basis, first_moment, second_moment, sketch, owner, rank):
    owners = lax.axis_size("rows")
    groups = lax.axis_size("dp")
    here = lax.axis_index("rows")
    group = lax.axis_index("dp")
    capacity, rank_full, quarter = first_moment.shape
    count, shard, width = weight.shape
    chips = owners // 2
    each = count // groups
    total_rows = shard * owners
    root = float(total_rows) ** 0.5
    inverse_root = float(total_rows) ** (-0.5)
    place = jnp.stack([group, here // 2, here % 2]).astype(jnp.int32)
    struct = jax.ShapeDtypeStruct

    call = Sequence()
    half = quarter // 2
    keep, relay, *sides = call(
        front_kernel,
        [struct((each, shard, rank_full), f32), struct((2, each, shard, half), f32)]
        + [struct((2, count + each, shard, half), bf16)] * 2,
        (place, grads, sketch),
        scalars=1,
    )
    sides = [swap(sides[i], "dp", 1 << i) for i in range(2)]
    left = chips
    moments, lent = call(
        pick_kernel,
        [struct((left, 2, rank_full, quarter), bf16)] * 2,
        (place, owner, first_moment, second_moment),
        scalars=2,
    )
    lent = swap(lent, "rows", 1)
    bit = -1
    while left > 1:
        left //= 2
        moments, lent = call(
            functools.partial(merge_kernel, bit=bit),
            [struct((left, 2, rank_full, quarter), bf16)] * 2,
            (place, owner, moments, lent),
            scalars=2,
        )
        bit += 1
        lent = swap(lent, "rows", 2 << bit)
    *sums, first_send, second_send = call(
        add_kernel,
        [struct((count, shard, half), f32)] * 2
        + [struct((count + each, shard, half), bf16)] * 2,
        (place, grads, relay, *sides),
        scalars=1,
    )
    relayed = [swap(first_send, "dp", 2), swap(second_send, "dp", 1)]
    mine, sample, other = call(
        functools.partial(project_kernel, scale=inverse_root),
        [
            struct((chips, rank_full, quarter), f32),
            struct((each, shard, rank_full), bf16),
            struct((chips, rank_full, quarter), bf16),
        ],
        (place, *sums, *relayed, *sides, keep, basis),
        scalars=1,
        after=(lent,),
    )
    other = swap(other, "rows", 1)
    mask = chips // 2
    arrived = swap(sample, "rows", 2 * mask)
    terms = call(
        pair_kernel,
        [struct((rank_full, quarter), f32)] + [struct((rank_full, quarter), bf16)] * (chips - 1),
        (place, mine, other),
        scalars=1,
    )
    terms = [terms[0]] + [swap(terms[k], "rows", 2 * k) for k in range(1, chips)]
    work_shape = struct((each, rank_full, 2 * rank_full), f32)
    last = rank_full // BLOCK - 1
    update, projected = call(
        functools.partial(update_kernel, chips=chips, bit=bit, start=0),
        [struct((rank_full, quarter), bf16)] * 2,
        (place, owner, rank, *terms, moments, lent),
        scalars=3,
    )
    near = [update] + [swap(update, "rows", 2 * k) for k in range(1, chips)]
    stacked = sample
    while mask > 1:
        both = struct((2 * stacked.shape[0], shard, rank_full), bf16)
        stacked = call(stack_kernel, both, (stacked, arrived))
        mask //= 2
        arrived = swap(stacked, "rows", 2 * mask)
    near = call(
        gather_kernel,
        struct((chips, rank_full, quarter), bf16),
        tuple(near),
        after=(arrived,),
    )
    far = swap(near, "rows", 1)
    gram = call(
        gram_kernel, struct((each, rank_full, rank_full), f32), (stacked, arrived)
    )
    other_gram = swap(gram, "rows", 1)
    delta, projected = call(
        functools.partial(delta_kernel, chips=chips, scale=inverse_root),
        [struct((count, shard, quarter), bf16), struct((rank_full, quarter), bf16)],
        (place, near, far, basis, projected),
        scalars=1,
        after=(other_gram,),
    )
    deltas = [delta] + [swap(delta, "dp", k) for k in range(1, groups)]
    gathered = lax.all_gather(projected, "rows", axis=0)
    work = call(start_kernel, work_shape, (gram, other_gram))
    for j in range(1, last):
        work = call(functools.partial(middle_kernel, j=j), work_shape, (work,))
    rows_basis = call(
        functools.partial(finish_kernel, j=last, scale=root),
        struct(sample.shape, bf16),
        (work, sample),
        scratch=[pltpu.VMEM(work_shape.shape, f32)],
    )
    shared = [rows_basis] + [swap(rows_basis, "dp", k) for k in range(1, groups)]
    first_out, second_out = call(
        functools.partial(moment_kernel, chunks=1),
        [struct(first_moment.shape, f32)] * 2,
        (place, owner, gathered, first_moment, second_moment),
        scalars=2,
    )
    new_weight = call(
        functools.partial(weight_kernel, groups=groups, chunks=1),
        struct(weight.shape, bf16),
        (place, weight, *deltas),
        scalars=1,
    )
    new_basis = call(basis_kernel, struct(basis.shape, f32), (place, *shared), scalars=1)
    return (new_weight, new_basis, first_out, second_out)


def solution(mesh):
    in_specs = (
        P("dp", None, "rows", None),
        P(None, "rows", None),
        P(None, "rows", None),
        P("rows", None, "dp"),
        P("rows", None, "dp"),
        P(),
        P(),
        P(),
    )
    out_specs = (
        P(None, "rows", None),
        P(None, "rows", None),
        P("rows", None, "dp"),
        P("rows", None, "dp"),
    )
    return jax.shard_map(
        per_device, mesh=mesh, in_specs=in_specs, out_specs=out_specs, check_vma=False
    )
```

```python
import functools

import jax
import jax.numpy as jnp
from jax import lax
from jax.experimental import pallas as pl
from jax.experimental.pallas import tpu as pltpu
from jax.sharding import PartitionSpec as P

beta_one = 0.9
beta_two = 0.95
bias_one = 1.0 - 0.9**10
bias_two = 1.0 - 0.95**10
step_size = 0.5
epsilon = 1e-08
BLOCK = 64
GROUP = 4
COST = 10_000
HIGHEST = lax.Precision.HIGHEST
VMEM_LIMIT = 48 * 1024 * 1024
VMEM = pl.BlockSpec(memory_space=pltpu.VMEM)
SMEM = pl.BlockSpec(memory_space=pltpu.SMEM)
f32 = jnp.float32
bf16 = jnp.bfloat16


class Sequence:
    def __init__(self):
        self.last = None

    def __call__(self, kernel, out_shape, args, scalars=0, us=2.0, scratch=(), after=()):
        many = isinstance(out_shape, (tuple, list))
        specs = [SMEM] * scalars + [VMEM] * (len(args) - scalars)
        body = kernel
        if self.last is not None:
            after = (self.last, *after)
        unread = len(after)
        if unread:
            specs = [pl.BlockSpec(memory_space=pl.ANY)] * unread + specs
            args = (*after, *args)

            def body(*refs):
                kernel(*refs[unread:])

        result = pl.pallas_call(
            body,
            out_shape=out_shape,
            in_specs=specs,
            out_specs=[VMEM] * len(out_shape) if many else VMEM,
            scratch_shapes=list(scratch),
            compiler_params=pltpu.CompilerParams(vmem_limit_bytes=VMEM_LIMIT),
            cost_estimate=pl.CostEstimate(
                flops=0, bytes_accessed=int(us * COST), transcendentals=0
            ),
        )(*args)
        self.last = result[-1] if many else result
        return result


def swap(x, axis, mask):
    size = lax.axis_size(axis)
    return lax.ppermute(x, axis, [(i, i ^ mask) for i in range(size)])


def front_kernel(place, grad_ref, sketch_ref, keep_ref, relay_ref, *outs):
    half = outs[0].shape[3]
    count, each = grad_ref.shape[1], keep_ref.shape[0]
    for side, out in enumerate(outs):
        for i, k in enumerate((1 << side, 3)):
            start = (place[0] ^ k) * 2 + side
            columns = pl.ds(pl.multiple_of(start * half, half), half)
            out[i, :count] = grad_ref[0, :, :, columns]
    for k in range(4):
        for i in range(each):
            m = (place[0] ^ k) * each + i
            part = jnp.dot(grad_ref[0, m], sketch_ref[...], preferred_element_type=f32)
            if k == 0:
                keep_ref[i] = part
                continue
            for side, out in enumerate(outs):
                piece = part[:, side * half : (side + 1) * half]
                if k == 2 >> side:
                    relay_ref[side, i] = piece
                else:
                    out[k // 3, count + i] = piece.astype(bf16)


def add_kernel(place, grad_ref, relay_ref, *refs):
    arrived, sums, sends = refs[:2], refs[2:4], refs[4:]
    count, _, half = sums[0].shape
    for side in range(2):
        for i, (k, out) in enumerate(((0, sums[side]), (2 >> side, sends[side]))):
            start = (place[0] ^ k) * 2 + side
            columns = pl.ds(pl.multiple_of(start * half, half), half)
            for m in range(count):
                total = grad_ref[0, m, :, columns].astype(f32) + arrived[side][i, m].astype(f32)
                out[m] = total.astype(out.dtype)
        for i in range(relay_ref.shape[1]):
            total = relay_ref[side, i] + arrived[side][1, count + i].astype(f32)
            sends[side][count + i] = total.astype(bf16)


def stack_kernel(own_ref, other_ref, out_ref):
    half = own_ref.shape[0]
    out_ref[:half] = own_ref[...]
    out_ref[half:] = other_ref[...]


def gather_kernel(*refs):
    for k, ref in enumerate(refs[:-1]):
        refs[-1][k] = ref[...]


def gram_kernel(*refs):
    out = refs[-1]
    each = out.shape[0]
    for i in range(each):
        total = None
        for ref in refs[:-1]:
            for j in range(i, ref.shape[0], each):
                block = ref[j]
                term = lax.dot_general(
                    block, block, (((0,), (0,)), ((), ())), preferred_element_type=f32
                )
                total = term if total is None else total + term
        out[i] = total


def eliminate(work, j):
    pair, size = work.shape[0], work.shape[1]
    lane = lax.broadcasted_iota(jnp.int32, (BLOCK, 2 * BLOCK), 1)
    sub = lax.broadcasted_iota(jnp.int32, (BLOCK, 2 * BLOCK), 0)
    eye_right = (lane - BLOCK == sub).astype(f32)
    lo = j * BLOCK
    base = lo // 128 * 128
    tiles = []
    for b in range(pair):
        slab = work[b, lo : lo + BLOCK, base : base + 128]
        if lo > base:
            slab = pltpu.roll(slab, 128 - (lo - base), 1)
        tiles.append(jnp.where(lane < BLOCK, slab, eye_right))
    for first in range(0, BLOCK, GROUP):
        for b in range(pair):
            tile = tiles[b]
            columns = [
                jnp.broadcast_to(tile[:, k : k + 1], tile.shape)
                for k in range(first, first + GROUP)
            ]
            rows = []
            for i in range(GROUP):
                k = first + i
                inverse = 1.0 / columns[i][k : k + 1, :]
                row = tile[k : k + 1, :]
                for j in range(i):
                    row = row - columns[j][k : k + 1, :] * rows[j]
                rows.append(row * inverse)
                columns[i] = jnp.where(sub > k, columns[i], 0.0)
                for j in range(i + 1, GROUP):
                    columns[j] = columns[j] - columns[i] * (columns[j][k : k + 1, :] * inverse)
            for i in range(GROUP):
                tile = tile - columns[i] * rows[i]
            tiles[b] = tile
    for b in range(pair):
        tile = tiles[b]
        diagonal = jnp.sum(jnp.where(lane == sub, tile, 0.0), axis=1, keepdims=True)
        inverse = pltpu.roll(tile, BLOCK, 1)[:, :BLOCK] * lax.rsqrt(diagonal)
        solved = jnp.dot(
            inverse, work[b, lo : lo + BLOCK, :], precision=HIGHEST, preferred_element_type=f32
        )
        work[b, lo : lo + BLOCK, size:] = solved[:, size:]
        if lo + BLOCK < size:
            change = lax.dot_general(
                solved[:, :size],
                solved,
                (((0,), (0,)), ((), ())),
                precision=HIGHEST,
                preferred_element_type=f32,
            )
            work[b, lo + BLOCK :, :] = work[b, lo + BLOCK :, :] - change[lo + BLOCK :, :]


def start_kernel(own_ref, other_ref, work):
    pair, size = own_ref.shape[0], own_ref.shape[1]
    row = lax.broadcasted_iota(jnp.int32, (size, size), 0)
    col = lax.broadcasted_iota(jnp.int32, (size, size), 1)
    eye = (row == col).astype(f32)
    for b in range(pair):
        work[b, :, :size] = own_ref[b] + other_ref[b]
        work[b, :, size:] = eye
    eliminate(work, 0)


def middle_kernel(work_in, work, *, j):
    work[...] = work_in[...]
    eliminate(work, j)


def finish_kernel(work_in, rows_ref, out_ref, work, *, j, scale):
    work[...] = work_in[...]
    eliminate(work, j)
    size = work.shape[1]
    for b in range(work.shape[0]):
        basis = lax.dot_general(
            rows_ref[b].astype(f32),
            work[b, :, size:],
            (((1,), (1,)), ((), ())),
            precision=HIGHEST,
            preferred_element_type=f32,
        )
        out_ref[b] = (basis * scale).astype(out_ref.dtype)


def pick_kernel(place, owner, first_ref, second_ref, mine_ref, other_ref):
    here, core = place[1] * 2 + place[2], place[2]
    capacity = first_ref.shape[0]
    seen = jnp.int32(0)
    at = []
    for m in range(owner.shape[0]):
        at.append(jnp.minimum(seen, capacity - 1))
        seen = seen + (owner[m] == here).astype(jnp.int32)
    chips = mine_ref.shape[0]
    for i in range(chips):
        for out, want in ((mine_ref, core), (other_ref, 1 - core)):
            slot = jnp.int32(0)
            m = 2 * (place[1] ^ i) + want
            for j in range(owner.shape[0]):
                slot = jnp.where(m == j, at[j], slot)
            out[i, 0] = first_ref[slot].astype(bf16)
            out[i, 1] = second_ref[slot].astype(bf16)


def near_half(place, owner, rel, bit):
    z, core = place[1], place[2]
    source = owner[2 * (z ^ rel) + core]
    if bit < 0:
        return (source & 1) == core
    return (((source >> 1) ^ z) >> bit) & 1 == 0


def divide(rels, bit):
    keep = [i for i, rel in enumerate(rels) if not rel >> bit & 1]
    send = [rels.index(rels[i] ^ (1 << bit)) for i in keep]
    return keep, send


def merge_kernel(place, owner, *refs, rels, bits, cuts):
    inputs, outs = refs[:-4], refs[-4:]
    for t in range(2):
        for where, out in zip(divide(rels[t], cuts[t]), outs[2 * t : 2 * t + 2]):
            for j, i in enumerate(where):
                local = near_half(place, owner, rels[t][i], bits[t])
                if len(inputs) == 2:
                    own, lent = inputs[0][i, t], inputs[1][i, t]
                else:
                    own, lent = inputs[2 * t][i], inputs[2 * t + 1][i]
                out[j] = jnp.where(local, own, lent)


def project_kernel(place, *refs, scale):
    sums, relayed, arrived = refs[:2], refs[2:4], refs[4:6]
    keep_ref, basis_ref, mine_ref, sample_ref, other_ref = refs[6:]
    core = place[2]
    count, _, half = sums[0].shape
    for i in range(mine_ref.shape[0]):
        for out, want in ((other_ref, 1 - core), (mine_ref, core)):
            m = 2 * i + want
            scaled = (basis_ref[m] * scale).astype(bf16)
            for side in range(2):
                total = sums[side][m] + relayed[side][m].astype(f32)
                product = lax.dot_general(
                    scaled,
                    total.astype(bf16),
                    (((0,), (0,)), ((), ())),
                    preferred_element_type=f32,
                )
                out[i, :, side * half : (side + 1) * half] = product.astype(out.dtype)
    for i in range(keep_ref.shape[0]):
        for side in range(2):
            columns = slice(side * half, (side + 1) * half)
            total = keep_ref[i, :, columns] + arrived[side][0, count + i].astype(f32)
            total = total + relayed[side][count + i].astype(f32)
            sample_ref[i, :, columns] = total.astype(bf16)


def pair_kernel(place, mine_ref, other_ref, *outs):
    for k, out in enumerate(outs):
        i = place[1] ^ k
        out[...] = (mine_ref[i] + other_ref[i].astype(f32)).astype(out.dtype)


def update_kernel(place, owner, rank, *refs, chips, bits, start):
    terms = refs[:chips]
    first_ref, first_lent, second_ref, second_lent, update_ref, projected_ref = refs[chips:]
    z, core = place[1], place[2]
    m = 2 * z + core
    projected = terms[0][...].astype(f32)
    for ref in terms[1:]:
        projected = projected + ref[...].astype(f32)
    width = projected.shape[1]
    columns = slice(start, start + width)
    near = near_half(place, owner, 0, bits[0])
    first = jnp.where(near, first_ref[0, :, columns], first_lent[0, :, columns])
    near = near_half(place, owner, 0, bits[1])
    second = jnp.where(near, second_ref[0, :, columns], second_lent[0, :, columns])
    first_new = beta_one * first.astype(f32) + (1.0 - beta_one) * projected
    second_new = beta_two * second.astype(f32) + (1.0 - beta_two) * projected * projected
    update = (first_new / bias_one) / (jnp.sqrt(second_new / bias_two) + epsilon)
    row = lax.broadcasted_iota(jnp.int32, update.shape, 0)
    update_ref[...] = jnp.where(row < rank[m], update, 0.0).astype(bf16)
    projected_ref[...] = projected.astype(bf16)


def delta_kernel(place, *refs, chips, scale):
    near, far, basis_ref, projected_ref, out_ref, passed_ref = refs
    z, core = place[1], place[2]
    passed_ref[...] = projected_ref[...]
    for k in range(chips):
        for ref, want in ((near, core), (far, 1 - core)):
            m = 2 * (z ^ k) + want
            product = jnp.dot(
                (basis_ref[m] * scale).astype(bf16), ref[k], preferred_element_type=f32
            )
            out_ref[m] = product.astype(bf16)


def weight_kernel(place, weight_ref, *refs, groups, chunks):
    out_ref = refs[-1]
    width = refs[0].shape[2]
    for h in range(chunks):
        for k in range(groups):
            start = ((place[0] ^ k) * chunks + h) * width
            columns = pl.ds(pl.multiple_of(start, 128), width)
            for m in range(out_ref.shape[0]):
                delta = refs[h * groups + k][m].astype(f32)
                old = weight_ref[m, :, columns].astype(f32)
                out_ref[m, :, columns] = (old - step_size * delta).astype(bf16)


def basis_kernel(place, *refs):
    out_ref = refs[-1]
    each = refs[0].shape[0]
    for k, ref in enumerate(refs[:-1]):
        for i in range(each):
            out_ref[(place[0] ^ k) * each + i] = ref[i].astype(f32)


def moment_kernel(place, owner, *refs, chunks):
    projected_refs = refs[:chunks]
    first_ref, second_ref, first_out, second_out = refs[chunks:]
    here = place[1] * 2 + place[2]
    capacity, rank_full, _ = first_out.shape
    width = projected_refs[0].shape[2]
    seen = jnp.int32(0)
    index = [jnp.int32(0)] * capacity
    for m in range(owner.shape[0]):
        hit = owner[m] == here
        for s in range(capacity):
            index[s] = jnp.where(hit & (seen == s), m, index[s])
        seen = seen + hit.astype(jnp.int32)
    for s in range(capacity):
        keep = seen > s
        for h in range(chunks):
            columns = slice(h * width, (h + 1) * width)
            projected = projected_refs[h][index[s]].astype(f32)
            first_new = beta_one * first_ref[s, :, columns] + (1.0 - beta_one) * projected
            second_new = (
                beta_two * second_ref[s, :, columns] + (1.0 - beta_two) * projected * projected
            )
            first_out[s, :, columns] = jnp.where(keep, first_new, 0.0)
            second_out[s, :, columns] = jnp.where(keep, second_new, 0.0)


def per_device(grads, weight, basis, first_moment, second_moment, sketch, owner, rank):
    owners = lax.axis_size("rows")
    groups = lax.axis_size("dp")
    here = lax.axis_index("rows")
    group = lax.axis_index("dp")
    capacity, rank_full, quarter = first_moment.shape
    count, shard, width = weight.shape
    chips = owners // 2
    each = count // groups
    total_rows = shard * owners
    root = float(total_rows) ** 0.5
    inverse_root = float(total_rows) ** (-0.5)
    place = jnp.stack([group, here // 2, here % 2]).astype(jnp.int32)
    struct = jax.ShapeDtypeStruct

    call = Sequence()
    half = quarter // 2
    keep, relay, *sides = call(
        front_kernel,
        [struct((each, shard, rank_full), f32), struct((2, each, shard, half), f32)]
        + [struct((2, count + each, shard, half), bf16)] * 2,
        (place, grads, sketch),
        scalars=1,
    )
    sides = [swap(sides[i], "dp", 1 << i) for i in range(2)]
    picked, lent = call(
        pick_kernel,
        [struct((chips, 2, rank_full, quarter), bf16)] * 2,
        (place, owner, first_moment, second_moment),
        scalars=2,
    )
    inputs = [picked, swap(lent, "rows", 1)]
    rels = [list(range(chips)), list(range(chips))]
    bits = (-1, -1)
    levels = chips.bit_length() - 1
    for level in range(levels):
        cuts = (level, levels - 1 - level)
        merged = call(
            functools.partial(merge_kernel, rels=rels, bits=bits, cuts=cuts),
            [struct((len(rels[0]) // 2, rank_full, quarter), bf16)] * 4,
            (place, owner, *inputs),
            scalars=2,
        )
        rels = [[rels[t][i] for i in divide(rels[t], cuts[t])[0]] for t in range(2)]
        bits = cuts
        inputs = []
        for t in range(2):
            inputs += [merged[2 * t], swap(merged[2 * t + 1], "rows", 2 << cuts[t])]
    *sums, first_send, second_send = call(
        add_kernel,
        [struct((count, shard, half), f32)] * 2
        + [struct((count + each, shard, half), bf16)] * 2,
        (place, grads, relay, *sides),
        scalars=1,
    )
    relayed = [swap(first_send, "dp", 2), swap(second_send, "dp", 1)]
    mine, sample, other = call(
        functools.partial(project_kernel, scale=inverse_root),
        [
            struct((chips, rank_full, quarter), f32),
            struct((each, shard, rank_full), bf16),
            struct((chips, rank_full, quarter), bf16),
        ],
        (place, *sums, *relayed, *sides, keep, basis),
        scalars=1,
        after=(inputs[1], inputs[3]),
    )
    other = swap(other, "rows", 1)
    mask = chips // 2
    arrived = swap(sample, "rows", 2 * mask)
    terms = call(
        pair_kernel,
        [struct((rank_full, quarter), f32)] + [struct((rank_full, quarter), bf16)] * (chips - 1),
        (place, mine, other),
        scalars=1,
    )
    terms = [terms[0]] + [swap(terms[k], "rows", 2 * k) for k in range(1, chips)]
    work_shape = struct((each, rank_full, 2 * rank_full), f32)
    last = rank_full // BLOCK - 1
    update, projected = call(
        functools.partial(update_kernel, chips=chips, bits=bits, start=0),
        [struct((rank_full, quarter), bf16)] * 2,
        (place, owner, rank, *terms, *inputs),
        scalars=3,
    )
    near = [update] + [swap(update, "rows", 2 * k) for k in range(1, chips)]
    stacked = sample
    while mask > 1:
        both = struct((2 * stacked.shape[0], shard, rank_full), bf16)
        stacked = call(stack_kernel, both, (stacked, arrived))
        mask //= 2
        arrived = swap(stacked, "rows", 2 * mask)
    near = call(
        gather_kernel,
        struct((chips, rank_full, quarter), bf16),
        tuple(near),
        after=(arrived,),
    )
    far = swap(near, "rows", 1)
    gram = call(
        gram_kernel, struct((each, rank_full, rank_full), f32), (stacked, arrived)
    )
    other_gram = swap(gram, "rows", 1)
    delta, projected = call(
        functools.partial(delta_kernel, chips=chips, scale=inverse_root),
        [struct((count, shard, quarter), bf16), struct((rank_full, quarter), bf16)],
        (place, near, far, basis, projected),
        scalars=1,
        after=(other_gram,),
    )
    deltas = [delta] + [swap(delta, "dp", k) for k in range(1, groups)]
    gathered = lax.all_gather(projected, "rows", axis=0)
    work = call(start_kernel, work_shape, (gram, other_gram))
    for j in range(1, last):
        work = call(functools.partial(middle_kernel, j=j), work_shape, (work,))
    rows_basis = call(
        functools.partial(finish_kernel, j=last, scale=root),
        struct(sample.shape, bf16),
        (work, sample),
        scratch=[pltpu.VMEM(work_shape.shape, f32)],
    )
    shared = [rows_basis] + [swap(rows_basis, "dp", k) for k in range(1, groups)]
    first_out, second_out = call(
        functools.partial(moment_kernel, chunks=1),
        [struct(first_moment.shape, f32)] * 2,
        (place, owner, gathered, first_moment, second_moment),
        scalars=2,
    )
    new_weight = call(
        functools.partial(weight_kernel, groups=groups, chunks=1),
        struct(weight.shape, bf16),
        (place, weight, *deltas),
        scalars=1,
    )
    new_basis = call(basis_kernel, struct(basis.shape, f32), (place, *shared), scalars=1)
    return (new_weight, new_basis, first_out, second_out)


def solution(mesh):
    in_specs = (
        P("dp", None, "rows", None),
        P(None, "rows", None),
        P(None, "rows", None),
        P("rows", None, "dp"),
        P("rows", None, "dp"),
        P(),
        P(),
        P(),
    )
    out_specs = (
        P(None, "rows", None),
        P(None, "rows", None),
        P("rows", None, "dp"),
        P("rows", None, "dp"),
    )
    return jax.shard_map(
        per_device, mesh=mesh, in_specs=in_specs, out_specs=out_specs, check_vma=False
    )
```

```python
import functools

import jax
import jax.numpy as jnp
from jax import lax
from jax.experimental import pallas as pl
from jax.experimental.pallas import tpu as pltpu
from jax.sharding import PartitionSpec as P

beta_one = 0.9
beta_two = 0.95
bias_one = 1.0 - 0.9**10
bias_two = 1.0 - 0.95**10
step_size = 0.5
epsilon = 1e-08
BLOCK = 64
GROUP = 4
COST = 10_000
HIGHEST = lax.Precision.HIGHEST
VMEM_LIMIT = 48 * 1024 * 1024
VMEM = pl.BlockSpec(memory_space=pltpu.VMEM)
SMEM = pl.BlockSpec(memory_space=pltpu.SMEM)
f32 = jnp.float32
bf16 = jnp.bfloat16


class Sequence:
    def __init__(self):
        self.last = None

    def __call__(self, kernel, out_shape, args, scalars=0, us=2.0, scratch=(), after=()):
        many = isinstance(out_shape, (tuple, list))
        specs = [SMEM] * scalars + [VMEM] * (len(args) - scalars)
        body = kernel
        if self.last is not None:
            after = (self.last, *after)
        unread = len(after)
        if unread:
            specs = [pl.BlockSpec(memory_space=pl.ANY)] * unread + specs
            args = (*after, *args)

            def body(*refs):
                kernel(*refs[unread:])

        result = pl.pallas_call(
            body,
            out_shape=out_shape,
            in_specs=specs,
            out_specs=[VMEM] * len(out_shape) if many else VMEM,
            scratch_shapes=list(scratch),
            compiler_params=pltpu.CompilerParams(vmem_limit_bytes=VMEM_LIMIT),
            cost_estimate=pl.CostEstimate(
                flops=0, bytes_accessed=int(us * COST), transcendentals=0
            ),
        )(*args)
        self.last = result[-1] if many else result
        return result


def swap(x, axis, mask):
    size = lax.axis_size(axis)
    return lax.ppermute(x, axis, [(i, i ^ mask) for i in range(size)])


def front_kernel(place, grad_ref, sketch_ref, keep_ref, relay_ref, *outs):
    half = outs[0].shape[3]
    count, each = grad_ref.shape[1], keep_ref.shape[0]
    for side, out in enumerate(outs):
        for i, k in enumerate((1 << side, 3)):
            start = (place[0] ^ k) * 2 + side
            columns = pl.ds(pl.multiple_of(start * half, half), half)
            out[i, :count] = grad_ref[0, :, :, columns]
    for k in range(4):
        for i in range(each):
            m = (place[0] ^ k) * each + i
            part = jnp.dot(grad_ref[0, m], sketch_ref[...], preferred_element_type=f32)
            if k == 0:
                keep_ref[i] = part
                continue
            for side, out in enumerate(outs):
                piece = part[:, side * half : (side + 1) * half]
                if k == 2 >> side:
                    relay_ref[side, i] = piece
                else:
                    out[k // 3, count + i] = piece.astype(bf16)


def add_kernel(place, grad_ref, relay_ref, *refs):
    arrived, sums, sends = refs[:2], refs[2:4], refs[4:]
    count, _, half = sums[0].shape
    for side in range(2):
        for i, (k, out) in enumerate(((0, sums[side]), (2 >> side, sends[side]))):
            start = (place[0] ^ k) * 2 + side
            columns = pl.ds(pl.multiple_of(start * half, half), half)
            for m in range(count):
                total = grad_ref[0, m, :, columns].astype(f32) + arrived[side][i, m].astype(f32)
                out[m] = total.astype(out.dtype)
        for i in range(relay_ref.shape[1]):
            total = relay_ref[side, i] + arrived[side][1, count + i].astype(f32)
            sends[side][count + i] = total.astype(bf16)


def stack_kernel(own_ref, other_ref, out_ref):
    half = own_ref.shape[0]
    out_ref[:half] = own_ref[...]
    out_ref[half:] = other_ref[...]


def gather_kernel(*refs):
    for k, ref in enumerate(refs[:-1]):
        refs[-1][k] = ref[...]


def pass_kernel(*refs):
    half = len(refs) // 2
    for ref, out in zip(refs[:half], refs[half:]):
        out[...] = ref[...]


def gram_kernel(*refs):
    out = refs[-1]
    each = out.shape[0]
    for i in range(each):
        total = None
        for ref in refs[:-1]:
            for j in range(i, ref.shape[0], each):
                block = ref[j]
                term = lax.dot_general(
                    block, block, (((0,), (0,)), ((), ())), preferred_element_type=f32
                )
                total = term if total is None else total + term
        out[i] = total


def eliminate(work, j):
    pair, size = work.shape[0], work.shape[1]
    lane = lax.broadcasted_iota(jnp.int32, (BLOCK, 2 * BLOCK), 1)
    sub = lax.broadcasted_iota(jnp.int32, (BLOCK, 2 * BLOCK), 0)
    eye_right = (lane - BLOCK == sub).astype(f32)
    lo = j * BLOCK
    base = lo // 128 * 128
    tiles = []
    for b in range(pair):
        slab = work[b, lo : lo + BLOCK, base : base + 128]
        if lo > base:
            slab = pltpu.roll(slab, 128 - (lo - base), 1)
        tiles.append(jnp.where(lane < BLOCK, slab, eye_right))
    for first in range(0, BLOCK, GROUP):
        for b in range(pair):
            tile = tiles[b]
            columns = [
                jnp.broadcast_to(tile[:, k : k + 1], tile.shape)
                for k in range(first, first + GROUP)
            ]
            rows = []
            for i in range(GROUP):
                k = first + i
                inverse = 1.0 / columns[i][k : k + 1, :]
                row = tile[k : k + 1, :]
                for j in range(i):
                    row = row - columns[j][k : k + 1, :] * rows[j]
                rows.append(row * inverse)
                columns[i] = jnp.where(sub > k, columns[i], 0.0)
                for j in range(i + 1, GROUP):
                    columns[j] = columns[j] - columns[i] * (columns[j][k : k + 1, :] * inverse)
            for i in range(GROUP):
                tile = tile - columns[i] * rows[i]
            tiles[b] = tile
    for b in range(pair):
        tile = tiles[b]
        diagonal = jnp.sum(jnp.where(lane == sub, tile, 0.0), axis=1, keepdims=True)
        inverse = pltpu.roll(tile, BLOCK, 1)[:, :BLOCK] * lax.rsqrt(diagonal)
        solved = jnp.dot(
            inverse, work[b, lo : lo + BLOCK, :], precision=HIGHEST, preferred_element_type=f32
        )
        work[b, lo : lo + BLOCK, size:] = solved[:, size:]
        if lo + BLOCK < size:
            change = lax.dot_general(
                solved[:, :size],
                solved,
                (((0,), (0,)), ((), ())),
                precision=HIGHEST,
                preferred_element_type=f32,
            )
            work[b, lo + BLOCK :, :] = work[b, lo + BLOCK :, :] - change[lo + BLOCK :, :]


def start_kernel(own_ref, other_ref, work):
    pair, size = own_ref.shape[0], own_ref.shape[1]
    row = lax.broadcasted_iota(jnp.int32, (size, size), 0)
    col = lax.broadcasted_iota(jnp.int32, (size, size), 1)
    eye = (row == col).astype(f32)
    for b in range(pair):
        work[b, :, :size] = own_ref[b] + other_ref[b]
        work[b, :, size:] = eye
    eliminate(work, 0)


def middle_kernel(work_in, work, *, j):
    work[...] = work_in[...]
    eliminate(work, j)


def finish_kernel(work_in, rows_ref, out_ref, work, *, j, scale):
    work[...] = work_in[...]
    eliminate(work, j)
    size = work.shape[1]
    for b in range(work.shape[0]):
        basis = lax.dot_general(
            rows_ref[b].astype(f32),
            work[b, :, size:],
            (((1,), (1,)), ((), ())),
            precision=HIGHEST,
            preferred_element_type=f32,
        )
        out_ref[b] = (basis * scale).astype(out_ref.dtype)


def pick_kernel(place, owner, first_ref, second_ref, mine_ref, other_ref):
    here, core = place[1] * 2 + place[2], place[2]
    capacity = first_ref.shape[0]
    seen = jnp.int32(0)
    at = []
    for m in range(owner.shape[0]):
        at.append(jnp.minimum(seen, capacity - 1))
        seen = seen + (owner[m] == here).astype(jnp.int32)
    chips = mine_ref.shape[0]
    for i in range(chips):
        for out, want in ((mine_ref, core), (other_ref, 1 - core)):
            slot = jnp.int32(0)
            m = 2 * (place[1] ^ i) + want
            for j in range(owner.shape[0]):
                slot = jnp.where(m == j, at[j], slot)
            out[i, 0] = first_ref[slot].astype(bf16)
            out[i, 1] = second_ref[slot].astype(bf16)


def near_half(place, owner, rel, bit):
    z, core = place[1], place[2]
    source = owner[2 * (z ^ rel) + core]
    if bit < 0:
        return (source & 1) == core
    return (((source >> 1) ^ z) >> bit) & 1 == 0


def divide(rels, bit):
    keep = [i for i, rel in enumerate(rels) if not rel >> bit & 1]
    send = [rels.index(rels[i] ^ (1 << bit)) for i in keep]
    return keep, send


def merge_kernel(place, owner, *refs, rels, bits, cuts):
    inputs, outs = refs[:-4], refs[-4:]
    for t in range(2):
        for where, out in zip(divide(rels[t], cuts[t]), outs[2 * t : 2 * t + 2]):
            for j, i in enumerate(where):
                local = near_half(place, owner, rels[t][i], bits[t])
                if len(inputs) == 2:
                    own, lent = inputs[0][i, t], inputs[1][i, t]
                else:
                    own, lent = inputs[2 * t][i], inputs[2 * t + 1][i]
                out[j] = jnp.where(local, own, lent)


def project_kernel(place, *refs, scale):
    sums, relayed, arrived = refs[:2], refs[2:4], refs[4:6]
    keep_ref, basis_ref, mine_ref, sample_ref, other_ref = refs[6:]
    core = place[2]
    count, _, half = sums[0].shape
    for i in range(mine_ref.shape[0]):
        for out, want in ((other_ref, 1 - core), (mine_ref, core)):
            m = 2 * i + want
            scaled = (basis_ref[m] * scale).astype(bf16)
            for side in range(2):
                total = sums[side][m] + relayed[side][m].astype(f32)
                product = lax.dot_general(
                    scaled,
                    total.astype(bf16),
                    (((0,), (0,)), ((), ())),
                    preferred_element_type=f32,
                )
                out[i, :, side * half : (side + 1) * half] = product.astype(out.dtype)
    for i in range(keep_ref.shape[0]):
        for side in range(2):
            columns = slice(side * half, (side + 1) * half)
            total = keep_ref[i, :, columns] + arrived[side][0, count + i].astype(f32)
            total = total + relayed[side][count + i].astype(f32)
            sample_ref[i, :, columns] = total.astype(bf16)


def pair_kernel(place, mine_ref, other_ref, *outs):
    for k, out in enumerate(outs):
        i = place[1] ^ k
        out[...] = (mine_ref[i] + other_ref[i].astype(f32)).astype(out.dtype)


def update_kernel(place, owner, rank, *refs, chips, bits, start):
    terms = refs[:chips]
    first_ref, first_lent, second_ref, second_lent, update_ref, projected_ref = refs[chips:]
    z, core = place[1], place[2]
    m = 2 * z + core
    projected = terms[0][...].astype(f32)
    for ref in terms[1:]:
        projected = projected + ref[...].astype(f32)
    width = projected.shape[1]
    columns = slice(start, start + width)
    near = near_half(place, owner, 0, bits[0])
    first = jnp.where(near, first_ref[0, :, columns], first_lent[0, :, columns])
    near = near_half(place, owner, 0, bits[1])
    second = jnp.where(near, second_ref[0, :, columns], second_lent[0, :, columns])
    first_new = beta_one * first.astype(f32) + (1.0 - beta_one) * projected
    second_new = beta_two * second.astype(f32) + (1.0 - beta_two) * projected * projected
    update = (first_new / bias_one) / (jnp.sqrt(second_new / bias_two) + epsilon)
    row = lax.broadcasted_iota(jnp.int32, update.shape, 0)
    update_ref[...] = jnp.where(row < rank[m], update, 0.0).astype(bf16)
    projected_ref[...] = projected.astype(bf16)


def delta_kernel(place, *refs, chips, scale):
    near, far, basis_ref, projected_ref, *outs, passed_ref = refs
    half = outs[0].shape[2]
    z, core = place[1], place[2]
    passed_ref[...] = projected_ref[...]
    for k in range(chips):
        for ref, want in ((near, core), (far, 1 - core)):
            m = 2 * (z ^ k) + want
            product = jnp.dot(
                (basis_ref[m] * scale).astype(bf16), ref[k], preferred_element_type=f32
            )
            for side, out in enumerate(outs):
                out[m] = product[:, side * half : (side + 1) * half].astype(bf16)


def weight_kernel(place, weight_ref, *refs, groups, chunks):
    out_ref = refs[-1]
    width = refs[0].shape[2]
    for h in range(chunks):
        for k in range(groups):
            start = ((place[0] ^ k) * chunks + h) * width
            columns = pl.ds(pl.multiple_of(start, 128), width)
            for m in range(out_ref.shape[0]):
                delta = refs[h * groups + k][m].astype(f32)
                old = weight_ref[m, :, columns].astype(f32)
                out_ref[m, :, columns] = (old - step_size * delta).astype(bf16)


def basis_kernel(place, *refs):
    out_ref = refs[-1]
    each = refs[0].shape[0]
    for k, ref in enumerate(refs[:-1]):
        for i in range(each):
            out_ref[(place[0] ^ k) * each + i] = ref[i].astype(f32)


def moment_kernel(place, owner, *refs, chunks):
    projected_refs = refs[:chunks]
    first_ref, second_ref, first_out, second_out = refs[chunks:]
    here = place[1] * 2 + place[2]
    capacity, rank_full, _ = first_out.shape
    width = projected_refs[0].shape[2]
    seen = jnp.int32(0)
    index = [jnp.int32(0)] * capacity
    for m in range(owner.shape[0]):
        hit = owner[m] == here
        for s in range(capacity):
            index[s] = jnp.where(hit & (seen == s), m, index[s])
        seen = seen + hit.astype(jnp.int32)
    for s in range(capacity):
        keep = seen > s
        for h in range(chunks):
            columns = slice(h * width, (h + 1) * width)
            projected = projected_refs[h][index[s]].astype(f32)
            first_new = beta_one * first_ref[s, :, columns] + (1.0 - beta_one) * projected
            second_new = (
                beta_two * second_ref[s, :, columns] + (1.0 - beta_two) * projected * projected
            )
            first_out[s, :, columns] = jnp.where(keep, first_new, 0.0)
            second_out[s, :, columns] = jnp.where(keep, second_new, 0.0)


def per_device(grads, weight, basis, first_moment, second_moment, sketch, owner, rank):
    owners = lax.axis_size("rows")
    groups = lax.axis_size("dp")
    here = lax.axis_index("rows")
    group = lax.axis_index("dp")
    capacity, rank_full, quarter = first_moment.shape
    count, shard, width = weight.shape
    chips = owners // 2
    each = count // groups
    total_rows = shard * owners
    root = float(total_rows) ** 0.5
    inverse_root = float(total_rows) ** (-0.5)
    place = jnp.stack([group, here // 2, here % 2]).astype(jnp.int32)
    struct = jax.ShapeDtypeStruct

    call = Sequence()
    half = quarter // 2
    keep, relay, *sides = call(
        front_kernel,
        [struct((each, shard, rank_full), f32), struct((2, each, shard, half), f32)]
        + [struct((2, count + each, shard, half), bf16)] * 2,
        (place, grads, sketch),
        scalars=1,
    )
    sides = [swap(sides[i], "dp", 1 << i) for i in range(2)]
    picked, lent = call(
        pick_kernel,
        [struct((chips, 2, rank_full, quarter), bf16)] * 2,
        (place, owner, first_moment, second_moment),
        scalars=2,
    )
    inputs = [picked, swap(lent, "rows", 1)]
    rels = [list(range(chips)), list(range(chips))]
    bits = (-1, -1)
    levels = chips.bit_length() - 1
    for level in range(levels):
        cuts = (level, levels - 1 - level)
        merged = call(
            functools.partial(merge_kernel, rels=rels, bits=bits, cuts=cuts),
            [struct((len(rels[0]) // 2, rank_full, quarter), bf16)] * 4,
            (place, owner, *inputs),
            scalars=2,
        )
        rels = [[rels[t][i] for i in divide(rels[t], cuts[t])[0]] for t in range(2)]
        bits = cuts
        inputs = []
        for t in range(2):
            inputs += [merged[2 * t], swap(merged[2 * t + 1], "rows", 2 << cuts[t])]
    *sums, first_send, second_send = call(
        add_kernel,
        [struct((count, shard, half), f32)] * 2
        + [struct((count + each, shard, half), bf16)] * 2,
        (place, grads, relay, *sides),
        scalars=1,
    )
    relayed = [swap(first_send, "dp", 2), swap(second_send, "dp", 1)]
    mine, sample, other = call(
        functools.partial(project_kernel, scale=inverse_root),
        [
            struct((chips, rank_full, quarter), f32),
            struct((each, shard, rank_full), bf16),
            struct((chips, rank_full, quarter), bf16),
        ],
        (place, *sums, *relayed, *sides, keep, basis),
        scalars=1,
        after=(inputs[1], inputs[3]),
    )
    other = swap(other, "rows", 1)
    mask = chips // 2
    arrived = swap(sample, "rows", 2 * mask)
    terms = call(
        pair_kernel,
        [struct((rank_full, quarter), f32)] + [struct((rank_full, quarter), bf16)] * (chips - 1),
        (place, mine, other),
        scalars=1,
    )
    terms = [terms[0]] + [swap(terms[k], "rows", 2 * k) for k in range(1, chips)]
    stacked = sample
    while mask > 1:
        both = struct((2 * stacked.shape[0], shard, rank_full), bf16)
        stacked = call(stack_kernel, both, (stacked, arrived))
        mask //= 2
        arrived = swap(stacked, "rows", 2 * mask)
    work_shape = struct((each, rank_full, 2 * rank_full), f32)
    last = rank_full // BLOCK - 1
    update, projected = call(
        functools.partial(update_kernel, chips=chips, bits=bits, start=0),
        [struct((rank_full, quarter), bf16)] * 2,
        (place, owner, rank, *terms, *inputs),
        scalars=3,
        after=(arrived,),
    )
    near = [update] + [swap(update, "rows", 2 * k) for k in range(1, chips)]
    gram = call(
        gram_kernel, struct((each, rank_full, rank_full), f32), (stacked, arrived)
    )
    other_gram = swap(gram, "rows", 1)
    work = call(start_kernel, work_shape, (gram, other_gram))
    early = last // 2 + 1
    for j in range(1, early):
        work = call(functools.partial(middle_kernel, j=j), work_shape, (work,))
    near = call(
        gather_kernel,
        struct((chips, rank_full, quarter), bf16),
        tuple(near),
    )
    far = swap(near, "rows", 1)
    *own, projected = call(
        functools.partial(delta_kernel, chips=chips, scale=inverse_root),
        [struct((count, shard, half), bf16)] * 2 + [struct((rank_full, quarter), bf16)],
        (place, near, far, basis, projected),
        scalars=1,
    )
    beside = [swap(own[0], "dp", 1), swap(own[1], "dp", 2)]
    later = [swap(own[1], "dp", 1), swap(own[0], "dp", 2)]
    gathered = lax.all_gather(projected, "rows", axis=0)
    for j in range(early, last):
        work = call(functools.partial(middle_kernel, j=j), work_shape, (work,))
    passed = call(pass_kernel, [struct(own[0].shape, bf16)] * 2, tuple(beside))
    across = [swap(passed[0], "dp", 2), swap(passed[1], "dp", 1)]
    deltas = [own[0], beside[0], later[1], across[0], own[1], later[0], beside[1], across[1]]
    rows_basis = call(
        functools.partial(finish_kernel, j=last, scale=root),
        struct(sample.shape, bf16),
        (work, sample),
        scratch=[pltpu.VMEM(work_shape.shape, f32)],
    )
    shared = [rows_basis] + [swap(rows_basis, "dp", k) for k in range(1, groups)]
    first_out, second_out = call(
        functools.partial(moment_kernel, chunks=1),
        [struct(first_moment.shape, f32)] * 2,
        (place, owner, gathered, first_moment, second_moment),
        scalars=2,
        after=tuple(across),
    )
    new_weight = call(
        functools.partial(weight_kernel, groups=groups, chunks=2),
        struct(weight.shape, bf16),
        (place, weight, *deltas),
        scalars=1,
    )
    new_basis = call(basis_kernel, struct(basis.shape, f32), (place, *shared), scalars=1)
    return (new_weight, new_basis, first_out, second_out)


def solution(mesh):
    in_specs = (
        P("dp", None, "rows", None),
        P(None, "rows", None),
        P(None, "rows", None),
        P("rows", None, "dp"),
        P("rows", None, "dp"),
        P(),
        P(),
        P(),
    )
    out_specs = (
        P(None, "rows", None),
        P(None, "rows", None),
        P("rows", None, "dp"),
        P("rows", None, "dp"),
    )
    return jax.shard_map(
        per_device, mesh=mesh, in_specs=in_specs, out_specs=out_specs, check_vma=False
    )
```

```python
import functools

import jax
import jax.numpy as jnp
from jax import lax
from jax.experimental import pallas as pl
from jax.experimental.pallas import tpu as pltpu
from jax.sharding import PartitionSpec as P

beta_one = 0.9
beta_two = 0.95
bias_one = 1.0 - 0.9**10
bias_two = 1.0 - 0.95**10
step_size = 0.5
epsilon = 1e-08
BLOCK = 64
GROUP = 4
COST = 10_000
HIGHEST = lax.Precision.HIGHEST
VMEM_LIMIT = 48 * 1024 * 1024
VMEM = pl.BlockSpec(memory_space=pltpu.VMEM)
ANY = pl.BlockSpec(memory_space=pl.ANY)
SMEM = pl.BlockSpec(memory_space=pltpu.SMEM)
f32 = jnp.float32
bf16 = jnp.bfloat16


class Sequence:
    def __init__(self):
        self.last = None

    def __call__(self, kernel, out_shape, args, scalars=0, us=2.0, scratch=(), after=(), hbm=0, direct=False):
        many = isinstance(out_shape, (tuple, list))
        specs = [SMEM] * scalars + [ANY] * hbm + [VMEM] * (len(args) - scalars - hbm)
        place_out = ANY if direct else VMEM
        body = kernel
        if self.last is not None:
            after = (self.last, *after)
        unread = len(after)
        if unread:
            specs = [ANY] * unread + specs
            args = (*after, *args)

            def body(*refs):
                kernel(*refs[unread:])

        result = pl.pallas_call(
            body,
            out_shape=out_shape,
            in_specs=specs,
            out_specs=[place_out] * len(out_shape) if many else place_out,
            scratch_shapes=list(scratch),
            compiler_params=pltpu.CompilerParams(vmem_limit_bytes=VMEM_LIMIT),
            cost_estimate=pl.CostEstimate(
                flops=0, bytes_accessed=int(us * COST), transcendentals=0
            ),
        )(*args)
        self.last = result[-1] if many else result
        return result


def swap(x, axis, mask):
    size = lax.axis_size(axis)
    return lax.ppermute(x, axis, [(i, i ^ mask) for i in range(size)])


def front_kernel(place, grad_ref, sketch_ref, keep_ref, relay_ref, *outs):
    half = outs[0].shape[3]
    count, each = grad_ref.shape[1], keep_ref.shape[0]
    for side, out in enumerate(outs):
        for i, k in enumerate((1 << side, 3)):
            start = (place[0] ^ k) * 2 + side
            columns = pl.ds(pl.multiple_of(start * half, half), half)
            out[i, :count] = grad_ref[0, :, :, columns]
    for k in range(4):
        for i in range(each):
            m = (place[0] ^ k) * each + i
            part = jnp.dot(grad_ref[0, m], sketch_ref[...], preferred_element_type=f32)
            if k == 0:
                keep_ref[i] = part
                continue
            for side, out in enumerate(outs):
                piece = part[:, side * half : (side + 1) * half]
                if k == 2 >> side:
                    relay_ref[side, i] = piece
                else:
                    out[k // 3, count + i] = piece.astype(bf16)


def add_kernel(place, grad_ref, relay_ref, *refs):
    arrived, sums, sends = refs[:2], refs[2:4], refs[4:]
    count, _, half = sums[0].shape
    for side in range(2):
        for i, (k, out) in enumerate(((0, sums[side]), (2 >> side, sends[side]))):
            start = (place[0] ^ k) * 2 + side
            columns = pl.ds(pl.multiple_of(start * half, half), half)
            for m in range(count):
                total = grad_ref[0, m, :, columns].astype(f32) + arrived[side][i, m].astype(f32)
                out[m] = total.astype(out.dtype)
        for i in range(relay_ref.shape[1]):
            total = relay_ref[side, i] + arrived[side][1, count + i].astype(f32)
            sends[side][count + i] = total.astype(bf16)


def gather_kernel(*refs):
    for k, ref in enumerate(refs[:-1]):
        refs[-1][k] = ref[...]


def pass_kernel(*refs):
    half = len(refs) // 2
    for ref, out in zip(refs[:half], refs[half:]):
        out[...] = ref[...]


def gram_kernel(mixed_ref, *refs):
    out = refs[-1]
    each, size, _ = out.shape
    shard = refs[0].shape[1]
    for i in range(each):
        first = size + i * shard
        blocks = [mixed_ref[first : first + shard]] + [ref[i] for ref in refs[:-1]]
        total = None
        for block in blocks:
            term = lax.dot_general(
                block, block, (((0,), (0,)), ((), ())), preferred_element_type=f32
            )
            total = term if total is None else total + term
        out[i] = total


def eliminate(work, j):
    pair, size = work.shape[0], work.shape[1]
    lane = lax.broadcasted_iota(jnp.int32, (BLOCK, 2 * BLOCK), 1)
    sub = lax.broadcasted_iota(jnp.int32, (BLOCK, 2 * BLOCK), 0)
    eye_right = (lane - BLOCK == sub).astype(f32)
    lo = j * BLOCK
    base = lo // 128 * 128
    tiles = []
    for b in range(pair):
        slab = work[b, lo : lo + BLOCK, base : base + 128]
        if lo > base:
            slab = pltpu.roll(slab, 128 - (lo - base), 1)
        tiles.append(jnp.where(lane < BLOCK, slab, eye_right))
    for first in range(0, BLOCK, GROUP):
        for b in range(pair):
            tile = tiles[b]
            columns = [
                jnp.broadcast_to(tile[:, k : k + 1], tile.shape)
                for k in range(first, first + GROUP)
            ]
            rows = []
            for i in range(GROUP):
                k = first + i
                inverse = 1.0 / columns[i][k : k + 1, :]
                row = tile[k : k + 1, :]
                for j in range(i):
                    row = row - columns[j][k : k + 1, :] * rows[j]
                rows.append(row * inverse)
                columns[i] = jnp.where(sub > k, columns[i], 0.0)
                for j in range(i + 1, GROUP):
                    columns[j] = columns[j] - columns[i] * (columns[j][k : k + 1, :] * inverse)
            for i in range(GROUP):
                tile = tile - columns[i] * rows[i]
            tiles[b] = tile
    for b in range(pair):
        tile = tiles[b]
        diagonal = jnp.sum(jnp.where(lane == sub, tile, 0.0), axis=1, keepdims=True)
        inverse = pltpu.roll(tile, BLOCK, 1)[:, :BLOCK] * lax.rsqrt(diagonal)
        solved = jnp.dot(
            inverse, work[b, lo : lo + BLOCK, :], precision=HIGHEST, preferred_element_type=f32
        )
        work[b, lo : lo + BLOCK, size:] = solved[:, size:]
        if lo + BLOCK < size:
            change = lax.dot_general(
                solved[:, :size],
                solved,
                (((0,), (0,)), ((), ())),
                precision=HIGHEST,
                preferred_element_type=f32,
            )
            work[b, lo + BLOCK :, :] = work[b, lo + BLOCK :, :] - change[lo + BLOCK :, :]


def start_kernel(own_ref, other_ref, work):
    pair, size = own_ref.shape[0], own_ref.shape[1]
    row = lax.broadcasted_iota(jnp.int32, (size, size), 0)
    col = lax.broadcasted_iota(jnp.int32, (size, size), 1)
    eye = (row == col).astype(f32)
    for b in range(pair):
        work[b, :, :size] = own_ref[b] + other_ref[b]
        work[b, :, size:] = eye
    eliminate(work, 0)


def middle_kernel(work_in, work, *, j):
    work[...] = work_in[...]
    eliminate(work, j)


def finish_kernel(work_in, rows_ref, out_ref, work, *, j, scale):
    work[...] = work_in[...]
    eliminate(work, j)
    size = work.shape[1]
    for b in range(work.shape[0]):
        basis = lax.dot_general(
            rows_ref[b].astype(f32),
            work[b, :, size:],
            (((1,), (1,)), ((), ())),
            precision=HIGHEST,
            preferred_element_type=f32,
        )
        out_ref[b] = (basis * scale).astype(out_ref.dtype)


def pick_kernel(place, owner, first_ref, second_ref, mine_ref, other_ref):
    here, core = place[1] * 2 + place[2], place[2]
    capacity = first_ref.shape[0]
    seen = jnp.int32(0)
    at = []
    for m in range(owner.shape[0]):
        at.append(jnp.minimum(seen, capacity - 1))
        seen = seen + (owner[m] == here).astype(jnp.int32)
    chips = mine_ref.shape[0]
    for i in range(chips):
        for out, want in ((mine_ref, core), (other_ref, 1 - core)):
            slot = jnp.int32(0)
            m = 2 * (place[1] ^ i) + want
            for j in range(owner.shape[0]):
                slot = jnp.where(m == j, at[j], slot)
            out[i, 0] = first_ref[slot].astype(bf16)
            out[i, 1] = second_ref[slot].astype(bf16)


def near_half(place, owner, rel, bit):
    z, core = place[1], place[2]
    source = owner[2 * (z ^ rel) + core]
    if bit < 0:
        return (source & 1) == core
    return (((source >> 1) ^ z) >> bit) & 1 == 0


def divide(rels, bit):
    keep = [i for i, rel in enumerate(rels) if not rel >> bit & 1]
    send = [rels.index(rels[i] ^ (1 << bit)) for i in keep]
    return keep, send


def merge_kernel(place, owner, *refs, rels, bits, cuts):
    inputs, outs = refs[:-4], refs[-4:]
    for t in range(2):
        for where, out in zip(divide(rels[t], cuts[t]), outs[2 * t : 2 * t + 2]):
            for j, i in enumerate(where):
                local = near_half(place, owner, rels[t][i], bits[t])
                if len(inputs) == 2:
                    own, lent = inputs[0][i, t], inputs[1][i, t]
                else:
                    own, lent = inputs[2 * t][i], inputs[2 * t + 1][i]
                out[j] = jnp.where(local, own, lent)


def project_kernel(place, *refs, scale):
    sums, relayed, arrived = refs[:2], refs[2:4], refs[4:6]
    keep_ref, basis_ref, mine_ref, sample_ref, other_ref = refs[6:]
    core = place[2]
    count, _, half = sums[0].shape
    for i in range(mine_ref.shape[0]):
        for out, want in ((other_ref, 1 - core), (mine_ref, core)):
            m = 2 * i + want
            scaled = (basis_ref[m] * scale).astype(bf16)
            for side in range(2):
                total = sums[side][m] + relayed[side][m].astype(f32)
                product = lax.dot_general(
                    scaled,
                    total.astype(bf16),
                    (((0,), (0,)), ((), ())),
                    preferred_element_type=f32,
                )
                out[i, :, side * half : (side + 1) * half] = product.astype(out.dtype)
    for i in range(keep_ref.shape[0]):
        for side in range(2):
            columns = slice(side * half, (side + 1) * half)
            total = keep_ref[i, :, columns] + arrived[side][0, count + i].astype(f32)
            total = total + relayed[side][count + i].astype(f32)
            sample_ref[i, :, columns] = total.astype(bf16)


def pair_kernel(place, mine_ref, other_ref, sample_ref, *outs):
    rank_full = mine_ref.shape[1]
    each, shard, _ = sample_ref.shape
    for k, out in enumerate(outs):
        i = place[1] ^ k
        out[:rank_full] = (mine_ref[i] + other_ref[i].astype(f32)).astype(out.dtype)
    for i in range(each):
        first = rank_full + i * shard
        outs[1][first : first + shard] = sample_ref[i]


def update_kernel(place, owner, rank, *refs, chips, bits, start):
    terms = refs[:chips]
    first_ref, first_lent, second_ref, second_lent, update_ref, projected_ref = refs[chips:]
    z, core = place[1], place[2]
    m = 2 * z + core
    projected = terms[0][...].astype(f32)
    for ref in terms[1:]:
        projected = projected + ref[: projected.shape[0]].astype(f32)
    width = projected.shape[1]
    columns = slice(start, start + width)
    near = near_half(place, owner, 0, bits[0])
    first = jnp.where(near, first_ref[0, :, columns], first_lent[0, :, columns])
    near = near_half(place, owner, 0, bits[1])
    second = jnp.where(near, second_ref[0, :, columns], second_lent[0, :, columns])
    first_new = beta_one * first.astype(f32) + (1.0 - beta_one) * projected
    second_new = beta_two * second.astype(f32) + (1.0 - beta_two) * projected * projected
    update = (first_new / bias_one) / (jnp.sqrt(second_new / bias_two) + epsilon)
    row = lax.broadcasted_iota(jnp.int32, update.shape, 0)
    update_ref[...] = jnp.where(row < rank[m], update, 0.0).astype(bf16)
    projected_ref[...] = projected.astype(bf16)


def delta_kernel(place, *refs, chips, scale):
    near, far, basis_ref, projected_ref, *outs, passed_ref = refs
    half = outs[0].shape[2]
    z, core = place[1], place[2]
    passed_ref[...] = projected_ref[...]
    for k in range(chips):
        for ref, want in ((near, core), (far, 1 - core)):
            m = 2 * (z ^ k) + want
            product = jnp.dot(
                (basis_ref[m] * scale).astype(bf16), ref[k], preferred_element_type=f32
            )
            for side, out in enumerate(outs):
                out[m] = product[:, side * half : (side + 1) * half].astype(bf16)


def weight_kernel(place, weight_ref, *refs, groups, chunks):
    *deltas, out_hbm, out_ref, sems = refs
    width = deltas[0].shape[2]
    copies = []
    for m in range(out_ref.shape[0]):
        for h in range(chunks):
            for k in range(groups):
                start = ((place[0] ^ k) * chunks + h) * width
                columns = pl.ds(pl.multiple_of(start, 128), width)
                delta = deltas[h * groups + k][m].astype(f32)
                old = weight_ref[m, :, columns].astype(f32)
                out_ref[m, :, columns] = (old - step_size * delta).astype(bf16)
        copies.append(pltpu.make_async_copy(out_ref.at[m], out_hbm.at[m], sems.at[m]))
        copies[-1].start()
    for copy in copies:
        copy.wait()


def basis_kernel(place, *refs):
    out_ref = refs[-1]
    each = refs[0].shape[0]
    for k, ref in enumerate(refs[:-1]):
        for i in range(each):
            out_ref[(place[0] ^ k) * each + i] = ref[i].astype(f32)


def moment_kernel(place, owner, projected_hbm, first_ref, second_ref, *refs):
    first_hbm, second_hbm, projected_ref, first_out, second_out, sems = refs
    here = place[1] * 2 + place[2]
    capacity = first_out.shape[0]
    seen = jnp.int32(0)
    index = [jnp.int32(0)] * capacity
    for m in range(owner.shape[0]):
        hit = owner[m] == here
        for s in range(capacity):
            index[s] = jnp.where(hit & (seen == s), m, index[s])
        seen = seen + hit.astype(jnp.int32)
    fetches = [
        pltpu.make_async_copy(projected_hbm.at[index[s]], projected_ref.at[s], sems.at[0, s])
        for s in range(capacity)
    ]
    for fetch in fetches:
        fetch.start()
    copies = []
    for s in range(capacity):
        fetches[s].wait()
        keep = seen > s
        projected = projected_ref[s].astype(f32)
        first_new = beta_one * first_ref[s] + (1.0 - beta_one) * projected
        second_new = beta_two * second_ref[s] + (1.0 - beta_two) * projected * projected
        first_out[s] = jnp.where(keep, first_new, 0.0)
        second_out[s] = jnp.where(keep, second_new, 0.0)
        pairs = ((first_out, first_hbm), (second_out, second_hbm))
        for t, (source, target) in enumerate(pairs):
            copies.append(
                pltpu.make_async_copy(source.at[s], target.at[s], sems.at[1 + t, s])
            )
            copies[-1].start()
    for copy in copies:
        copy.wait()


def per_device(grads, weight, basis, first_moment, second_moment, sketch, owner, rank):
    owners = lax.axis_size("rows")
    groups = lax.axis_size("dp")
    here = lax.axis_index("rows")
    group = lax.axis_index("dp")
    capacity, rank_full, quarter = first_moment.shape
    count, shard, width = weight.shape
    chips = owners // 2
    each = count // groups
    total_rows = shard * owners
    root = float(total_rows) ** 0.5
    inverse_root = float(total_rows) ** (-0.5)
    place = jnp.stack([group, here // 2, here % 2]).astype(jnp.int32)
    struct = jax.ShapeDtypeStruct

    call = Sequence()
    half = quarter // 2
    keep, relay, *sides = call(
        front_kernel,
        [struct((each, shard, rank_full), f32), struct((2, each, shard, half), f32)]
        + [struct((2, count + each, shard, half), bf16)] * 2,
        (place, grads, sketch),
        scalars=1,
    )
    sides = [swap(sides[i], "dp", 1 << i) for i in range(2)]
    picked, lent = call(
        pick_kernel,
        [struct((chips, 2, rank_full, quarter), bf16)] * 2,
        (place, owner, first_moment, second_moment),
        scalars=2,
    )
    inputs = [picked, swap(lent, "rows", 1)]
    rels = [list(range(chips)), list(range(chips))]
    bits = (-1, -1)
    levels = chips.bit_length() - 1
    for level in range(levels):
        cuts = (level, levels - 1 - level)
        merged = call(
            functools.partial(merge_kernel, rels=rels, bits=bits, cuts=cuts),
            [struct((len(rels[0]) // 2, rank_full, quarter), bf16)] * 4,
            (place, owner, *inputs),
            scalars=2,
        )
        rels = [[rels[t][i] for i in divide(rels[t], cuts[t])[0]] for t in range(2)]
        bits = cuts
        inputs = []
        for t in range(2):
            inputs += [merged[2 * t], swap(merged[2 * t + 1], "rows", 2 << cuts[t])]
    *sums, first_send, second_send = call(
        add_kernel,
        [struct((count, shard, half), f32)] * 2
        + [struct((count + each, shard, half), bf16)] * 2,
        (place, grads, relay, *sides),
        scalars=1,
    )
    relayed = [swap(first_send, "dp", 2), swap(second_send, "dp", 1)]
    mine, sample, other = call(
        functools.partial(project_kernel, scale=inverse_root),
        [
            struct((chips, rank_full, quarter), f32),
            struct((each, shard, rank_full), bf16),
            struct((chips, rank_full, quarter), bf16),
        ],
        (place, *sums, *relayed, *sides, keep, basis),
        scalars=1,
        after=(inputs[1], inputs[3]),
    )
    other = swap(other, "rows", 1)
    samples = [sample]
    mask = chips // 2
    while mask > 1:
        samples += [swap(x, "rows", 2 * mask) for x in samples]
        mask //= 2
    terms = call(
        pair_kernel,
        [
            struct((rank_full, quarter), f32),
            struct((rank_full + each * shard, quarter), bf16),
        ]
        + [struct((rank_full, quarter), bf16)] * (chips - 2),
        (place, mine, other, sample),
        scalars=1,
    )
    samples += [swap(x, "rows", 2) for x in samples[1:]]
    terms = [terms[0]] + [swap(terms[k], "rows", 2 * k) for k in range(1, chips)]
    work_shape = struct((each, rank_full, 2 * rank_full), f32)
    last = rank_full // BLOCK - 1
    update, projected = call(
        functools.partial(update_kernel, chips=chips, bits=bits, start=0),
        [struct((rank_full, quarter), bf16)] * 2,
        (place, owner, rank, *terms, *inputs),
        scalars=3,
        after=tuple(samples[1:]),
    )
    near = [update] + [swap(update, "rows", 2 * k) for k in range(1, chips)]
    gram = call(
        gram_kernel, struct((each, rank_full, rank_full), f32), (terms[1], *samples)
    )
    other_gram = swap(gram, "rows", 1)
    work = call(start_kernel, work_shape, (gram, other_gram))
    early = last // 2 + 1
    for j in range(1, early):
        work = call(functools.partial(middle_kernel, j=j), work_shape, (work,))
    near = call(
        gather_kernel,
        struct((chips, rank_full, quarter), bf16),
        tuple(near),
    )
    far = swap(near, "rows", 1)
    *own, projected = call(
        functools.partial(delta_kernel, chips=chips, scale=inverse_root),
        [struct((count, shard, half), bf16)] * 2 + [struct((rank_full, quarter), bf16)],
        (place, near, far, basis, projected),
        scalars=1,
    )
    beside = [swap(own[0], "dp", 1), swap(own[1], "dp", 2)]
    later = [swap(own[1], "dp", 1), swap(own[0], "dp", 2)]
    gathered = lax.all_gather(projected, "rows", axis=0)
    for j in range(early, last):
        work = call(functools.partial(middle_kernel, j=j), work_shape, (work,))
    passed = call(pass_kernel, [struct(own[0].shape, bf16)] * 2, tuple(beside))
    across = [swap(passed[0], "dp", 2), swap(passed[1], "dp", 1)]
    deltas = [own[0], beside[0], later[1], across[0], own[1], later[0], beside[1], across[1]]
    rows_basis = call(
        functools.partial(finish_kernel, j=last, scale=root),
        struct(sample.shape, bf16),
        (work, sample),
        scratch=[pltpu.VMEM(work_shape.shape, f32)],
    )
    shared = [rows_basis] + [swap(rows_basis, "dp", k) for k in range(1, groups)]
    first_out, second_out = call(
        moment_kernel,
        [struct(first_moment.shape, f32)] * 2,
        (place, owner, gathered, first_moment, second_moment),
        scalars=2,
        after=tuple(across),
        hbm=1,
        direct=True,
        scratch=[
            pltpu.VMEM(first_moment.shape, bf16),
            pltpu.VMEM(first_moment.shape, f32),
            pltpu.VMEM(first_moment.shape, f32),
            pltpu.SemaphoreType.DMA((3, capacity)),
        ],
    )
    new_weight = call(
        functools.partial(weight_kernel, groups=groups, chunks=2),
        struct(weight.shape, bf16),
        (place, weight, *deltas),
        scalars=1,
        direct=True,
        scratch=[pltpu.VMEM(weight.shape, bf16), pltpu.SemaphoreType.DMA((count,))],
    )
    new_basis = call(basis_kernel, struct(basis.shape, f32), (place, *shared), scalars=1)
    return (new_weight, new_basis, first_out, second_out)


def solution(mesh):
    in_specs = (
        P("dp", None, "rows", None),
        P(None, "rows", None),
        P(None, "rows", None),
        P("rows", None, "dp"),
        P("rows", None, "dp"),
        P(),
        P(),
        P(),
    )
    out_specs = (
        P(None, "rows", None),
        P(None, "rows", None),
        P("rows", None, "dp"),
        P("rows", None, "dp"),
    )
    return jax.shard_map(
        per_device, mesh=mesh, in_specs=in_specs, out_specs=out_specs, check_vma=False
    )
```

```python
import functools

import jax
import jax.numpy as jnp
from jax import lax
from jax.experimental import pallas as pl
from jax.experimental.pallas import tpu as pltpu
from jax.sharding import PartitionSpec as P

beta_one = 0.9
beta_two = 0.95
bias_one = 1.0 - 0.9**10
bias_two = 1.0 - 0.95**10
step_size = 0.5
epsilon = 1e-08
BLOCK = 64
GROUP = 4
COST = 10_000
HIGHEST = lax.Precision.HIGHEST
VMEM_LIMIT = 48 * 1024 * 1024
VMEM = pl.BlockSpec(memory_space=pltpu.VMEM)
ANY = pl.BlockSpec(memory_space=pl.ANY)
HBM = pl.BlockSpec(memory_space=pltpu.HBM)
SMEM = pl.BlockSpec(memory_space=pltpu.SMEM)
f32 = jnp.float32
bf16 = jnp.bfloat16


class Sequence:
    def __init__(self):
        self.last = None

    def __call__(self, kernel, out_shape, args, scalars=0, us=2.0, scratch=(), after=(), hbm=0, direct=False):
        many = isinstance(out_shape, (tuple, list))
        specs = [SMEM] * scalars + [HBM] * hbm + [VMEM] * (len(args) - scalars - hbm)
        place_out = HBM if direct else VMEM
        body = kernel
        if self.last is not None:
            after = (self.last, *after)
        unread = len(after)
        if unread:
            specs = [ANY] * unread + specs
            args = (*after, *args)

            def body(*refs):
                kernel(*refs[unread:])

        result = pl.pallas_call(
            body,
            out_shape=out_shape,
            in_specs=specs,
            out_specs=[place_out] * len(out_shape) if many else place_out,
            scratch_shapes=list(scratch),
            compiler_params=pltpu.CompilerParams(vmem_limit_bytes=VMEM_LIMIT),
            cost_estimate=pl.CostEstimate(
                flops=0, bytes_accessed=int(us * COST), transcendentals=0
            ),
        )(*args)
        self.last = result[-1] if many else result
        return result


def swap(x, axis, mask):
    size = lax.axis_size(axis)
    return lax.ppermute(x, axis, [(i, i ^ mask) for i in range(size)])


def front_kernel(place, grad_ref, sketch_ref, keep_ref, relay_ref, *outs):
    half = outs[0].shape[3]
    count, each = grad_ref.shape[1], keep_ref.shape[0]
    for side, out in enumerate(outs):
        for i, k in enumerate((1 << side, 3)):
            start = (place[0] ^ k) * 2 + side
            columns = pl.ds(pl.multiple_of(start * half, half), half)
            out[i, :count] = grad_ref[0, :, :, columns]
    for k in range(4):
        for i in range(each):
            m = (place[0] ^ k) * each + i
            part = jnp.dot(grad_ref[0, m], sketch_ref[...], preferred_element_type=f32)
            if k == 0:
                keep_ref[i] = part
                continue
            for side, out in enumerate(outs):
                piece = part[:, side * half : (side + 1) * half]
                if k == 2 >> side:
                    relay_ref[side, i] = piece
                else:
                    out[k // 3, count + i] = piece.astype(bf16)


def add_kernel(place, grad_ref, relay_ref, *refs):
    arrived, sums, sends = refs[:2], refs[2:4], refs[4:]
    count, _, half = sums[0].shape
    for side in range(2):
        for i, (k, out) in enumerate(((0, sums[side]), (2 >> side, sends[side]))):
            start = (place[0] ^ k) * 2 + side
            columns = pl.ds(pl.multiple_of(start * half, half), half)
            for m in range(count):
                total = grad_ref[0, m, :, columns].astype(f32) + arrived[side][i, m].astype(f32)
                out[m] = total.astype(out.dtype)
        for i in range(relay_ref.shape[1]):
            total = relay_ref[side, i] + arrived[side][1, count + i].astype(f32)
            sends[side][count + i] = total.astype(bf16)


def gather_kernel(*refs):
    for k, ref in enumerate(refs[:-1]):
        refs[-1][k] = ref[...]


def pass_kernel(*refs):
    half = len(refs) // 2
    for ref, out in zip(refs[:half], refs[half:]):
        out[...] = ref[...]


def gram_kernel(mixed_ref, *refs):
    out = refs[-1]
    each, size, _ = out.shape
    shard = refs[0].shape[1]
    for i in range(each):
        first = size + i * shard
        blocks = [mixed_ref[first : first + shard]] + [ref[i] for ref in refs[:-1]]
        total = None
        for block in blocks:
            term = lax.dot_general(
                block, block, (((0,), (0,)), ((), ())), preferred_element_type=f32
            )
            total = term if total is None else total + term
        out[i] = total


def eliminate(work, j):
    pair, size = work.shape[0], work.shape[1]
    lane = lax.broadcasted_iota(jnp.int32, (BLOCK, 2 * BLOCK), 1)
    sub = lax.broadcasted_iota(jnp.int32, (BLOCK, 2 * BLOCK), 0)
    eye_right = (lane - BLOCK == sub).astype(f32)
    lo = j * BLOCK
    base = lo // 128 * 128
    tiles = []
    for b in range(pair):
        slab = work[b, lo : lo + BLOCK, base : base + 128]
        if lo > base:
            slab = pltpu.roll(slab, 128 - (lo - base), 1)
        tiles.append(jnp.where(lane < BLOCK, slab, eye_right))
    for first in range(0, BLOCK, GROUP):
        for b in range(pair):
            tile = tiles[b]
            columns = [
                jnp.broadcast_to(tile[:, k : k + 1], tile.shape)
                for k in range(first, first + GROUP)
            ]
            rows = []
            for i in range(GROUP):
                k = first + i
                inverse = 1.0 / columns[i][k : k + 1, :]
                row = tile[k : k + 1, :]
                for j in range(i):
                    row = row - columns[j][k : k + 1, :] * rows[j]
                rows.append(row * inverse)
                columns[i] = jnp.where(sub > k, columns[i], 0.0)
                for j in range(i + 1, GROUP):
                    columns[j] = columns[j] - columns[i] * (columns[j][k : k + 1, :] * inverse)
            for i in range(GROUP):
                tile = tile - columns[i] * rows[i]
            tiles[b] = tile
    for b in range(pair):
        tile = tiles[b]
        diagonal = jnp.sum(jnp.where(lane == sub, tile, 0.0), axis=1, keepdims=True)
        inverse = pltpu.roll(tile, BLOCK, 1)[:, :BLOCK] * lax.rsqrt(diagonal)
        solved = jnp.dot(
            inverse, work[b, lo : lo + BLOCK, :], precision=HIGHEST, preferred_element_type=f32
        )
        work[b, lo : lo + BLOCK, size:] = solved[:, size:]
        if lo + BLOCK < size:
            change = lax.dot_general(
                solved[:, :size],
                solved,
                (((0,), (0,)), ((), ())),
                precision=HIGHEST,
                preferred_element_type=f32,
            )
            work[b, lo + BLOCK :, :] = work[b, lo + BLOCK :, :] - change[lo + BLOCK :, :]


def start_kernel(own_ref, other_ref, work):
    pair, size = own_ref.shape[0], own_ref.shape[1]
    row = lax.broadcasted_iota(jnp.int32, (size, size), 0)
    col = lax.broadcasted_iota(jnp.int32, (size, size), 1)
    eye = (row == col).astype(f32)
    for b in range(pair):
        work[b, :, :size] = own_ref[b] + other_ref[b]
        work[b, :, size:] = eye
    eliminate(work, 0)


def middle_kernel(work_in, work, *, j):
    work[...] = work_in[...]
    eliminate(work, j)


def finish_kernel(work_in, rows_ref, out_ref, work, *, j, scale):
    work[...] = work_in[...]
    eliminate(work, j)
    size = work.shape[1]
    for b in range(work.shape[0]):
        basis = lax.dot_general(
            rows_ref[b].astype(f32),
            work[b, :, size:],
            (((1,), (1,)), ((), ())),
            precision=HIGHEST,
            preferred_element_type=f32,
        )
        out_ref[b] = (basis * scale).astype(out_ref.dtype)


def pick_kernel(place, owner, first_ref, second_ref, mine_ref, other_ref):
    here, core = place[1] * 2 + place[2], place[2]
    capacity = first_ref.shape[0]
    seen = jnp.int32(0)
    at = []
    for m in range(owner.shape[0]):
        at.append(jnp.minimum(seen, capacity - 1))
        seen = seen + (owner[m] == here).astype(jnp.int32)
    chips = mine_ref.shape[0]
    for i in range(chips):
        for out, want in ((mine_ref, core), (other_ref, 1 - core)):
            slot = jnp.int32(0)
            m = 2 * (place[1] ^ i) + want
            for j in range(owner.shape[0]):
                slot = jnp.where(m == j, at[j], slot)
            out[i, 0] = first_ref[slot].astype(bf16)
            out[i, 1] = second_ref[slot].astype(bf16)


def near_half(place, owner, rel, bit):
    z, core = place[1], place[2]
    source = owner[2 * (z ^ rel) + core]
    if bit < 0:
        return (source & 1) == core
    return (((source >> 1) ^ z) >> bit) & 1 == 0


def divide(rels, bit):
    keep = [i for i, rel in enumerate(rels) if not rel >> bit & 1]
    send = [rels.index(rels[i] ^ (1 << bit)) for i in keep]
    return keep, send


def merge_kernel(place, owner, *refs, rels, bits, cuts):
    inputs, outs = refs[:-4], refs[-4:]
    for t in range(2):
        for where, out in zip(divide(rels[t], cuts[t]), outs[2 * t : 2 * t + 2]):
            for j, i in enumerate(where):
                local = near_half(place, owner, rels[t][i], bits[t])
                if len(inputs) == 2:
                    own, lent = inputs[0][i, t], inputs[1][i, t]
                else:
                    own, lent = inputs[2 * t][i], inputs[2 * t + 1][i]
                out[j] = jnp.where(local, own, lent)


def project_kernel(place, *refs, scale):
    sums, relayed, arrived = refs[:2], refs[2:4], refs[4:6]
    keep_ref, basis_ref, mine_ref, sample_ref, other_ref = refs[6:]
    core = place[2]
    count, _, half = sums[0].shape
    for i in range(mine_ref.shape[0]):
        for out, want in ((other_ref, 1 - core), (mine_ref, core)):
            m = 2 * i + want
            scaled = (basis_ref[m] * scale).astype(bf16)
            for side in range(2):
                total = sums[side][m] + relayed[side][m].astype(f32)
                product = lax.dot_general(
                    scaled,
                    total.astype(bf16),
                    (((0,), (0,)), ((), ())),
                    preferred_element_type=f32,
                )
                out[i, :, side * half : (side + 1) * half] = product.astype(out.dtype)
    for i in range(keep_ref.shape[0]):
        for side in range(2):
            columns = slice(side * half, (side + 1) * half)
            total = keep_ref[i, :, columns] + arrived[side][0, count + i].astype(f32)
            total = total + relayed[side][count + i].astype(f32)
            sample_ref[i, :, columns] = total.astype(bf16)


def pair_kernel(place, mine_ref, other_ref, sample_ref, *outs):
    rank_full = mine_ref.shape[1]
    each, shard, _ = sample_ref.shape
    for k, out in enumerate(outs):
        i = place[1] ^ k
        out[:rank_full] = (mine_ref[i] + other_ref[i].astype(f32)).astype(out.dtype)
    for i in range(each):
        first = rank_full + i * shard
        outs[1][first : first + shard] = sample_ref[i]


def update_kernel(place, owner, rank, *refs, chips, bits, start):
    terms = refs[:chips]
    first_ref, first_lent, second_ref, second_lent, update_ref, projected_ref = refs[chips:]
    z, core = place[1], place[2]
    m = 2 * z + core
    projected = terms[0][...].astype(f32)
    for ref in terms[1:]:
        projected = projected + ref[: projected.shape[0]].astype(f32)
    width = projected.shape[1]
    columns = slice(start, start + width)
    near = near_half(place, owner, 0, bits[0])
    first = jnp.where(near, first_ref[0, :, columns], first_lent[0, :, columns])
    near = near_half(place, owner, 0, bits[1])
    second = jnp.where(near, second_ref[0, :, columns], second_lent[0, :, columns])
    first_new = beta_one * first.astype(f32) + (1.0 - beta_one) * projected
    second_new = beta_two * second.astype(f32) + (1.0 - beta_two) * projected * projected
    update = (first_new / bias_one) / (jnp.sqrt(second_new / bias_two) + epsilon)
    row = lax.broadcasted_iota(jnp.int32, update.shape, 0)
    update_ref[...] = jnp.where(row < rank[m], update, 0.0).astype(bf16)
    projected_ref[...] = projected.astype(bf16)


def delta_kernel(place, *refs, chips, scale):
    near, far, basis_ref, projected_ref, *outs, passed_ref = refs
    half = outs[0].shape[2]
    z, core = place[1], place[2]
    passed_ref[...] = projected_ref[...]
    for k in range(chips):
        for ref, want in ((near, core), (far, 1 - core)):
            m = 2 * (z ^ k) + want
            product = jnp.dot(
                (basis_ref[m] * scale).astype(bf16), ref[k], preferred_element_type=f32
            )
            for side, out in enumerate(outs):
                out[m] = product[:, side * half : (side + 1) * half].astype(bf16)


def weight_kernel(place, weight_ref, *refs, groups, chunks):
    *deltas, out_hbm, out_ref, sems = refs
    width = deltas[0].shape[2]
    copies = []
    for m in range(out_ref.shape[0]):
        for h in range(chunks):
            for k in range(groups):
                start = ((place[0] ^ k) * chunks + h) * width
                columns = pl.ds(pl.multiple_of(start, 128), width)
                delta = deltas[h * groups + k][m].astype(f32)
                old = weight_ref[m, :, columns].astype(f32)
                out_ref[m, :, columns] = (old - step_size * delta).astype(bf16)
        copies.append(pltpu.make_async_copy(out_ref.at[m], out_hbm.at[m], sems.at[m]))
        copies[-1].start()
    for copy in copies:
        copy.wait()


def basis_kernel(place, *refs):
    out_ref = refs[-1]
    each = refs[0].shape[0]
    for k, ref in enumerate(refs[:-1]):
        for i in range(each):
            out_ref[(place[0] ^ k) * each + i] = ref[i].astype(f32)


def moment_kernel(place, owner, projected_hbm, first_ref, second_ref, *refs):
    first_hbm, second_hbm, projected_ref, first_out, second_out, sems = refs
    here = place[1] * 2 + place[2]
    capacity = first_out.shape[0]
    seen = jnp.int32(0)
    index = [jnp.int32(0)] * capacity
    for m in range(owner.shape[0]):
        hit = owner[m] == here
        for s in range(capacity):
            index[s] = jnp.where(hit & (seen == s), m, index[s])
        seen = seen + hit.astype(jnp.int32)
    fetches = [
        pltpu.make_async_copy(projected_hbm.at[index[s]], projected_ref.at[s], sems.at[0, s])
        for s in range(capacity)
    ]
    for fetch in fetches:
        fetch.start()
    copies = []
    for s in range(capacity):
        fetches[s].wait()
        keep = seen > s
        projected = projected_ref[s].astype(f32)
        first_new = beta_one * first_ref[s] + (1.0 - beta_one) * projected
        second_new = beta_two * second_ref[s] + (1.0 - beta_two) * projected * projected
        first_out[s] = jnp.where(keep, first_new, 0.0)
        second_out[s] = jnp.where(keep, second_new, 0.0)
        pairs = ((first_out, first_hbm), (second_out, second_hbm))
        for t, (source, target) in enumerate(pairs):
            copies.append(
                pltpu.make_async_copy(source.at[s], target.at[s], sems.at[1 + t, s])
            )
            copies[-1].start()
    for copy in copies:
        copy.wait()


def per_device(grads, weight, basis, first_moment, second_moment, sketch, owner, rank):
    owners = lax.axis_size("rows")
    groups = lax.axis_size("dp")
    here = lax.axis_index("rows")
    group = lax.axis_index("dp")
    capacity, rank_full, quarter = first_moment.shape
    count, shard, width = weight.shape
    chips = owners // 2
    each = count // groups
    total_rows = shard * owners
    root = float(total_rows) ** 0.5
    inverse_root = float(total_rows) ** (-0.5)
    place = jnp.stack([group, here // 2, here % 2]).astype(jnp.int32)
    struct = jax.ShapeDtypeStruct

    call = Sequence()
    half = quarter // 2
    keep, relay, *sides = call(
        front_kernel,
        [struct((each, shard, rank_full), f32), struct((2, each, shard, half), f32)]
        + [struct((2, count + each, shard, half), bf16)] * 2,
        (place, grads, sketch),
        scalars=1,
    )
    sides = [swap(sides[i], "dp", 1 << i) for i in range(2)]
    picked, lent = call(
        pick_kernel,
        [struct((chips, 2, rank_full, quarter), bf16)] * 2,
        (place, owner, first_moment, second_moment),
        scalars=2,
    )
    inputs = [picked, swap(lent, "rows", 1)]
    rels = [list(range(chips)), list(range(chips))]
    bits = (-1, -1)
    levels = chips.bit_length() - 1
    for level in range(levels):
        cuts = (level, levels - 1 - level)
        merged = call(
            functools.partial(merge_kernel, rels=rels, bits=bits, cuts=cuts),
            [struct((len(rels[0]) // 2, rank_full, quarter), bf16)] * 4,
            (place, owner, *inputs),
            scalars=2,
        )
        rels = [[rels[t][i] for i in divide(rels[t], cuts[t])[0]] for t in range(2)]
        bits = cuts
        inputs = []
        for t in range(2):
            inputs += [merged[2 * t], swap(merged[2 * t + 1], "rows", 2 << cuts[t])]
    *sums, first_send, second_send = call(
        add_kernel,
        [struct((count, shard, half), f32)] * 2
        + [struct((count + each, shard, half), bf16)] * 2,
        (place, grads, relay, *sides),
        scalars=1,
    )
    relayed = [swap(first_send, "dp", 2), swap(second_send, "dp", 1)]
    mine, sample, other = call(
        functools.partial(project_kernel, scale=inverse_root),
        [
            struct((chips, rank_full, quarter), f32),
            struct((each, shard, rank_full), bf16),
            struct((chips, rank_full, quarter), bf16),
        ],
        (place, *sums, *relayed, *sides, keep, basis),
        scalars=1,
        after=(inputs[1], inputs[3]),
    )
    other = swap(other, "rows", 1)
    samples = [sample]
    mask = chips // 2
    while mask > 1:
        samples += [swap(x, "rows", 2 * mask) for x in samples]
        mask //= 2
    terms = call(
        pair_kernel,
        [
            struct((rank_full, quarter), f32),
            struct((rank_full + each * shard, quarter), bf16),
        ]
        + [struct((rank_full, quarter), bf16)] * (chips - 2),
        (place, mine, other, sample),
        scalars=1,
    )
    samples += [swap(x, "rows", 2) for x in samples[1:]]
    terms = [terms[0]] + [swap(terms[k], "rows", 2 * k) for k in range(1, chips)]
    work_shape = struct((each, rank_full, 2 * rank_full), f32)
    last = rank_full // BLOCK - 1
    update, projected = call(
        functools.partial(update_kernel, chips=chips, bits=bits, start=0),
        [struct((rank_full, quarter), bf16)] * 2,
        (place, owner, rank, *terms, *inputs),
        scalars=3,
    )
    near = [update] + [swap(update, "rows", 2 * k) for k in range(1, chips)]
    gram = call(
        gram_kernel, struct((each, rank_full, rank_full), f32), (terms[1], *samples)
    )
    other_gram = swap(gram, "rows", 1)
    work = call(start_kernel, work_shape, (gram, other_gram))
    early = last // 2 + 1
    for j in range(1, early):
        work = call(functools.partial(middle_kernel, j=j), work_shape, (work,))
    near = call(
        gather_kernel,
        struct((chips, rank_full, quarter), bf16),
        tuple(near),
    )
    far = swap(near, "rows", 1)
    *own, projected = call(
        functools.partial(delta_kernel, chips=chips, scale=inverse_root),
        [struct((count, shard, half), bf16)] * 2 + [struct((rank_full, quarter), bf16)],
        (place, near, far, basis, projected),
        scalars=1,
    )
    beside = [swap(own[0], "dp", 1), swap(own[1], "dp", 2)]
    later = [swap(own[1], "dp", 1), swap(own[0], "dp", 2)]
    gathered = lax.all_gather(projected, "rows", axis=0)
    for j in range(early, last):
        work = call(functools.partial(middle_kernel, j=j), work_shape, (work,))
    passed = call(pass_kernel, [struct(own[0].shape, bf16)] * 2, tuple(beside))
    across = [swap(passed[0], "dp", 2), swap(passed[1], "dp", 1)]
    deltas = [own[0], beside[0], later[1], across[0], own[1], later[0], beside[1], across[1]]
    rows_basis = call(
        functools.partial(finish_kernel, j=last, scale=root),
        struct(sample.shape, bf16),
        (work, sample),
        scratch=[pltpu.VMEM(work_shape.shape, f32)],
    )
    shared = [rows_basis] + [swap(rows_basis, "dp", k) for k in range(1, groups)]
    first_out, second_out = call(
        moment_kernel,
        [struct(first_moment.shape, f32)] * 2,
        (place, owner, gathered, first_moment, second_moment),
        scalars=2,
        after=tuple(across),
        hbm=1,
        direct=True,
        scratch=[
            pltpu.VMEM(first_moment.shape, bf16),
            pltpu.VMEM(first_moment.shape, f32),
            pltpu.VMEM(first_moment.shape, f32),
            pltpu.SemaphoreType.DMA((3, capacity)),
        ],
    )
    new_weight = call(
        functools.partial(weight_kernel, groups=groups, chunks=2),
        struct(weight.shape, bf16),
        (place, weight, *deltas),
        scalars=1,
        direct=True,
        scratch=[pltpu.VMEM(weight.shape, bf16), pltpu.SemaphoreType.DMA((count,))],
    )
    new_basis = call(basis_kernel, struct(basis.shape, f32), (place, *shared), scalars=1)
    return (new_weight, new_basis, first_out, second_out)


def solution(mesh):
    in_specs = (
        P("dp", None, "rows", None),
        P(None, "rows", None),
        P(None, "rows", None),
        P("rows", None, "dp"),
        P("rows", None, "dp"),
        P(),
        P(),
        P(),
    )
    out_specs = (
        P(None, "rows", None),
        P(None, "rows", None),
        P("rows", None, "dp"),
        P("rows", None, "dp"),
    )
    return jax.shard_map(
        per_device, mesh=mesh, in_specs=in_specs, out_specs=out_specs, check_vma=False
    )
```

```python
import functools

import jax
import jax.numpy as jnp
from jax import lax
from jax.experimental import pallas as pl
from jax.experimental.pallas import tpu as pltpu
from jax.sharding import PartitionSpec as P

beta_one = 0.9
beta_two = 0.95
bias_one = 1.0 - 0.9**10
bias_two = 1.0 - 0.95**10
step_size = 0.5
epsilon = 1e-08
BLOCK = 64
GROUP = 4
COST = 10_000
HIGHEST = lax.Precision.HIGHEST
VMEM_LIMIT = 48 * 1024 * 1024
VMEM = pl.BlockSpec(memory_space=pltpu.VMEM)
ANY = pl.BlockSpec(memory_space=pl.ANY)
HBM = pl.BlockSpec(memory_space=pltpu.HBM)
SMEM = pl.BlockSpec(memory_space=pltpu.SMEM)
f32 = jnp.float32
bf16 = jnp.bfloat16


class Sequence:
    def __init__(self):
        self.last = None

    def __call__(self, kernel, out_shape, args, scalars=0, us=2.0, scratch=(), after=(), hbm=0, direct=0):
        many = isinstance(out_shape, (tuple, list))
        specs = [SMEM] * scalars + [HBM] * hbm + [VMEM] * (len(args) - scalars - hbm)
        outs = len(out_shape) if many else 1
        out_specs = [HBM] * direct + [VMEM] * (outs - direct)
        body = kernel
        if self.last is not None:
            after = (self.last, *after)
        unread = len(after)
        if unread:
            specs = [ANY] * unread + specs
            args = (*after, *args)

            def body(*refs):
                kernel(*refs[unread:])

        result = pl.pallas_call(
            body,
            out_shape=out_shape,
            in_specs=specs,
            out_specs=out_specs if many else out_specs[0],
            scratch_shapes=list(scratch),
            compiler_params=pltpu.CompilerParams(vmem_limit_bytes=VMEM_LIMIT),
            cost_estimate=pl.CostEstimate(
                flops=0, bytes_accessed=int(us * COST), transcendentals=0
            ),
        )(*args)
        self.last = min(result, key=lambda x: x.size) if many else result
        return result


def swap(x, axis, mask):
    size = lax.axis_size(axis)
    return lax.ppermute(x, axis, [(i, i ^ mask) for i in range(size)])


def front_kernel(place, grad_ref, sketch_ref, keep_ref, relay_ref, *outs):
    half = outs[0].shape[3]
    count, each = grad_ref.shape[1], keep_ref.shape[0]
    for side, out in enumerate(outs):
        for i, k in enumerate((1 << side, 3)):
            start = (place[0] ^ k) * 2 + side
            columns = pl.ds(pl.multiple_of(start * half, half), half)
            out[i, :count] = grad_ref[0, :, :, columns]
    for k in range(4):
        for i in range(each):
            m = (place[0] ^ k) * each + i
            part = jnp.dot(grad_ref[0, m], sketch_ref[...], preferred_element_type=f32)
            if k == 0:
                keep_ref[i] = part
                continue
            for side, out in enumerate(outs):
                piece = part[:, side * half : (side + 1) * half]
                if k == 2 >> side:
                    relay_ref[side, i] = piece
                else:
                    out[k // 3, count + i] = piece.astype(bf16)


def add_kernel(place, grad_ref, relay_ref, *refs):
    arrived, sums, sends = refs[:2], refs[2:4], refs[4:]
    count, _, half = sums[0].shape
    for side in range(2):
        for i, (k, out) in enumerate(((0, sums[side]), (2 >> side, sends[side]))):
            start = (place[0] ^ k) * 2 + side
            columns = pl.ds(pl.multiple_of(start * half, half), half)
            for m in range(count):
                total = grad_ref[0, m, :, columns].astype(f32) + arrived[side][i, m].astype(f32)
                out[m] = total.astype(out.dtype)
        for i in range(relay_ref.shape[1]):
            total = relay_ref[side, i] + arrived[side][1, count + i].astype(f32)
            sends[side][count + i] = total.astype(bf16)


def gather_kernel(*refs):
    for k, ref in enumerate(refs[:-1]):
        refs[-1][k] = ref[...]


def pass_kernel(*refs):
    half = len(refs) // 2
    for ref, out in zip(refs[:half], refs[half:]):
        out[...] = ref[...]


def gram_kernel(mixed_ref, *refs):
    out = refs[-1]
    each, size, _ = out.shape
    shard = refs[0].shape[1]
    for i in range(each):
        first = size + i * shard
        blocks = [mixed_ref[first : first + shard]] + [ref[i] for ref in refs[:-1]]
        total = None
        for block in blocks:
            term = lax.dot_general(
                block, block, (((0,), (0,)), ((), ())), preferred_element_type=f32
            )
            total = term if total is None else total + term
        out[i] = total


def eliminate(work, j):
    pair, size = work.shape[0], work.shape[1]
    lane = lax.broadcasted_iota(jnp.int32, (BLOCK, 2 * BLOCK), 1)
    sub = lax.broadcasted_iota(jnp.int32, (BLOCK, 2 * BLOCK), 0)
    eye_right = (lane - BLOCK == sub).astype(f32)
    lo = j * BLOCK
    base = lo // 128 * 128
    tiles = []
    for b in range(pair):
        slab = work[b, lo : lo + BLOCK, base : base + 128]
        if lo > base:
            slab = pltpu.roll(slab, 128 - (lo - base), 1)
        tiles.append(jnp.where(lane < BLOCK, slab, eye_right))
    for first in range(0, BLOCK, GROUP):
        for b in range(pair):
            tile = tiles[b]
            columns = [
                jnp.broadcast_to(tile[:, k : k + 1], tile.shape)
                for k in range(first, first + GROUP)
            ]
            rows = []
            for i in range(GROUP):
                k = first + i
                inverse = 1.0 / columns[i][k : k + 1, :]
                row = tile[k : k + 1, :]
                for j in range(i):
                    row = row - columns[j][k : k + 1, :] * rows[j]
                rows.append(row * inverse)
                columns[i] = jnp.where(sub > k, columns[i], 0.0)
                for j in range(i + 1, GROUP):
                    columns[j] = columns[j] - columns[i] * (columns[j][k : k + 1, :] * inverse)
            for i in range(GROUP):
                tile = tile - columns[i] * rows[i]
            tiles[b] = tile
    for b in range(pair):
        tile = tiles[b]
        diagonal = jnp.sum(jnp.where(lane == sub, tile, 0.0), axis=1, keepdims=True)
        inverse = pltpu.roll(tile, BLOCK, 1)[:, :BLOCK] * lax.rsqrt(diagonal)
        solved = jnp.dot(
            inverse, work[b, lo : lo + BLOCK, :], precision=HIGHEST, preferred_element_type=f32
        )
        work[b, lo : lo + BLOCK, size:] = solved[:, size:]
        if lo + BLOCK < size:
            change = lax.dot_general(
                solved[:, :size],
                solved,
                (((0,), (0,)), ((), ())),
                precision=HIGHEST,
                preferred_element_type=f32,
            )
            work[b, lo + BLOCK :, :] = work[b, lo + BLOCK :, :] - change[lo + BLOCK :, :]


def start_kernel(own_ref, other_ref, work):
    pair, size = own_ref.shape[0], own_ref.shape[1]
    row = lax.broadcasted_iota(jnp.int32, (size, size), 0)
    col = lax.broadcasted_iota(jnp.int32, (size, size), 1)
    eye = (row == col).astype(f32)
    for b in range(pair):
        work[b, :, :size] = own_ref[b] + other_ref[b]
        work[b, :, size:] = eye
    eliminate(work, 0)


def middle_kernel(work_in, work, *, j):
    work[...] = work_in[...]
    eliminate(work, j)


def finish_kernel(work_in, rows_ref, out_ref, work, *, j, scale):
    work[...] = work_in[...]
    eliminate(work, j)
    size = work.shape[1]
    for b in range(work.shape[0]):
        basis = lax.dot_general(
            rows_ref[b].astype(f32),
            work[b, :, size:],
            (((1,), (1,)), ((), ())),
            precision=HIGHEST,
            preferred_element_type=f32,
        )
        out_ref[b] = (basis * scale).astype(out_ref.dtype)


def pick_kernel(place, owner, first_ref, second_ref, mine_ref, other_ref):
    here, core = place[1] * 2 + place[2], place[2]
    capacity = first_ref.shape[0]
    seen = jnp.int32(0)
    at = []
    for m in range(owner.shape[0]):
        at.append(jnp.minimum(seen, capacity - 1))
        seen = seen + (owner[m] == here).astype(jnp.int32)
    chips = mine_ref.shape[0]
    for i in range(chips):
        for out, want in ((mine_ref, core), (other_ref, 1 - core)):
            slot = jnp.int32(0)
            m = 2 * (place[1] ^ i) + want
            for j in range(owner.shape[0]):
                slot = jnp.where(m == j, at[j], slot)
            out[i, 0] = first_ref[slot].astype(bf16)
            out[i, 1] = second_ref[slot].astype(bf16)


def near_half(place, owner, rel, bit):
    z, core = place[1], place[2]
    source = owner[2 * (z ^ rel) + core]
    if bit < 0:
        return (source & 1) == core
    return (((source >> 1) ^ z) >> bit) & 1 == 0


def divide(rels, bit):
    keep = [i for i, rel in enumerate(rels) if not rel >> bit & 1]
    send = [rels.index(rels[i] ^ (1 << bit)) for i in keep]
    return keep, send


def merge_kernel(place, owner, *refs, rels, bits, cuts):
    inputs, outs = refs[:-4], refs[-4:]
    for t in range(2):
        for where, out in zip(divide(rels[t], cuts[t]), outs[2 * t : 2 * t + 2]):
            for j, i in enumerate(where):
                local = near_half(place, owner, rels[t][i], bits[t])
                if len(inputs) == 2:
                    own, lent = inputs[0][i, t], inputs[1][i, t]
                else:
                    own, lent = inputs[2 * t][i], inputs[2 * t + 1][i]
                out[j] = jnp.where(local, own, lent)


def project_kernel(place, *refs, scale):
    sums, relayed, arrived = refs[:2], refs[2:4], refs[4:6]
    keep_ref, basis_ref, mine_ref, sample_ref, other_ref = refs[6:]
    core = place[2]
    count, _, half = sums[0].shape
    for i in range(mine_ref.shape[0]):
        for out, want in ((other_ref, 1 - core), (mine_ref, core)):
            m = 2 * i + want
            scaled = (basis_ref[m] * scale).astype(bf16)
            for side in range(2):
                total = sums[side][m] + relayed[side][m].astype(f32)
                product = lax.dot_general(
                    scaled,
                    total.astype(bf16),
                    (((0,), (0,)), ((), ())),
                    preferred_element_type=f32,
                )
                out[i, :, side * half : (side + 1) * half] = product.astype(out.dtype)
    for i in range(keep_ref.shape[0]):
        for side in range(2):
            columns = slice(side * half, (side + 1) * half)
            total = keep_ref[i, :, columns] + arrived[side][0, count + i].astype(f32)
            total = total + relayed[side][count + i].astype(f32)
            sample_ref[i, :, columns] = total.astype(bf16)


def pair_kernel(place, mine_ref, other_ref, sample_ref, *outs):
    rank_full = mine_ref.shape[1]
    each, shard, _ = sample_ref.shape
    for k, out in enumerate(outs):
        i = place[1] ^ k
        out[:rank_full] = (mine_ref[i] + other_ref[i].astype(f32)).astype(out.dtype)
    for i in range(each):
        first = rank_full + i * shard
        outs[1][first : first + shard] = sample_ref[i]


def update_kernel(place, owner, rank, *refs, chips, bits, start):
    terms = refs[:chips]
    first_ref, first_lent, second_ref, second_lent, update_ref, projected_ref = refs[chips:]
    z, core = place[1], place[2]
    m = 2 * z + core
    projected = terms[0][...].astype(f32)
    for ref in terms[1:]:
        projected = projected + ref[: projected.shape[0]].astype(f32)
    width = projected.shape[1]
    columns = slice(start, start + width)
    near = near_half(place, owner, 0, bits[0])
    first = jnp.where(near, first_ref[0, :, columns], first_lent[0, :, columns])
    near = near_half(place, owner, 0, bits[1])
    second = jnp.where(near, second_ref[0, :, columns], second_lent[0, :, columns])
    first_new = beta_one * first.astype(f32) + (1.0 - beta_one) * projected
    second_new = beta_two * second.astype(f32) + (1.0 - beta_two) * projected * projected
    update = (first_new / bias_one) / (jnp.sqrt(second_new / bias_two) + epsilon)
    row = lax.broadcasted_iota(jnp.int32, update.shape, 0)
    update_ref[...] = jnp.where(row < rank[m], update, 0.0).astype(bf16)
    projected_ref[...] = projected.astype(bf16)


def delta_kernel(place, *refs, chips, scale):
    near, far, basis_ref, projected_ref, *outs, passed_ref = refs
    half = outs[0].shape[2]
    z, core = place[1], place[2]
    passed_ref[...] = projected_ref[...]
    for k in range(chips):
        for ref, want in ((near, core), (far, 1 - core)):
            m = 2 * (z ^ k) + want
            product = jnp.dot(
                (basis_ref[m] * scale).astype(bf16), ref[k], preferred_element_type=f32
            )
            for side, out in enumerate(outs):
                out[m] = product[:, side * half : (side + 1) * half].astype(bf16)


def weight_kernel(place, weight_ref, *refs, groups, chunks):
    *deltas, out_hbm, done_ref, out_ref, sems = refs
    done_ref[...] = jnp.zeros(done_ref.shape, f32)
    width = deltas[0].shape[2]
    copies = []
    for m in range(out_ref.shape[0]):
        for h in range(chunks):
            for k in range(groups):
                start = ((place[0] ^ k) * chunks + h) * width
                columns = pl.ds(pl.multiple_of(start, 128), width)
                delta = deltas[h * groups + k][m].astype(f32)
                old = weight_ref[m, :, columns].astype(f32)
                out_ref[m, :, columns] = (old - step_size * delta).astype(bf16)
        copies.append(pltpu.make_async_copy(out_ref.at[m], out_hbm.at[m], sems.at[m]))
        copies[-1].start()
    for copy in copies:
        copy.wait()


def basis_kernel(place, *refs):
    out_ref = refs[-1]
    each = refs[0].shape[0]
    for k, ref in enumerate(refs[:-1]):
        for i in range(each):
            out_ref[(place[0] ^ k) * each + i] = ref[i].astype(f32)


def moment_kernel(place, owner, projected_hbm, first_ref, second_ref, *refs):
    first_hbm, second_hbm, done_ref, projected_ref, first_out, second_out, sems = refs
    done_ref[...] = jnp.zeros(done_ref.shape, f32)
    here = place[1] * 2 + place[2]
    capacity = first_out.shape[0]
    seen = jnp.int32(0)
    index = [jnp.int32(0)] * capacity
    for m in range(owner.shape[0]):
        hit = owner[m] == here
        for s in range(capacity):
            index[s] = jnp.where(hit & (seen == s), m, index[s])
        seen = seen + hit.astype(jnp.int32)
    fetches = [
        pltpu.make_async_copy(projected_hbm.at[index[s]], projected_ref.at[s], sems.at[0, s])
        for s in range(capacity)
    ]
    for fetch in fetches:
        fetch.start()
    copies = []
    for s in range(capacity):
        fetches[s].wait()
        keep = seen > s
        projected = projected_ref[s].astype(f32)
        first_new = beta_one * first_ref[s] + (1.0 - beta_one) * projected
        second_new = beta_two * second_ref[s] + (1.0 - beta_two) * projected * projected
        first_out[s] = jnp.where(keep, first_new, 0.0)
        second_out[s] = jnp.where(keep, second_new, 0.0)
        pairs = ((first_out, first_hbm), (second_out, second_hbm))
        for t, (source, target) in enumerate(pairs):
            copies.append(
                pltpu.make_async_copy(source.at[s], target.at[s], sems.at[1 + t, s])
            )
            copies[-1].start()
    for copy in copies:
        copy.wait()


def per_device(grads, weight, basis, first_moment, second_moment, sketch, owner, rank):
    owners = lax.axis_size("rows")
    groups = lax.axis_size("dp")
    here = lax.axis_index("rows")
    group = lax.axis_index("dp")
    capacity, rank_full, quarter = first_moment.shape
    count, shard, width = weight.shape
    chips = owners // 2
    each = count // groups
    total_rows = shard * owners
    root = float(total_rows) ** 0.5
    inverse_root = float(total_rows) ** (-0.5)
    place = jnp.stack([group, here // 2, here % 2]).astype(jnp.int32)
    struct = jax.ShapeDtypeStruct

    call = Sequence()
    half = quarter // 2
    keep, relay, *sides = call(
        front_kernel,
        [struct((each, shard, rank_full), f32), struct((2, each, shard, half), f32)]
        + [struct((2, count + each, shard, half), bf16)] * 2,
        (place, grads, sketch),
        scalars=1,
    )
    sides = [swap(sides[i], "dp", 1 << i) for i in range(2)]
    picked, lent = call(
        pick_kernel,
        [struct((chips, 2, rank_full, quarter), bf16)] * 2,
        (place, owner, first_moment, second_moment),
        scalars=2,
    )
    inputs = [picked, swap(lent, "rows", 1)]
    rels = [list(range(chips)), list(range(chips))]
    bits = (-1, -1)
    levels = chips.bit_length() - 1
    for level in range(levels):
        cuts = (level, levels - 1 - level)
        merged = call(
            functools.partial(merge_kernel, rels=rels, bits=bits, cuts=cuts),
            [struct((len(rels[0]) // 2, rank_full, quarter), bf16)] * 4,
            (place, owner, *inputs),
            scalars=2,
        )
        rels = [[rels[t][i] for i in divide(rels[t], cuts[t])[0]] for t in range(2)]
        bits = cuts
        inputs = []
        for t in range(2):
            inputs += [merged[2 * t], swap(merged[2 * t + 1], "rows", 2 << cuts[t])]
    *sums, first_send, second_send = call(
        add_kernel,
        [struct((count, shard, half), f32)] * 2
        + [struct((count + each, shard, half), bf16)] * 2,
        (place, grads, relay, *sides),
        scalars=1,
    )
    relayed = [swap(first_send, "dp", 2), swap(second_send, "dp", 1)]
    mine, sample, other = call(
        functools.partial(project_kernel, scale=inverse_root),
        [
            struct((chips, rank_full, quarter), f32),
            struct((each, shard, rank_full), bf16),
            struct((chips, rank_full, quarter), bf16),
        ],
        (place, *sums, *relayed, *sides, keep, basis),
        scalars=1,
        after=(inputs[1], inputs[3]),
    )
    other = swap(other, "rows", 1)
    samples = [sample]
    mask = chips // 2
    while mask > 1:
        samples += [swap(x, "rows", 2 * mask) for x in samples]
        mask //= 2
    terms = call(
        pair_kernel,
        [
            struct((rank_full, quarter), f32),
            struct((rank_full + each * shard, quarter), bf16),
        ]
        + [struct((rank_full, quarter), bf16)] * (chips - 2),
        (place, mine, other, sample),
        scalars=1,
    )
    samples += [swap(x, "rows", 2) for x in samples[1:]]
    terms = [terms[0]] + [swap(terms[k], "rows", 2 * k) for k in range(1, chips)]
    work_shape = struct((each, rank_full, 2 * rank_full), f32)
    last = rank_full // BLOCK - 1
    update, projected = call(
        functools.partial(update_kernel, chips=chips, bits=bits, start=0),
        [struct((rank_full, quarter), bf16)] * 2,
        (place, owner, rank, *terms, *inputs),
        scalars=3,
    )
    near = [update] + [swap(update, "rows", 2 * k) for k in range(1, chips)]
    gram = call(
        gram_kernel, struct((each, rank_full, rank_full), f32), (terms[1], *samples)
    )
    other_gram = swap(gram, "rows", 1)
    work = call(start_kernel, work_shape, (gram, other_gram))
    early = last // 2 + 1
    for j in range(1, early):
        work = call(functools.partial(middle_kernel, j=j), work_shape, (work,))
    near = call(
        gather_kernel,
        struct((chips, rank_full, quarter), bf16),
        tuple(near),
    )
    far = swap(near, "rows", 1)
    *own, projected = call(
        functools.partial(delta_kernel, chips=chips, scale=inverse_root),
        [struct((count, shard, half), bf16)] * 2 + [struct((rank_full, quarter), bf16)],
        (place, near, far, basis, projected),
        scalars=1,
    )
    beside = [swap(own[0], "dp", 1), swap(own[1], "dp", 2)]
    later = [swap(own[1], "dp", 1), swap(own[0], "dp", 2)]
    gathered = lax.all_gather(projected, "rows", axis=0)
    for j in range(early, last):
        work = call(functools.partial(middle_kernel, j=j), work_shape, (work,))
    passed = call(pass_kernel, [struct(own[0].shape, bf16)] * 2, tuple(beside))
    across = [swap(passed[0], "dp", 2), swap(passed[1], "dp", 1)]
    deltas = [own[0], beside[0], later[1], across[0], own[1], later[0], beside[1], across[1]]
    rows_basis = call(
        functools.partial(finish_kernel, j=last, scale=root),
        struct(sample.shape, bf16),
        (work, sample),
        scratch=[pltpu.VMEM(work_shape.shape, f32)],
    )
    shared = [rows_basis] + [swap(rows_basis, "dp", k) for k in range(1, groups)]
    first_out, second_out, _ = call(
        moment_kernel,
        [struct(first_moment.shape, f32)] * 2 + [struct((8, 128), f32)],
        (place, owner, gathered, first_moment, second_moment),
        scalars=2,
        after=tuple(across),
        hbm=1,
        direct=2,
        scratch=[
            pltpu.VMEM(first_moment.shape, bf16),
            pltpu.VMEM(first_moment.shape, f32),
            pltpu.VMEM(first_moment.shape, f32),
            pltpu.SemaphoreType.DMA((3, capacity)),
        ],
    )
    new_weight, _ = call(
        functools.partial(weight_kernel, groups=groups, chunks=2),
        [struct(weight.shape, bf16), struct((8, 128), f32)],
        (place, weight, *deltas),
        scalars=1,
        direct=1,
        scratch=[pltpu.VMEM(weight.shape, bf16), pltpu.SemaphoreType.DMA((count,))],
    )
    new_basis = call(basis_kernel, struct(basis.shape, f32), (place, *shared), scalars=1)
    return (new_weight, new_basis, first_out, second_out)


def solution(mesh):
    in_specs = (
        P("dp", None, "rows", None),
        P(None, "rows", None),
        P(None, "rows", None),
        P("rows", None, "dp"),
        P("rows", None, "dp"),
        P(),
        P(),
        P(),
    )
    out_specs = (
        P(None, "rows", None),
        P(None, "rows", None),
        P("rows", None, "dp"),
        P("rows", None, "dp"),
    )
    return jax.shard_map(
        per_device, mesh=mesh, in_specs=in_specs, out_specs=out_specs, check_vma=False
    )
```

```python
import functools

import jax
import jax.numpy as jnp
from jax import lax
from jax.experimental import pallas as pl
from jax.experimental.pallas import tpu as pltpu
from jax.sharding import PartitionSpec as P

beta_one = 0.9
beta_two = 0.95
bias_one = 1.0 - 0.9**10
bias_two = 1.0 - 0.95**10
step_size = 0.5
epsilon = 1e-08
BLOCK = 64
GROUP = 8
COST = 10_000
HIGHEST = lax.Precision.HIGHEST
VMEM_LIMIT = 48 * 1024 * 1024
VMEM = pl.BlockSpec(memory_space=pltpu.VMEM)
ANY = pl.BlockSpec(memory_space=pl.ANY)
HBM = pl.BlockSpec(memory_space=pltpu.HBM)
SMEM = pl.BlockSpec(memory_space=pltpu.SMEM)
f32 = jnp.float32
bf16 = jnp.bfloat16


class Sequence:
    def __init__(self):
        self.last = None

    def __call__(self, kernel, out_shape, args, scalars=0, us=2.0, scratch=(), after=(), hbm=0, direct=0):
        many = isinstance(out_shape, (tuple, list))
        specs = [SMEM] * scalars + [HBM] * hbm + [VMEM] * (len(args) - scalars - hbm)
        outs = len(out_shape) if many else 1
        out_specs = [HBM] * direct + [VMEM] * (outs - direct)
        body = kernel
        if self.last is not None:
            after = (self.last, *after)
        unread = len(after)
        if unread:
            specs = [ANY] * unread + specs
            args = (*after, *args)

            def body(*refs):
                kernel(*refs[unread:])

        result = pl.pallas_call(
            body,
            out_shape=out_shape,
            in_specs=specs,
            out_specs=out_specs if many else out_specs[0],
            scratch_shapes=list(scratch),
            compiler_params=pltpu.CompilerParams(vmem_limit_bytes=VMEM_LIMIT),
            cost_estimate=pl.CostEstimate(
                flops=0, bytes_accessed=int(us * COST), transcendentals=0
            ),
        )(*args)
        self.last = min(result, key=lambda x: x.size) if many else result
        return result


def swap(x, axis, mask):
    size = lax.axis_size(axis)
    return lax.ppermute(x, axis, [(i, i ^ mask) for i in range(size)])


def front_kernel(place, grad_ref, sketch_ref, keep_ref, relay_ref, *outs):
    half = outs[0].shape[3]
    count, each = grad_ref.shape[1], keep_ref.shape[0]
    for side, out in enumerate(outs):
        for i, k in enumerate((1 << side, 3)):
            start = (place[0] ^ k) * 2 + side
            columns = pl.ds(pl.multiple_of(start * half, half), half)
            out[i, :count] = grad_ref[0, :, :, columns]
    for k in range(4):
        for i in range(each):
            m = (place[0] ^ k) * each + i
            part = jnp.dot(grad_ref[0, m], sketch_ref[...], preferred_element_type=f32)
            if k == 0:
                keep_ref[i] = part
                continue
            for side, out in enumerate(outs):
                piece = part[:, side * half : (side + 1) * half]
                if k == 2 >> side:
                    relay_ref[side, i] = piece
                else:
                    out[k // 3, count + i] = piece.astype(bf16)


def add_kernel(place, grad_ref, relay_ref, *refs):
    arrived, sums, sends = refs[:2], refs[2:4], refs[4:]
    count, _, half = sums[0].shape
    for side in range(2):
        for i, (k, out) in enumerate(((0, sums[side]), (2 >> side, sends[side]))):
            start = (place[0] ^ k) * 2 + side
            columns = pl.ds(pl.multiple_of(start * half, half), half)
            for m in range(count):
                total = grad_ref[0, m, :, columns].astype(f32) + arrived[side][i, m].astype(f32)
                out[m] = total.astype(out.dtype)
        for i in range(relay_ref.shape[1]):
            total = relay_ref[side, i] + arrived[side][1, count + i].astype(f32)
            sends[side][count + i] = total.astype(bf16)


def gather_kernel(*refs):
    for k, ref in enumerate(refs[:-1]):
        refs[-1][k] = ref[...]


def pass_kernel(*refs):
    half = len(refs) // 2
    for ref, out in zip(refs[:half], refs[half:]):
        out[...] = ref[...]


def gram_kernel(mixed_ref, *refs):
    out = refs[-1]
    each, size, _ = out.shape
    shard = refs[0].shape[1]
    for i in range(each):
        first = size + i * shard
        blocks = [mixed_ref[first : first + shard]] + [ref[i] for ref in refs[:-1]]
        total = None
        for block in blocks:
            term = lax.dot_general(
                block, block, (((0,), (0,)), ((), ())), preferred_element_type=f32
            )
            total = term if total is None else total + term
        out[i] = total


def eliminate(work, j):
    pair, size = work.shape[0], work.shape[1]
    lane = lax.broadcasted_iota(jnp.int32, (BLOCK, 2 * BLOCK), 1)
    sub = lax.broadcasted_iota(jnp.int32, (BLOCK, 2 * BLOCK), 0)
    eye_right = (lane - BLOCK == sub).astype(f32)
    lo = j * BLOCK
    base = lo // 128 * 128
    tiles = []
    for b in range(pair):
        slab = work[b, lo : lo + BLOCK, base : base + 128]
        if lo > base:
            slab = pltpu.roll(slab, 128 - (lo - base), 1)
        tiles.append(jnp.where(lane < BLOCK, slab, eye_right))
    for first in range(0, BLOCK, GROUP):
        for b in range(pair):
            tile = tiles[b]
            columns = [
                jnp.broadcast_to(tile[:, k : k + 1], tile.shape)
                for k in range(first, first + GROUP)
            ]
            rows = []
            for i in range(GROUP):
                k = first + i
                inverse = 1.0 / columns[i][k : k + 1, :]
                row = tile[k : k + 1, :]
                for j in range(i):
                    row = row - columns[j][k : k + 1, :] * rows[j]
                rows.append(row * inverse)
                columns[i] = jnp.where(sub > k, columns[i], 0.0)
                for j in range(i + 1, GROUP):
                    columns[j] = columns[j] - columns[i] * (columns[j][k : k + 1, :] * inverse)
            for i in range(GROUP):
                tile = tile - columns[i] * rows[i]
            tiles[b] = tile
    for b in range(pair):
        tile = tiles[b]
        diagonal = jnp.sum(jnp.where(lane == sub, tile, 0.0), axis=1, keepdims=True)
        inverse = pltpu.roll(tile, BLOCK, 1)[:, :BLOCK] * lax.rsqrt(diagonal)
        solved = jnp.dot(
            inverse, work[b, lo : lo + BLOCK, :], precision=HIGHEST, preferred_element_type=f32
        )
        work[b, lo : lo + BLOCK, size:] = solved[:, size:]
        if lo + BLOCK < size:
            change = lax.dot_general(
                solved[:, :size],
                solved,
                (((0,), (0,)), ((), ())),
                precision=HIGHEST,
                preferred_element_type=f32,
            )
            work[b, lo + BLOCK :, :] = work[b, lo + BLOCK :, :] - change[lo + BLOCK :, :]


def start_kernel(own_ref, other_ref, work):
    pair, size = own_ref.shape[0], own_ref.shape[1]
    row = lax.broadcasted_iota(jnp.int32, (size, size), 0)
    col = lax.broadcasted_iota(jnp.int32, (size, size), 1)
    eye = (row == col).astype(f32)
    for b in range(pair):
        work[b, :, :size] = own_ref[b] + other_ref[b]
        work[b, :, size:] = eye
    eliminate(work, 0)


def middle_kernel(work_in, work, *, j):
    work[...] = work_in[...]
    eliminate(work, j)


def finish_kernel(work_in, rows_ref, out_ref, work, *, j, scale):
    work[...] = work_in[...]
    eliminate(work, j)
    size = work.shape[1]
    for b in range(work.shape[0]):
        basis = lax.dot_general(
            rows_ref[b].astype(f32),
            work[b, :, size:],
            (((1,), (1,)), ((), ())),
            precision=HIGHEST,
            preferred_element_type=f32,
        )
        out_ref[b] = (basis * scale).astype(out_ref.dtype)


def pick_kernel(place, owner, first_ref, second_ref, mine_ref, other_ref):
    here, core = place[1] * 2 + place[2], place[2]
    capacity = first_ref.shape[0]
    seen = jnp.int32(0)
    at = []
    for m in range(owner.shape[0]):
        at.append(jnp.minimum(seen, capacity - 1))
        seen = seen + (owner[m] == here).astype(jnp.int32)
    chips = mine_ref.shape[0]
    for i in range(chips):
        for out, want in ((mine_ref, core), (other_ref, 1 - core)):
            slot = jnp.int32(0)
            m = 2 * (place[1] ^ i) + want
            for j in range(owner.shape[0]):
                slot = jnp.where(m == j, at[j], slot)
            out[i, 0] = first_ref[slot].astype(bf16)
            out[i, 1] = second_ref[slot].astype(bf16)


def near_half(place, owner, rel, bit):
    z, core = place[1], place[2]
    source = owner[2 * (z ^ rel) + core]
    if bit < 0:
        return (source & 1) == core
    return (((source >> 1) ^ z) >> bit) & 1 == 0


def divide(rels, bit):
    keep = [i for i, rel in enumerate(rels) if not rel >> bit & 1]
    send = [rels.index(rels[i] ^ (1 << bit)) for i in keep]
    return keep, send


def merge_kernel(place, owner, *refs, rels, bits, cuts):
    inputs, outs = refs[:-4], refs[-4:]
    for t in range(2):
        for where, out in zip(divide(rels[t], cuts[t]), outs[2 * t : 2 * t + 2]):
            for j, i in enumerate(where):
                local = near_half(place, owner, rels[t][i], bits[t])
                if len(inputs) == 2:
                    own, lent = inputs[0][i, t], inputs[1][i, t]
                else:
                    own, lent = inputs[2 * t][i], inputs[2 * t + 1][i]
                out[j] = jnp.where(local, own, lent)


def project_kernel(place, *refs, scale):
    sums, relayed, arrived = refs[:2], refs[2:4], refs[4:6]
    keep_ref, basis_ref, mine_ref, sample_ref, other_ref = refs[6:]
    core = place[2]
    count, _, half = sums[0].shape
    for i in range(mine_ref.shape[0]):
        for out, want in ((other_ref, 1 - core), (mine_ref, core)):
            m = 2 * i + want
            scaled = (basis_ref[m] * scale).astype(bf16)
            for side in range(2):
                total = sums[side][m] + relayed[side][m].astype(f32)
                product = lax.dot_general(
                    scaled,
                    total.astype(bf16),
                    (((0,), (0,)), ((), ())),
                    preferred_element_type=f32,
                )
                out[i, :, side * half : (side + 1) * half] = product.astype(out.dtype)
    for i in range(keep_ref.shape[0]):
        for side in range(2):
            columns = slice(side * half, (side + 1) * half)
            total = keep_ref[i, :, columns] + arrived[side][0, count + i].astype(f32)
            total = total + relayed[side][count + i].astype(f32)
            sample_ref[i, :, columns] = total.astype(bf16)


def pair_kernel(place, mine_ref, other_ref, sample_ref, *outs):
    rank_full = mine_ref.shape[1]
    each, shard, _ = sample_ref.shape
    for k, out in enumerate(outs):
        i = place[1] ^ k
        out[:rank_full] = (mine_ref[i] + other_ref[i].astype(f32)).astype(out.dtype)
    for i in range(each):
        first = rank_full + i * shard
        outs[1][first : first + shard] = sample_ref[i]


def update_kernel(place, owner, rank, *refs, chips, bits, start):
    terms = refs[:chips]
    first_ref, first_lent, second_ref, second_lent, update_ref, projected_ref = refs[chips:]
    z, core = place[1], place[2]
    m = 2 * z + core
    projected = terms[0][...].astype(f32)
    for ref in terms[1:]:
        projected = projected + ref[: projected.shape[0]].astype(f32)
    width = projected.shape[1]
    columns = slice(start, start + width)
    near = near_half(place, owner, 0, bits[0])
    first = jnp.where(near, first_ref[0, :, columns], first_lent[0, :, columns])
    near = near_half(place, owner, 0, bits[1])
    second = jnp.where(near, second_ref[0, :, columns], second_lent[0, :, columns])
    first_new = beta_one * first.astype(f32) + (1.0 - beta_one) * projected
    second_new = beta_two * second.astype(f32) + (1.0 - beta_two) * projected * projected
    update = (first_new / bias_one) / (jnp.sqrt(second_new / bias_two) + epsilon)
    row = lax.broadcasted_iota(jnp.int32, update.shape, 0)
    update_ref[...] = jnp.where(row < rank[m], update, 0.0).astype(bf16)
    projected_ref[...] = projected.astype(bf16)


def delta_kernel(place, *refs, chips, scale):
    near, far, basis_ref, projected_ref, *outs, passed_ref = refs
    half = outs[0].shape[2]
    z, core = place[1], place[2]
    passed_ref[...] = projected_ref[...]
    for k in range(chips):
        for ref, want in ((near, core), (far, 1 - core)):
            m = 2 * (z ^ k) + want
            product = jnp.dot(
                (basis_ref[m] * scale).astype(bf16), ref[k], preferred_element_type=f32
            )
            for side, out in enumerate(outs):
                out[m] = product[:, side * half : (side + 1) * half].astype(bf16)


def weight_kernel(place, weight_ref, *refs, groups, chunks):
    *deltas, out_hbm, done_ref, out_ref, sems = refs
    done_ref[...] = jnp.zeros(done_ref.shape, f32)
    width = deltas[0].shape[2]
    copies = []
    for m in range(out_ref.shape[0]):
        for h in range(chunks):
            for k in range(groups):
                start = ((place[0] ^ k) * chunks + h) * width
                columns = pl.ds(pl.multiple_of(start, 128), width)
                delta = deltas[h * groups + k][m].astype(f32)
                old = weight_ref[m, :, columns].astype(f32)
                out_ref[m, :, columns] = (old - step_size * delta).astype(bf16)
        copies.append(pltpu.make_async_copy(out_ref.at[m], out_hbm.at[m], sems.at[m]))
        copies[-1].start()
    for copy in copies:
        copy.wait()


def basis_kernel(place, *refs):
    out_ref = refs[-1]
    each = refs[0].shape[0]
    for k, ref in enumerate(refs[:-1]):
        for i in range(each):
            out_ref[(place[0] ^ k) * each + i] = ref[i].astype(f32)


def moment_kernel(place, owner, projected_hbm, first_ref, second_ref, *refs):
    first_hbm, second_hbm, done_ref, projected_ref, first_out, second_out, sems = refs
    done_ref[...] = jnp.zeros(done_ref.shape, f32)
    here = place[1] * 2 + place[2]
    capacity = first_out.shape[0]
    seen = jnp.int32(0)
    index = [jnp.int32(0)] * capacity
    for m in range(owner.shape[0]):
        hit = owner[m] == here
        for s in range(capacity):
            index[s] = jnp.where(hit & (seen == s), m, index[s])
        seen = seen + hit.astype(jnp.int32)
    fetches = [
        pltpu.make_async_copy(projected_hbm.at[index[s]], projected_ref.at[s], sems.at[0, s])
        for s in range(capacity)
    ]
    for fetch in fetches:
        fetch.start()
    copies = []
    for s in range(capacity):
        fetches[s].wait()
        keep = seen > s
        projected = projected_ref[s].astype(f32)
        first_new = beta_one * first_ref[s] + (1.0 - beta_one) * projected
        second_new = beta_two * second_ref[s] + (1.0 - beta_two) * projected * projected
        first_out[s] = jnp.where(keep, first_new, 0.0)
        second_out[s] = jnp.where(keep, second_new, 0.0)
        pairs = ((first_out, first_hbm), (second_out, second_hbm))
        for t, (source, target) in enumerate(pairs):
            copies.append(
                pltpu.make_async_copy(source.at[s], target.at[s], sems.at[1 + t, s])
            )
            copies[-1].start()
    for copy in copies:
        copy.wait()


def per_device(grads, weight, basis, first_moment, second_moment, sketch, owner, rank):
    owners = lax.axis_size("rows")
    groups = lax.axis_size("dp")
    here = lax.axis_index("rows")
    group = lax.axis_index("dp")
    capacity, rank_full, quarter = first_moment.shape
    count, shard, width = weight.shape
    chips = owners // 2
    each = count // groups
    total_rows = shard * owners
    root = float(total_rows) ** 0.5
    inverse_root = float(total_rows) ** (-0.5)
    place = jnp.stack([group, here // 2, here % 2]).astype(jnp.int32)
    struct = jax.ShapeDtypeStruct

    call = Sequence()
    half = quarter // 2
    keep, relay, *sides = call(
        front_kernel,
        [struct((each, shard, rank_full), f32), struct((2, each, shard, half), f32)]
        + [struct((2, count + each, shard, half), bf16)] * 2,
        (place, grads, sketch),
        scalars=1,
    )
    sides = [swap(sides[i], "dp", 1 << i) for i in range(2)]
    picked, lent = call(
        pick_kernel,
        [struct((chips, 2, rank_full, quarter), bf16)] * 2,
        (place, owner, first_moment, second_moment),
        scalars=2,
    )
    inputs = [picked, swap(lent, "rows", 1)]
    rels = [list(range(chips)), list(range(chips))]
    bits = (-1, -1)
    levels = chips.bit_length() - 1
    for level in range(levels):
        cuts = (level, levels - 1 - level)
        merged = call(
            functools.partial(merge_kernel, rels=rels, bits=bits, cuts=cuts),
            [struct((len(rels[0]) // 2, rank_full, quarter), bf16)] * 4,
            (place, owner, *inputs),
            scalars=2,
        )
        rels = [[rels[t][i] for i in divide(rels[t], cuts[t])[0]] for t in range(2)]
        bits = cuts
        inputs = []
        for t in range(2):
            inputs += [merged[2 * t], swap(merged[2 * t + 1], "rows", 2 << cuts[t])]
    *sums, first_send, second_send = call(
        add_kernel,
        [struct((count, shard, half), f32)] * 2
        + [struct((count + each, shard, half), bf16)] * 2,
        (place, grads, relay, *sides),
        scalars=1,
    )
    relayed = [swap(first_send, "dp", 2), swap(second_send, "dp", 1)]
    mine, sample, other = call(
        functools.partial(project_kernel, scale=inverse_root),
        [
            struct((chips, rank_full, quarter), f32),
            struct((each, shard, rank_full), bf16),
            struct((chips, rank_full, quarter), bf16),
        ],
        (place, *sums, *relayed, *sides, keep, basis),
        scalars=1,
        after=(inputs[1], inputs[3]),
    )
    other = swap(other, "rows", 1)
    samples = [sample]
    mask = chips // 2
    while mask > 1:
        samples += [swap(x, "rows", 2 * mask) for x in samples]
        mask //= 2
    terms = call(
        pair_kernel,
        [
            struct((rank_full, quarter), f32),
            struct((rank_full + each * shard, quarter), bf16),
        ]
        + [struct((rank_full, quarter), bf16)] * (chips - 2),
        (place, mine, other, sample),
        scalars=1,
    )
    samples += [swap(x, "rows", 2) for x in samples[1:]]
    terms = [terms[0]] + [swap(terms[k], "rows", 2 * k) for k in range(1, chips)]
    work_shape = struct((each, rank_full, 2 * rank_full), f32)
    last = rank_full // BLOCK - 1
    update, projected = call(
        functools.partial(update_kernel, chips=chips, bits=bits, start=0),
        [struct((rank_full, quarter), bf16)] * 2,
        (place, owner, rank, *terms, *inputs),
        scalars=3,
    )
    near = [update] + [swap(update, "rows", 2 * k) for k in range(1, chips)]
    gram = call(
        gram_kernel, struct((each, rank_full, rank_full), f32), (terms[1], *samples)
    )
    other_gram = swap(gram, "rows", 1)
    work = call(start_kernel, work_shape, (gram, other_gram))
    early = last // 2 + 1
    for j in range(1, early):
        work = call(functools.partial(middle_kernel, j=j), work_shape, (work,))
    near = call(
        gather_kernel,
        struct((chips, rank_full, quarter), bf16),
        tuple(near),
    )
    far = swap(near, "rows", 1)
    *own, projected = call(
        functools.partial(delta_kernel, chips=chips, scale=inverse_root),
        [struct((count, shard, half), bf16)] * 2 + [struct((rank_full, quarter), bf16)],
        (place, near, far, basis, projected),
        scalars=1,
    )
    beside = [swap(own[0], "dp", 1), swap(own[1], "dp", 2)]
    later = [swap(own[1], "dp", 1), swap(own[0], "dp", 2)]
    gathered = lax.all_gather(projected, "rows", axis=0)
    for j in range(early, last):
        work = call(functools.partial(middle_kernel, j=j), work_shape, (work,))
    passed = call(pass_kernel, [struct(own[0].shape, bf16)] * 2, tuple(beside))
    across = [swap(passed[0], "dp", 2), swap(passed[1], "dp", 1)]
    deltas = [own[0], beside[0], later[1], across[0], own[1], later[0], beside[1], across[1]]
    rows_basis = call(
        functools.partial(finish_kernel, j=last, scale=root),
        struct(sample.shape, bf16),
        (work, sample),
        scratch=[pltpu.VMEM(work_shape.shape, f32)],
    )
    shared = [rows_basis] + [swap(rows_basis, "dp", k) for k in range(1, groups)]
    first_out, second_out, _ = call(
        moment_kernel,
        [struct(first_moment.shape, f32)] * 2 + [struct((8, 128), f32)],
        (place, owner, gathered, first_moment, second_moment),
        scalars=2,
        after=tuple(across),
        hbm=1,
        direct=2,
        scratch=[
            pltpu.VMEM(first_moment.shape, bf16),
            pltpu.VMEM(first_moment.shape, f32),
            pltpu.VMEM(first_moment.shape, f32),
            pltpu.SemaphoreType.DMA((3, capacity)),
        ],
    )
    new_weight, _ = call(
        functools.partial(weight_kernel, groups=groups, chunks=2),
        [struct(weight.shape, bf16), struct((8, 128), f32)],
        (place, weight, *deltas),
        scalars=1,
        direct=1,
        scratch=[pltpu.VMEM(weight.shape, bf16), pltpu.SemaphoreType.DMA((count,))],
    )
    new_basis = call(basis_kernel, struct(basis.shape, f32), (place, *shared), scalars=1)
    return (new_weight, new_basis, first_out, second_out)


def solution(mesh):
    in_specs = (
        P("dp", None, "rows", None),
        P(None, "rows", None),
        P(None, "rows", None),
        P("rows", None, "dp"),
        P("rows", None, "dp"),
        P(),
        P(),
        P(),
    )
    out_specs = (
        P(None, "rows", None),
        P(None, "rows", None),
        P("rows", None, "dp"),
        P("rows", None, "dp"),
    )
    return jax.shard_map(
        per_device, mesh=mesh, in_specs=in_specs, out_specs=out_specs, check_vma=False
    )
```
